32 devices in a mesh: rows: 16 (over z, y, core), ctx: 2 (over x).
Axes of the slice: x: 2, y: 2, z: 4, core: 2. Of those that a mesh axis runs over, the one named last changes fastest.
Arguments:
- tokens: bfloat16 [32, 512, 1024], P('rows', 'ctx'), may hold values from -6 to 6
- cotangent: bfloat16 [32, 512, 1024], P('rows', 'ctx'), may hold values from -6 to 6
- w_qkv: bfloat16 [1024, 3072], replicated, may hold values from -0.1875 to 0.1875
- w_out: bfloat16 [1024, 1024], replicated, may hold values from -0.1875 to 0.1875
- w_fc1: bfloat16 [1024, 4096], replicated, may hold values from -0.1875 to 0.1875
- w_fc2: bfloat16 [4096, 1024], replicated, may hold values from -0.09375 to 0.09375
- norm_gain: float32 [3, 1024], replicated, may hold values from 0.1 to 1.9
- norm_bias: float32 [3, 1024], replicated, may hold values from -1.5 to 1.5
- mid_gain: float32 [4096], replicated, may hold values from 0.1 to 1.9
- mid_bias: float32 [4096], replicated, may hold values from -1.5 to 1.5
- head_scale: float32 [16], replicated, may hold values from 0.5 to 2
- doc_lengths: int32 [32, 4], P('rows'), may hold values from 1 to 256, 512 in all within a row
Outputs:
- output: bfloat16 [32, 512, 1024], P('rows', 'ctx')
- grad_tokens: float32 [32, 512, 1024], P('rows', 'ctx')
- grad_w_qkv: float32 [1024, 3072], P('ctx')
- grad_w_out: float32 [1024, 1024], P('ctx')
- grad_w_fc1: float32 [1024, 4096], P('ctx')
- grad_w_fc2: float32 [4096, 1024], P('ctx')
- grad_norm_gain: float32 [3, 1024], P(None, 'ctx')
- grad_norm_bias: float32 [3, 1024], P(None, 'ctx')
- grad_mid_gain: float32 [4096], P('ctx')
- grad_mid_bias: float32 [4096], P('ctx')
- grad_head_scale: float32 [16], P('ctx')
The draws below stay inside these ranges and needn't reach their ends.
Inputs may be any that keep to these rules, and one draw needn't show every extreme that they name: `doc_lengths`: in each row the 4 lengths sum to 512, and the largest is exactly 256.
All inputs are finite; a program needn't handle non-finite values.
Results may differ from the reference program's by a relative error of at most 0.011.
Values may be sent and summed in bfloat16 or wider, within the bound.
A program may use at most 256 MiB of HBM per device.

```python
import math
import jax
import jax.numpy as jnp
import numpy as np
from jax import lax

D = 1024
HEADS = 16
FF = 4096
NDOCS = 4
ROW_LEN = 512
MOST_DOC = 256
ROWS = 32


def levels(rng, extent, shards, smallest, top_value):
    factor_of = 1.0
    for axis_at, shards_of in shards:
        steps = jax.random.uniform(jax.random.fold_in(jax.random.fold_in(rng, 6), axis_at), (shards_of,), jnp.float32, smallest / len(shards), top_value / len(shards))
        factor_of = factor_of * jnp.repeat(jnp.exp(steps), extent[axis_at] // shards_of).reshape((-1,) + (1,) * (len(extent) - 1 - axis_at))
    return factor_of


def split_up(number_of, total, bound, skew):
    loads = [(1 << 20) // math.isqrt(rank ** skew) + 1 for rank in range(2, number_of + 1)]
    spare, holding = total - bound - (number_of - 1), [1] * (number_of - 1)
    while spare > 0:
        candidates = [i for i in range(number_of - 1) if holding[i] < bound]
        mass, budget = sum([loads[i] for i in candidates]), spare
        for i in candidates:
            more = min(bound - holding[i], max(1, budget * loads[i] // mass), spare)
            holding[i] = holding[i] + more
            spare = spare - more
    return np.array([bound] + holding)


def uneven(key, number_of, total, reach, skew):
    if number_of == 2:
        one = jax.random.randint(key, (), max(1, total - reach), min(reach, total - 1) + 1)
        return jnp.stack([one, total - one])
    sizes = jnp.asarray(split_up(number_of, total, reach, skew), jnp.int32)
    twos = (number_of - 1) // 2
    donor, taker = sizes[1:1 + 2 * twos:2], sizes[2:2 + 2 * twos:2]
    margin = jnp.minimum(donor - 1, reach - taker)
    shifted = jax.random.randint(jax.random.fold_in(key, 1), (twos,), 0, 1 << 20) % (margin + 1)
    sizes = sizes.at[1:1 + 2 * twos:2].set(donor - shifted).at[2:2 + 2 * twos:2].set(taker + shifted)
    return sizes[jax.random.permutation(jax.random.fold_in(key, 2), number_of)]


def centred(stream_key, shape, spread, bound, pieces=(), kind=jnp.bfloat16):
    gain = levels(stream_key, shape, pieces, -0.22, 0.18) if pieces else 1.0
    drawn = jax.random.normal(stream_key, shape, jnp.float32) * spread * gain
    return jnp.minimum(jnp.maximum(drawn, -bound), bound).astype(kind)


def setup_inputs(seed: int = 0) -> dict:
    key_list = jax.random.split(jax.random.key(seed), 13)
    tokens = centred(key_list[0], (ROWS, ROW_LEN, D), 1.0, 6.0, ((0, 16), (1, 2)))
    cotangent = centred(key_list[1], (ROWS, ROW_LEN, D), 1.0, 6.0, ((0, 16), (1, 2)))
    w_qkv = centred(key_list[2], (D, 3 * D), D ** -0.5, 0.1875)
    w_out = centred(key_list[3], (D, D), D ** -0.5, 0.1875)
    w_fc1 = centred(key_list[4], (D, FF), D ** -0.5, 0.1875)
    w_fc2 = centred(key_list[5], (FF, D), FF ** -0.5, 0.09375)
    norm_gain = jnp.clip(1.0 + 0.18 * jax.random.normal(key_list[6], (3, D), jnp.float32), 0.1, 1.9)
    norm_bias = centred(key_list[7], (3, D), 0.3, 1.5, (), jnp.float32)
    mid_gain = jnp.clip(1.0 + 0.18 * jax.random.normal(key_list[8], (FF,), jnp.float32), 0.1, 1.9)
    mid_bias = centred(key_list[9], (FF,), 0.3, 1.5, (), jnp.float32)
    head_scale = jnp.clip(jnp.exp(jax.random.uniform(key_list[10], (HEADS,), jnp.float32, math.log(0.5), math.log(2.0))), 0.5, 2.0)
    doc_lengths = jax.vmap(lambda own: uneven(own, NDOCS, ROW_LEN, MOST_DOC, 2))(jax.random.split(key_list[11], ROWS)).reshape((ROWS, NDOCS)).astype(jnp.int32)
    return dict(tokens=tokens, cotangent=cotangent, w_qkv=w_qkv, w_out=w_out, w_fc1=w_fc1, w_fc2=w_fc2, norm_gain=norm_gain, norm_bias=norm_bias, mid_gain=mid_gain, mid_bias=mid_bias, head_scale=head_scale, doc_lengths=doc_lengths)


epsilon = 1e-05
masked_value = -1e+30
highest = lax.Precision.HIGHEST

@jax.custom_vjp
def low(v):
    return lax.optimization_barrier(v.astype(jnp.bfloat16)).astype(jnp.float32)

@jax.custom_vjp
def low_back(v):
    return v

def low_keep(v):
    return (low(v), None)

def low_pass(kept, grad):
    return (grad,)

def back_keep(v):
    return (v, None)

def back_low(kept, grad):
    return (low(grad),)
low.defvjp(low_keep, low_pass)
low_back.defvjp(back_keep, back_low)

def layer_norm(values, gain_vec, offset_vec):
    average = lax.optimization_barrier(jnp.mean(values, axis=-1, keepdims=True))
    centered = values - average
    variance = lax.optimization_barrier(jnp.mean(centered * centered, axis=-1, keepdims=True))
    return centered * lax.rsqrt(variance + epsilon) * gain_vec + offset_vec

def row_layer(weights, row_input, lengths):
    w_qkv, w_out, w_fc1, w_fc2, norm_gain, norm_bias, mid_gain, mid_bias, head_scale = weights
    length_total = row_input.shape[0]
    model_width = row_input.shape[1]
    head_count = head_scale.shape[0]
    head_size = model_width // head_count
    bounds = jnp.cumsum(lengths.astype(jnp.int32), dtype=jnp.int32)
    places = jnp.arange(length_total, dtype=jnp.int32)
    labels = lax.optimization_barrier(jnp.sum((places[:, None] >= bounds[None, :]).astype(jnp.int32), axis=1, dtype=jnp.int32))
    allowed = (labels[:, None] == labels[None, :]) & (places[:, None] >= places[None, :])
    normed = low(layer_norm(row_input, norm_gain[0], norm_bias[0]))
    qkv_rows = low(low_back(jnp.dot(normed, w_qkv, precision=highest)))
    qkv_rows = qkv_rows.reshape(length_total, 3, head_count, head_size)
    raw_scores = jnp.einsum('qhd,khd->hqk', qkv_rows[:, 0], qkv_rows[:, 1], precision=highest)
    scores = jnp.where(allowed[None], low_back(raw_scores) * head_size ** (-0.5), masked_value)
    row_max = lax.optimization_barrier(jnp.max(scores, axis=-1, keepdims=True))
    powers = jnp.exp(scores - row_max)
    attn_probs = low(powers / lax.optimization_barrier(jnp.sum(powers, axis=-1, keepdims=True)))
    attended = low_back(jnp.einsum('hqk,khd->qhd', attn_probs, qkv_rows[:, 2], precision=highest))
    sent_heads = low(low_back(attended * head_scale[None, :, None])).reshape(length_total, model_width)
    projected = low_back(jnp.dot(sent_heads, w_out, precision=highest))
    hidden = row_input + layer_norm(projected, norm_gain[1], norm_bias[1])
    ffn_in = low(layer_norm(hidden, norm_gain[2], norm_bias[2]))
    first_out = low_back(jnp.dot(ffn_in, w_fc1, precision=highest))
    middle = low(layer_norm(jax.nn.gelu(first_out, approximate=False), mid_gain, mid_bias))
    return hidden + jnp.dot(middle, w_fc2, precision=highest)

def reference(tokens, cotangent, w_qkv, w_out, w_fc1, w_fc2, norm_gain, norm_bias, mid_gain, mid_bias, head_scale, doc_lengths):
    weights = (w_qkv.astype(jnp.float32), w_out.astype(jnp.float32), w_fc1.astype(jnp.float32), w_fc2.astype(jnp.float32), norm_gain, norm_bias, mid_gain, mid_bias, head_scale)
    inputs = tokens.astype(jnp.float32)

    def forward(weight_set, layer_input):

        def row_step(paired):
            return row_layer(weight_set, paired[0], paired[1])
        return lax.map(jax.checkpoint(row_step), (layer_input, doc_lengths))
    result, pullback = jax.vjp(forward, weights, inputs)
    grad_weights, grad_inputs = pullback(cotangent.astype(jnp.float32))
    return (result.astype(jnp.bfloat16), grad_inputs, grad_weights[0], grad_weights[1], grad_weights[2], grad_weights[3], grad_weights[4], grad_weights[5], grad_weights[6], grad_weights[7], grad_weights[8])
```

```python
import functools

import jax
import jax.numpy as jnp
from jax import lax
from jax.experimental import pallas as pl
from jax.experimental.pallas import tpu as pltpu
from jax.sharding import PartitionSpec as P

EPS = 1e-05
MASKED = -1e30
BF = jnp.bfloat16
F32 = jnp.float32
REACH = 256
QB = 128
TILE = 1024


def dot(a, b, ca, cb):
    return lax.dot_general(a, b, (((ca,), (cb,)), ((), ())), preferred_element_type=F32)


def ln_stats(v):
    mean = jnp.mean(v, axis=-1, keepdims=True)
    cen = v - mean
    inv = lax.rsqrt(jnp.mean(cen * cen, axis=-1, keepdims=True) + EPS)
    return cen * inv, inv


def ln_back(e, gain, n, inv):
    a = e * gain
    return inv * (
        a - jnp.mean(a, axis=-1, keepdims=True) - n * jnp.mean(a * n, axis=-1, keepdims=True)
    )


def colsum(v):
    return jnp.sum(v, axis=0, keepdims=True)


def params(mib=60):
    return pltpu.CompilerParams(vmem_limit_bytes=mib * 2**20)


def cost(macs, nbytes, trans=0):
    return pl.CostEstimate(flops=2 * macs, bytes_accessed=nbytes, transcendentals=trans)


def call(kernel, grid, scalars, in_specs, out_specs, out_shape, scratch, ce):
    return pl.pallas_call(
        kernel,
        grid_spec=pltpu.PrefetchScalarGridSpec(
            num_scalar_prefetch=1,
            grid=grid,
            in_specs=in_specs,
            out_specs=out_specs,
            scratch_shapes=scratch,
        ),
        out_shape=out_shape,
        compiler_params=params(),
        cost_estimate=ce,
    )


def const_spec(shape):
    return pl.BlockSpec(shape, lambda i, s: (0,) * len(shape))


def struct(shape, dtype):
    return jax.ShapeDtypeStruct(shape, dtype)


def qkv_kernel(s, x, w, g, b, normed, qkv):
    @pl.when(pl.program_id(0) == 0)
    def _():
        n, _ = ln_stats(x[...].astype(F32))
        normed[...] = (n * g[...] + b[...]).astype(BF)

    qkv[0] = dot(normed[...], w[...], 1, 0).astype(BF)


def qkv_call(idx, x, w, g, b):
    t, d = x.shape
    return call(
        qkv_kernel,
        (3,),
        1,
        [
            const_spec((t, d)),
            pl.BlockSpec((d, d), lambda i, s: (0, i)),
            const_spec((1, d)),
            const_spec((1, d)),
        ],
        [const_spec((t, d)), pl.BlockSpec((1, t, d), lambda i, s: (i, 0, 0))],
        [struct((t, d), BF), struct((3, t, d), BF)],
        [],
        cost(3 * t * d * d, 2 * (3 * d * d + 5 * t * d)),
    )(idx, x, w, g, b)


def key_range(i):
    return max(0, i * QB - REACH), (i + 1) * QB


def fill_bias(start, bias, t):
    for i in range(t // QB):
        k0, k1 = key_range(i)
        u = lax.broadcasted_iota(jnp.int32, (k1 - k0, QB), 0) + k0
        q = lax.broadcasted_iota(jnp.int32, (k1 - k0, QB), 1) + i * QB
        first = start[:, i * QB : (i + 1) * QB]
        ok = (u >= first) & (u <= q)
        one = jnp.where(ok, 0.0, MASKED).astype(F32)
        bias[i, 0 : k1 - k0, 0:QB] = one
        bias[i, 0 : k1 - k0, QB : 2 * QB] = one


def both_heads(v, hd):
    lane = lax.broadcasted_iota(jnp.int32, v.shape, 1)
    zero = jnp.zeros_like(v)
    return jnp.concatenate([jnp.where(lane < hd, v, zero), jnp.where(lane < hd, zero, v)], axis=0)


def attn_fwd_kernel(s, q, k, v, start, scale, sent, lse, bias):
    t, w = q.shape[1], q.shape[2]
    hd = w // 2

    @pl.when(pl.program_id(0) == 0)
    def _():
        fill_bias(start, bias, t)

    vt = v[0].astype(F32).T.astype(BF)
    for i in range(t // QB):
        k0, k1 = key_range(i)
        qs = slice(i * QB, (i + 1) * QB)
        qm = both_heads(q[0, qs, :], hd) * (hd**-0.5)
        st = dot(k[0, k0:k1, :], qm.astype(BF), 1, 1) + bias[i, 0 : k1 - k0, :]
        top = jnp.max(st, axis=0, keepdims=True)
        pt = jnp.exp(st - top)
        total = jnp.sum(pt, axis=0, keepdims=True)
        ot = dot(vt[:, k0:k1], pt.astype(BF), 1, 0) * (1.0 / total)
        o = jnp.concatenate([ot[0:hd, 0:QB], ot[hd:, QB:]], axis=0).T
        sent[qs, :] = (o * scale[...]).astype(BF)
        ls = top + jnp.log(total)
        lse[0, 0:1, qs] = ls[:, 0:QB]
        lse[0, 1:2, qs] = ls[:, QB:]


def attn_fwd_call(idx, qkv, start, scale):
    _, t, d = qkv.shape
    pairs = d // 128
    part = lambda j: pl.BlockSpec((1, t, 128), lambda i, s: (j, 0, i))
    return call(
        attn_fwd_kernel,
        (pairs,),
        1,
        [part(0), part(1), part(2), const_spec((1, t)), pl.BlockSpec((1, 128), lambda i, s: (0, i))],
        [
            pl.BlockSpec((t, 128), lambda i, s: (0, i)),
            pl.BlockSpec((1, 2, t), lambda i, s: (i, 0, 0)),
        ],
        [struct((t, d), BF), struct((pairs, 2, t), F32)],
        [pltpu.VMEM((t // QB, QB + REACH, 2 * QB), F32)],
        cost(t * d * t * 2, 8 * t * d, t * t * 8),
    )(idx, qkv, qkv, qkv, start, scale)


def attn_bwd_kernel(s, q, k, v, gs, sent, lse, start, scale, send, keep, hsum, bias, gk, gv, gqt):
    t, w = q.shape[1], q.shape[2]
    hd = w // 2
    pid = pl.program_id(0)
    half = pl.num_programs(0) // 2

    @pl.when(pid == 0)
    def _():
        fill_bias(start, bias, t)

    kt = k[0].astype(F32).T.astype(BF)
    gsf = gs[...].astype(F32)
    prod = (gsf * sent[...].astype(F32)).T
    d0 = jnp.sum(prod[0:hd], axis=0, keepdims=True)
    d1 = jnp.sum(prod[hd:], axis=0, keepdims=True)
    hsum[0] = jnp.concatenate([d0, d1], axis=0)
    ga = (gsf * scale[...]).astype(BF)
    gk[...] = jnp.zeros_like(gk)
    gv[...] = jnp.zeros_like(gv)
    for i in range(t // QB):
        k0, k1 = key_range(i)
        qs = slice(i * QB, (i + 1) * QB)
        qm = (both_heads(q[0, qs, :], hd) * (hd**-0.5)).astype(BF)
        gm = both_heads(ga[qs, :], hd)
        st = dot(k[0, k0:k1, :], qm, 1, 1) + bias[i, 0 : k1 - k0, :]
        ls = jnp.concatenate([lse[0, 0:1, qs], lse[0, 1:2, qs]], axis=1)
        dd = jnp.concatenate([d0[:, qs], d1[:, qs]], axis=1)
        pt = jnp.exp(st - ls)
        gp = dot(v[0, k0:k1, :], gm, 1, 1)
        ds = (pt * (gp - dd)).astype(BF)
        gv[k0:k1, :] += dot(pt.astype(BF), gm, 1, 0)
        gk[k0:k1, :] += dot(ds, qm, 1, 0)
        gq = dot(kt[:, k0:k1], ds, 1, 0) * (hd**-0.5)
        gqt[:, qs] = jnp.concatenate([gq[0:hd, 0:QB], gq[hd:, QB:]], axis=0)

    def put(out):
        out[0] = gqt[...].T.astype(BF)
        out[1] = gk[...].astype(BF)
        out[2] = gv[...].astype(BF)

    pl.when(pid < half)(lambda: put(send))
    pl.when(pid >= half)(lambda: put(keep))


def attn_bwd_call(idx, qkv, gs, sent, lse, start, scale):
    _, t, d = qkv.shape
    pairs = d // 128
    half = pairs // 2

    def at(i, s):
        return jnp.where(i < half, i + (1 - s[1]) * half, i - half + s[1] * half)

    part = lambda j: pl.BlockSpec((1, t, 128), lambda i, s: (j, 0, at(i, s)))
    flat = pl.BlockSpec((t, 128), lambda i, s: (0, at(i, s)))
    return call(
        attn_bwd_kernel,
        (pairs,),
        1,
        [
            part(0),
            part(1),
            part(2),
            flat,
            flat,
            pl.BlockSpec((1, 2, t), lambda i, s: (at(i, s), 0, 0)),
            const_spec((1, t)),
            pl.BlockSpec((1, 128), lambda i, s: (0, at(i, s))),
        ],
        [
            pl.BlockSpec((3, t, 128), lambda i, s: (0, 0, jnp.minimum(i, half - 1))),
            pl.BlockSpec((3, t, 128), lambda i, s: (0, 0, jnp.maximum(i - half, 0))),
            pl.BlockSpec((1, 2, t), lambda i, s: (at(i, s), 0, 0)),
        ],
        [
            struct((3, t, d // 2), BF),
            struct((3, t, d // 2), BF),
            struct((pairs, 2, t), F32),
        ],
        [
            pltpu.VMEM((t // QB, QB + REACH, 2 * QB), F32),
            pltpu.VMEM((t, 128), F32),
            pltpu.VMEM((t, 128), F32),
            pltpu.VMEM((128, t), F32),
        ],
        cost(t * d * t * 5, 16 * t * d, t * t * 8),
    )(idx, qkv, qkv, qkv, gs, sent, lse, start, scale)


def ffn_block(i, s):
    return (i % 2) * 2 + jnp.where(i < 2, 1 - s[1], s[1])


def ffn_fwd_kernel(
    s, sent, x, wo, g, b, w1, mg, mb, n1, s1, n2, s2, ffn_in, slope, nmid, smid, send, keep, act, tot
):
    i = pl.program_id(0)
    blocks = pl.num_programs(0) // 2
    width = blocks * act.shape[2]

    @pl.when(i == 0)
    def _():
        n, inv = ln_stats(dot(sent[...], wo[...], 1, 0))
        n1[...] = n
        s1[...] = inv
        hidden = x[...].astype(F32) + n * g[1:2, :] + b[1:2, :]
        n, inv = ln_stats(hidden)
        n2[...] = n
        s2[...] = inv
        ffn_in[...] = (n * g[2:3, :] + b[2:3, :]).astype(BF)
        tot[...] = jnp.zeros_like(tot)

    @pl.when(i < blocks)
    def _():
        f = dot(ffn_in[...], w1[...], 1, 0)
        phi = 0.5 + 0.5 * lax.erf(f * (0.5**0.5))
        a = f * phi
        slope[0] = (phi + f * (jnp.exp(-0.5 * f * f) * 0.3989422804014327)).astype(BF)
        act[i] = a
        tot[...] += jnp.sum(a, axis=-1, keepdims=True)

    @pl.when(i == blocks)
    def _():
        mean = tot[...] * (1.0 / width)
        sq = jnp.zeros_like(mean)
        for j in range(4):
            c = act[j] - mean
            act[j] = c
            sq += jnp.sum(c * c, axis=-1, keepdims=True)
        smid[...] = lax.rsqrt(sq * (1.0 / width) + EPS)

    @pl.when(i >= blocks)
    def _():
        n = act[i - blocks] * smid[...]
        nmid[0] = n.astype(BF)
        m = (n * mg[...] + mb[...]).astype(BF)

        @pl.when(i < blocks + blocks // 2)
        def _():
            send[0] = m

        @pl.when(i >= blocks + blocks // 2)
        def _():
            keep[0] = m


def ffn_fwd_call(idx, sent, x, wo, g, b, w1, mg, mb):
    t, d = x.shape
    ff = w1.shape[1]
    bw = ff // 4
    first = lambda i: jnp.minimum(i, 3)
    second = lambda i: jnp.maximum(i - 4, 0)
    vec = pl.BlockSpec((1, bw), lambda i, s: (0, ffn_block(second(i), s)))
    return call(
        ffn_fwd_kernel,
        (8,),
        1,
        [
            const_spec((t, d)),
            const_spec((t, d)),
            const_spec((d, d)),
            const_spec((3, d)),
            const_spec((3, d)),
            pl.BlockSpec((d, bw), lambda i, s: (0, ffn_block(first(i), s))),
            vec,
            vec,
        ],
        [
            const_spec((t, d)),
            const_spec((t, 1)),
            const_spec((t, d)),
            const_spec((t, 1)),
            const_spec((t, d)),
            pl.BlockSpec((1, t, bw), lambda i, s: (first(i), 0, 0)),
            pl.BlockSpec((1, t, bw), lambda i, s: (second(i), 0, 0)),
            const_spec((t, 1)),
            pl.BlockSpec((1, t, bw), lambda i, s: (jnp.clip(i - 4, 0, 1), 0, 0)),
            pl.BlockSpec((1, t, bw), lambda i, s: (jnp.clip(i - 6, 0, 1), 0, 0)),
        ],
        [
            struct((t, d), F32),
            struct((t, 1), F32),
            struct((t, d), F32),
            struct((t, 1), F32),
            struct((t, d), BF),
            struct((4, t, bw), BF),
            struct((4, t, bw), BF),
            struct((t, 1), F32),
            struct((2, t, bw), BF),
            struct((2, t, bw), BF),
        ],
        [pltpu.VMEM((4, t, bw), F32), pltpu.VMEM((t, 1), F32)],
        cost(t * d * (d + ff), 2 * d * (d + ff) + 30 * t * d, 2 * t * ff),
    )(idx, sent, x, wo, g, b, w1, mg, mb)


def out_kernel(s, send, keep, w2, x, n1, g, b, out, acc):
    i = pl.program_id(0)

    @pl.when(i == 0)
    def _():
        acc[...] = x[...].astype(F32) + n1[...] * g[1:2, :] + b[1:2, :]

    @pl.when(i < 2)
    def _():
        acc[...] += dot(send[0], w2[...], 1, 0)

    @pl.when(i >= 2)
    def _():
        acc[...] += dot(keep[0], w2[...], 1, 0)

    @pl.when(i == 3)
    def _():
        out[...] = acc[...].astype(BF)


def out_call(idx, send, keep, w2, x, n1, g, b):
    t, d = x.shape
    ff = w2.shape[0]
    bw = ff // 4
    return call(
        out_kernel,
        (4,),
        1,
        [
            pl.BlockSpec((1, t, bw), lambda i, s: (jnp.clip(i, 0, 1), 0, 0)),
            pl.BlockSpec((1, t, bw), lambda i, s: (jnp.clip(i - 2, 0, 1), 0, 0)),
            pl.BlockSpec((bw, d), lambda i, s: (ffn_block(i, s), 0)),
            const_spec((t, d)),
            const_spec((t, d)),
            const_spec((3, d)),
            const_spec((3, d)),
        ],
        const_spec((t, d)),
        struct((t, d), BF),
        [pltpu.VMEM((t, d), F32)],
        cost(t * d * ff, 2 * d * ff + 16 * t * d),
    )(idx, send, keep, w2, x, n1, g, b)


def ffn_bwd_kernel(
    s, cot, w2, mg, nmid, smid, slope, w1, n1, s1, n2, s2, g, wo,
    send, keep, ghid, gp_send, gp_keep, gsent, gmg, gmb, gn, bn, ebuf, ta, tan, acc,
):
    i = pl.program_id(0)
    blocks = pl.num_programs(0) // 2
    width = blocks * ebuf.shape[2]

    @pl.when(i == 0)
    def _():
        ta[...] = jnp.zeros_like(ta)
        tan[...] = jnp.zeros_like(tan)
        acc[...] = jnp.zeros_like(acc)

    @pl.when(i < blocks)
    def _():
        e = dot(cot[...], w2[...], 1, 1)
        n = nmid[0].astype(F32)
        gmg[...] = colsum(e * n)
        gmb[...] = colsum(e)
        a = e * mg[...]
        ebuf[i] = a
        ta[...] += jnp.sum(a, axis=-1, keepdims=True)
        tan[...] += jnp.sum(a * n, axis=-1, keepdims=True)

    @pl.when(i >= blocks)
    def _():
        n = nmid[0].astype(F32)
        a = ebuf[i - blocks] - ta[...] * (1.0 / width) - n * (tan[...] * (1.0 / width))
        gf = (a * smid[...] * slope[0].astype(F32)).astype(BF)

        @pl.when(i < blocks + blocks // 2)
        def _():
            send[0] = gf

        @pl.when(i >= blocks + blocks // 2)
        def _():
            keep[0] = gf

        acc[...] += dot(gf, w1[...], 1, 1)

    @pl.when(i == 2 * blocks - 1)
    def _():
        e = acc[...]
        n = n2[...]
        gn[1:2, :] = colsum(e * n)
        bn[1:2, :] = colsum(e)
        gh = cot[...].astype(F32) + ln_back(e, g[2:3, :], n, s2[...])
        ghid[...] = gh
        n = n1[...]
        gn[0:1, :] = colsum(gh * n)
        bn[0:1, :] = colsum(gh)
        gp = ln_back(gh, g[1:2, :], n, s1[...]).astype(BF)
        gsent[...] = dot(gp, wo[...], 1, 1).astype(BF)
        h = gp.shape[1] // 2

        @pl.when(s[1] == 0)
        def _():
            gp_keep[...] = gp[:, :h]
            gp_send[...] = gp[:, h:]

        @pl.when(s[1] == 1)
        def _():
            gp_keep[...] = gp[:, h:]
            gp_send[...] = gp[:, :h]


def ffn_bwd_call(idx, cot, w2, mg, nmid, smid, slope, w1, n1, s1, n2, s2, g, wo):
    t, d = cot.shape
    ff = w1.shape[1]
    bw = ff // 4
    first = lambda i: jnp.minimum(i, 3)
    second = lambda i: jnp.maximum(i - 4, 0)
    vec = pl.BlockSpec((1, bw), lambda i, s: (0, ffn_block(first(i), s)))
    return call(
        ffn_bwd_kernel,
        (8,),
        1,
        [
            const_spec((t, d)),
            pl.BlockSpec((bw, d), lambda i, s: (ffn_block(first(i), s), 0)),
            vec,
            pl.BlockSpec((1, t, bw), lambda i, s: (i % 4, 0, 0)),
            const_spec((t, 1)),
            pl.BlockSpec((1, t, bw), lambda i, s: (second(i), 0, 0)),
            pl.BlockSpec((d, bw), lambda i, s: (0, ffn_block(second(i), s))),
            const_spec((t, d)),
            const_spec((t, 1)),
            const_spec((t, d)),
            const_spec((t, 1)),
            const_spec((3, d)),
            const_spec((d, d)),
        ],
        [
            pl.BlockSpec((1, t, bw), lambda i, s: (jnp.clip(i - 4, 0, 1), 0, 0)),
            pl.BlockSpec((1, t, bw), lambda i, s: (jnp.clip(i - 6, 0, 1), 0, 0)),
            const_spec((t, d)),
            const_spec((t, d // 2)),
            const_spec((t, d // 2)),
            const_spec((t, d)),
            vec,
            vec,
            const_spec((2, d)),
            const_spec((2, d)),
        ],
        [
            struct((2, t, bw), BF),
            struct((2, t, bw), BF),
            struct((t, d), F32),
            struct((t, d // 2), BF),
            struct((t, d // 2), BF),
            struct((t, d), BF),
            struct((1, ff), F32),
            struct((1, ff), F32),
            struct((2, d), F32),
            struct((2, d), F32),
        ],
        [
            pltpu.VMEM((4, t, bw), F32),
            pltpu.VMEM((t, 1), F32),
            pltpu.VMEM((t, 1), F32),
            pltpu.VMEM((t, d), F32),
        ],
        cost(t * d * (d + 2 * ff), 2 * d * (d + 2 * ff) + 40 * t * d),
    )(idx, cot, w2, mg, nmid, smid, slope, w1, n1, s1, n2, s2, g, wo)


def in_bwd_kernel(s, send, keep, w, x, ghid, g, gx, gn, bn, acc):
    i = pl.program_id(0)

    @pl.when(i == 0)
    def _():
        acc[...] = jnp.zeros_like(acc)

    @pl.when(i < 3)
    def _():
        acc[...] += dot(send[0], w[...], 1, 1)

    @pl.when(i >= 3)
    def _():
        acc[...] += dot(keep[0], w[...], 1, 1)

    @pl.when(i == 5)
    def _():
        e = acc[...]
        n, inv = ln_stats(x[...].astype(F32))
        gn[...] = colsum(e * n)
        bn[...] = colsum(e)
        gx[...] = ghid[...] + ln_back(e, g[0:1, :], n, inv)


def in_bwd_call(idx, send, keep, w, x, ghid, g):
    t, d = x.shape
    h = d // 2
    return call(
        in_bwd_kernel,
        (6,),
        1,
        [
            pl.BlockSpec((1, t, h), lambda i, s: (jnp.minimum(i, 2), 0, 0)),
            pl.BlockSpec((1, t, h), lambda i, s: (jnp.maximum(i - 3, 0), 0, 0)),
            pl.BlockSpec((d, h), lambda i, s: (0, (i % 3) * 2 + jnp.where(i < 3, 1 - s[1], s[1]))),
            const_spec((t, d)),
            const_spec((t, d)),
            const_spec((3, d)),
        ],
        [const_spec((t, d)), const_spec((1, d)), const_spec((1, d))],
        [struct((t, d), F32), struct((1, d), F32), struct((1, d), F32)],
        [pltpu.VMEM((t, d), F32)],
        cost(3 * t * d * d, 6 * d * d + 24 * t * d),
    )(idx, send, keep, w, x, ghid, g)


def wgrad_kernel(s, a0, a1, b0, b1, send, keep):
    get = lambda r: r[...].reshape(r.shape[-2:])
    v = dot(get(a0), get(b0), 0, 0) + dot(get(a1), get(b1), 0, 0)

    @pl.when(pl.program_id(0) == 0)
    def _():
        send[...] = v.astype(BF)

    @pl.when(pl.program_id(0) == 1)
    def _():
        keep[...] = v.astype(BF)


def wgrad(idx, a, b, a_at, b_at):
    far = lambda i, s: jnp.where(i == 0, 1 - s[0], s[0])
    spec = lambda at: pl.BlockSpec(at[0], lambda i, s: at[1](far(i, s)))
    t, rows, cols = a_at[0][-2], a_at[0][-1], b_at[0][-1]
    return call(
        wgrad_kernel,
        (2,),
        1,
        [spec(a_at), spec(a_at), spec(b_at), spec(b_at)],
        [const_spec((rows, cols)), const_spec((rows, cols))],
        [struct((rows, cols), BF), struct((rows, cols), BF)],
        [],
        cost(4 * t * rows * cols, 8 * t * rows + 8 * t * cols + 4 * rows * cols),
    )(idx, a[0], a[1], b[0], b[1])


def add_split_kernel(s, *refs, terms, slot):
    f = len(refs) - terms
    i = pl.program_id(0)
    v = refs[0][...].astype(F32)
    for r in refs[1:terms]:
        v = v + r[...].astype(F32)
    v = v.astype(BF)
    for j in range(f):
        @pl.when(i == j)
        def _(j=j):
            refs[terms + j][...] = v


def add_split(idx, arrays, f, slot):
    rows, cols = arrays[0].shape
    part = rows // f
    own = pl.BlockSpec((part, cols), lambda i, s: (i ^ s[slot] if f > 1 else i, 0))
    return call(
        functools.partial(add_split_kernel, terms=len(arrays), slot=slot),
        (f,),
        1,
        [own] * len(arrays),
        [const_spec((part, cols))] * f,
        [struct((part, cols), BF)] * f,
        [],
        cost(rows * cols, (len(arrays) + 1) * 2 * rows * cols),
    )(idx, *arrays)


def factors_of(n):
    out, want, rest = [2], 2, n // 2
    while rest > 1:
        f = min(want, rest)
        out.append(f)
        rest //= f
        want *= 2
    return out


def swap(v, stride, n):
    return lax.ppermute(v, "rows", [(i, i ^ stride) for i in range(n)])


def swap_ctx(v):
    return lax.ppermute(v, "ctx", [(0, 1), (1, 0)])


def strides_of(factors):
    out, s = [], 1
    for f in factors:
        out.append(s)
        s *= f
    return out


def all_gather_pieces(piece, factors, n):
    cur = [piece]
    for f, st in reversed(list(zip(factors, strides_of(factors)))):
        if len(cur) > 2:
            cur = [jnp.concatenate(cur, axis=0)]
        cur = cur + [swap(c, j * st, n) for j in range(1, f) for c in cur]
    return cur


def all_reduce(idx, send, keep, factors):
    n = 1
    for f in factors:
        n *= f
    shape = keep.shape
    short = shape[0] * 2 // n
    if short < 16:
        keep = keep.reshape(shape[0] * 16 // short, -1)
        send = send.reshape(keep.shape)
    terms = [keep, swap_ctx(send)]
    for k, (f, st) in enumerate(list(zip(factors, strides_of(factors)))[1:]):
        parts = add_split(idx, terms, f, 2 + k)
        terms = [parts[0]] + [swap(parts[j], j * st, n) for j in range(1, f)]
    [piece] = add_split(idx, terms, 1, 2)
    return all_gather_pieces(piece, factors, n)


def finish_kernel(s, *refs, pieces, slots):
    out = refs[-1]
    i = pl.program_id(0)
    z = 0
    for slot, f in slots:
        z = z * f + s[slot]
    for j, src in enumerate(refs[:-1]):

        @pl.when(i == j)
        def _(src=src):
            part = src.shape[0] // pieces
            for k in range(pieces):
                rows = pl.ds(pl.multiple_of((k ^ z) * part, part), part)
                out[k * part : (k + 1) * part, :] = src[rows, :].astype(F32)


def finish(idx, groups, shape, place, factors):
    pieces = 1
    for f in factors[2:]:
        pieces *= f
    slots = [(3 + k, f) for k, f in enumerate(factors[2:])]
    rows, cols = groups[0][0].shape
    flat = [v for g in groups for v in g]

    def at(i, s):
        chunk = i // 4
        core = ((i // 2) % 2) ^ s[1]
        y = (i % 2) ^ s[2]
        r, c = place(chunk, core)
        return (r * 2 + y, c)

    return call(
        functools.partial(finish_kernel, pieces=pieces, slots=slots),
        (4 * len(groups),),
        1,
        [const_spec((rows, cols))] * len(flat),
        pl.BlockSpec((rows, cols), at),
        struct(shape, F32),
        [],
        cost(rows * cols * len(flat), 6 * rows * cols * len(flat)),
    )(idx, *flat)


def finish_all(idx, groups, chunk, blocks, place, factors):
    rows, cols = chunk
    shape = (blocks[0] * rows, blocks[1] * cols)
    r, c = groups[0][0].shape
    if r * 2 == rows:
        return finish(idx, groups, shape, place, factors)
    count = len(groups)
    flat = finish(idx, groups, (count * 4 * r, c), lambda j, core: (j * 2 + core, 0), factors)
    flat = flat.reshape(count, 2, rows, cols)
    out = jnp.zeros(shape, F32)
    for j in range(count):
        for core in range(2):
            a, b = place(j, core)
            out = lax.dynamic_update_slice(out, flat[j, core], (a * rows, b * cols))
    return out


def local(
    tokens, cotangent, w_qkv, w_out, w_fc1, w_fc2, norm_gain, norm_bias, mid_gain, mid_bias, head_scale, doc_lengths
):
    n = lax.axis_size("rows")
    factors = factors_of(n)
    d = tokens.shape[2]
    ff = w_fc1.shape[1]
    heads = head_scale.shape[0]
    ctx = lax.axis_index("ctx")
    row = lax.axis_index("rows")
    places = []
    rest = row
    for f in factors:
        places.append(rest % f)
        rest = rest // f
    idx = jnp.stack([ctx] + places).astype(jnp.int32)

    def whole_row(v):
        mine = lax.dynamic_index_in_dim(v, ctx, 0, False)
        got = swap_ctx(lax.dynamic_index_in_dim(v, 1 - ctx, 0, False))
        lo = jnp.where(ctx == 0, mine, got)
        hi = jnp.where(ctx == 0, got, mine)
        return jnp.concatenate([lo, hi], axis=0)

    x = whole_row(tokens)
    cot = whole_row(cotangent)
    t = x.shape[0]
    lengths = lax.dynamic_index_in_dim(doc_lengths, ctx, 0, False)
    at = jnp.arange(t, dtype=jnp.int32)
    start = jnp.zeros((t,), jnp.int32)
    bound = jnp.zeros((), jnp.int32)
    for i in range(lengths.shape[0]):
        bound = bound + lengths[i]
        start = jnp.where(at >= bound, bound, start)
    start = start[None, :]
    scale = jnp.repeat(head_scale, d // heads)[None, :]
    mg, mb = mid_gain[None, :], mid_bias[None, :]

    core = lambda v: (v, swap(v, 1, n))
    normed, qkv = qkv_call(idx, x, w_qkv, norm_gain[0:1], norm_bias[0:1])
    sent, lse = attn_fwd_call(idx, qkv, start, scale)
    n1, s1, n2, s2, ffn_in, slope, nmid, smid, mid_send, mid_keep = ffn_fwd_call(
        idx, sent, x, w_out, norm_gain, norm_bias, w_fc1, mg, mb
    )
    mid_pair = (mid_keep, swap(mid_send, 1, n))
    cot_pair = core(cot)
    gf_send, gf_keep, ghid, gp_send, gp_keep, gsent, gmg, gmb, gn12, bn12 = ffn_bwd_call(
        idx, cot, w_fc2, mg, nmid, smid, slope, w_fc1, n1, s1, n2, s2, norm_gain, w_out
    )
    half = d // 2

    def chunks(*args):
        return all_reduce(idx, *wgrad(idx, *args), factors)

    got2 = [
        chunks(mid_pair, cot_pair, ((1, t, half), lambda x, j=j: (x, 0, j)), ((t, d), lambda x: (0, 0)))
        for j in range(2)
    ]
    gf_pair = (gf_keep, swap(gf_send, 1, n))
    in_pair = core(ffn_in)
    got1 = [
        chunks(in_pair, gf_pair, ((t, half), lambda x: (0, x)), ((1, t, ff // 4), lambda x, j=j: (j, 0, 0)))
        for j in range(2)
    ]
    sent_pair = core(sent)
    gp_pair = (gp_keep, swap(gp_send, 1, n))
    got_o = [chunks(sent_pair, gp_pair, ((t, half), lambda x: (0, x)), ((t, half), lambda x: (0, 0)))]
    gq_send, gq_keep, hsum = attn_bwd_call(idx, qkv, gsent, sent, lse, start, scale)
    gq_pair = (gq_keep, swap(gq_send, 1, n))
    normed_pair = core(normed)
    got_q = [
        chunks(normed_pair, gq_pair, ((t, half), lambda x: (0, x)), ((1, t, half), lambda x, j=j: (j, 0, 0)))
        for j in range(3)
    ]
    gx, gn0, bn0 = in_bwd_call(idx, gq_send, gq_keep, w_qkv, x, ghid, norm_gain)
    out = out_call(idx, mid_send, mid_keep, w_fc2, x, n1, norm_gain, norm_bias)

    ghs = jnp.sum(hsum, axis=-1).reshape(-1) / head_scale
    small = jnp.concatenate(
        [jnp.concatenate([gn0, gn12]).reshape(-1), jnp.concatenate([bn0, bn12]).reshape(-1), gmg[0], gmb[0], ghs]
    )
    small = lax.psum(small, ("rows", "ctx"))

    def take(v, axis):
        size = v.shape[axis] // 2
        return lax.dynamic_slice_in_dim(v, ctx * size, size, axis)

    gn = take(small[: 3 * d].reshape(3, d), 1)
    bn = take(small[3 * d : 6 * d].reshape(3, d), 1)
    gmg = take(small[6 * d : 6 * d + ff], 0)
    gmb = take(small[6 * d + ff : 6 * d + 2 * ff], 0)
    ghs = take(small[6 * d + 2 * ff :], 0)

    def halves(v):
        seg = t // 2
        mine = lax.dynamic_slice_in_dim(v, ctx * seg, seg, 0)
        other = lax.dynamic_slice_in_dim(v, (1 - ctx) * seg, seg, 0)
        got = swap_ctx(other.astype(BF)).astype(v.dtype)
        lo = jnp.where(ctx == 0, mine, got)
        hi = jnp.where(ctx == 0, got, mine)
        return jnp.stack([lo, hi])

    g2 = finish_all(idx, got2, (half, d), (4, 1), lambda j, c: (c * 2 + j, 0), factors)
    g1 = finish_all(idx, got1, (half, d), (1, 4), lambda j, c: (0, j * 2 + c), factors)
    go = finish_all(idx, got_o, (half, half), (1, 2), lambda j, c: (0, c), factors)
    gq = finish_all(idx, got_q, (half, half), (1, 6), lambda j, c: (0, j * 2 + c), factors)
    return (halves(out), halves(gx), gq, go, g1, g2, gn, bn, gmg, gmb, ghs)


def solution(mesh):
    rows = P("rows", "ctx", None)
    in_specs = (rows, rows) + (P(),) * 9 + (P("rows", None),)
    ctx0 = P("ctx", None)
    out_specs = (rows, rows, ctx0, ctx0, ctx0, ctx0, P(None, "ctx"), P(None, "ctx"), P("ctx"), P("ctx"), P("ctx"))
    return jax.shard_map(local, mesh=mesh, in_specs=in_specs, out_specs=out_specs, check_vma=False)
```

```python
import functools

import jax
import jax.numpy as jnp
from jax import lax
from jax.experimental import pallas as pl
from jax.experimental.pallas import tpu as pltpu
from jax.sharding import PartitionSpec as P

EPS = 1e-05
MASKED = -1e30
BF = jnp.bfloat16
F32 = jnp.float32
REACH = 256
QB = 128
TILE = 1024


def dot(a, b, ca, cb):
    return lax.dot_general(a, b, (((ca,), (cb,)), ((), ())), preferred_element_type=F32)


def ln_stats(v):
    mean = jnp.mean(v, axis=-1, keepdims=True)
    cen = v - mean
    inv = lax.rsqrt(jnp.mean(cen * cen, axis=-1, keepdims=True) + EPS)
    return cen * inv, inv


def ln_back(e, gain, n, inv):
    a = e * gain
    return inv * (
        a - jnp.mean(a, axis=-1, keepdims=True) - n * jnp.mean(a * n, axis=-1, keepdims=True)
    )


def colsum(v):
    return jnp.sum(v, axis=0, keepdims=True)


def params(mib=60):
    return pltpu.CompilerParams(vmem_limit_bytes=mib * 2**20)


def cost(macs, nbytes, trans=0):
    return pl.CostEstimate(flops=2 * macs, bytes_accessed=nbytes, transcendentals=trans)


def call(kernel, grid, scalars, in_specs, out_specs, out_shape, scratch, ce):
    return pl.pallas_call(
        kernel,
        grid_spec=pltpu.PrefetchScalarGridSpec(
            num_scalar_prefetch=1,
            grid=grid,
            in_specs=in_specs,
            out_specs=out_specs,
            scratch_shapes=scratch,
        ),
        out_shape=out_shape,
        compiler_params=params(),
        cost_estimate=ce,
    )


def const_spec(shape):
    return pl.BlockSpec(shape, lambda i, s: (0,) * len(shape))


def struct(shape, dtype):
    return jax.ShapeDtypeStruct(shape, dtype)


def qkv_kernel(s, x, w, g, b, normed, qkv):
    @pl.when(pl.program_id(0) == 0)
    def _():
        n, _ = ln_stats(x[...].astype(F32))
        normed[...] = (n * g[...] + b[...]).astype(BF)

    qkv[0] = dot(normed[...], w[...], 1, 0).astype(BF)


def qkv_call(idx, x, w, g, b):
    t, d = x.shape
    return call(
        qkv_kernel,
        (3,),
        1,
        [
            const_spec((t, d)),
            pl.BlockSpec((d, d), lambda i, s: (0, i)),
            const_spec((1, d)),
            const_spec((1, d)),
        ],
        [const_spec((t, d)), pl.BlockSpec((1, t, d), lambda i, s: (i, 0, 0))],
        [struct((t, d), BF), struct((3, t, d), BF)],
        [],
        cost(3 * t * d * d, 2 * (3 * d * d + 5 * t * d)),
    )(idx, x, w, g, b)


def key_range(i):
    return max(0, i * QB - REACH), (i + 1) * QB


def fill_bias(start, bias, t):
    for i in range(t // QB):
        k0, k1 = key_range(i)
        u = lax.broadcasted_iota(jnp.int32, (k1 - k0, QB), 0) + k0
        q = lax.broadcasted_iota(jnp.int32, (k1 - k0, QB), 1) + i * QB
        first = start[:, i * QB : (i + 1) * QB]
        ok = (u >= first) & (u <= q)
        one = jnp.where(ok, 0.0, MASKED).astype(F32)
        bias[i, 0 : k1 - k0, 0:QB] = one
        bias[i, 0 : k1 - k0, QB : 2 * QB] = one


def both_heads(v, hd):
    lane = lax.broadcasted_iota(jnp.int32, v.shape, 1)
    zero = jnp.zeros_like(v)
    return jnp.concatenate([jnp.where(lane < hd, v, zero), jnp.where(lane < hd, zero, v)], axis=0)


def attn_fwd_kernel(s, q, k, v, start, scale, sent, lse, bias):
    t, w = q.shape[1], q.shape[2]
    hd = w // 2

    @pl.when(pl.program_id(0) == 0)
    def _():
        fill_bias(start, bias, t)

    vt = v[0].astype(F32).T.astype(BF)
    for i in range(t // QB):
        k0, k1 = key_range(i)
        qs = slice(i * QB, (i + 1) * QB)
        qm = both_heads(q[0, qs, :], hd) * (hd**-0.5)
        st = dot(k[0, k0:k1, :], qm.astype(BF), 1, 1) + bias[i, 0 : k1 - k0, :]
        top = jnp.max(st, axis=0, keepdims=True)
        pt = jnp.exp(st - top)
        total = jnp.sum(pt, axis=0, keepdims=True)
        ot = dot(vt[:, k0:k1], pt.astype(BF), 1, 0) * (1.0 / total)
        o = jnp.concatenate([ot[0:hd, 0:QB], ot[hd:, QB:]], axis=0).T
        sent[qs, :] = (o * scale[...]).astype(BF)
        ls = top + jnp.log(total)
        lse[0, 0:1, qs] = ls[:, 0:QB]
        lse[0, 1:2, qs] = ls[:, QB:]


def attn_fwd_call(idx, qkv, start, scale):
    _, t, d = qkv.shape
    pairs = d // 128
    part = lambda j: pl.BlockSpec((1, t, 128), lambda i, s: (j, 0, i))
    return call(
        attn_fwd_kernel,
        (pairs,),
        1,
        [part(0), part(1), part(2), const_spec((1, t)), pl.BlockSpec((1, 128), lambda i, s: (0, i))],
        [
            pl.BlockSpec((t, 128), lambda i, s: (0, i)),
            pl.BlockSpec((1, 2, t), lambda i, s: (i, 0, 0)),
        ],
        [struct((t, d), BF), struct((pairs, 2, t), F32)],
        [pltpu.VMEM((t // QB, QB + REACH, 2 * QB), F32)],
        cost(t * d * t * 2, 8 * t * d, t * t * 8),
    )(idx, qkv, qkv, qkv, start, scale)


def attn_bwd_kernel(s, q, k, v, gs, sent, lse, start, scale, send, keep, hsum, bias, gk, gv, gqt):
    t, w = q.shape[1], q.shape[2]
    hd = w // 2
    pid = pl.program_id(0)
    half = pl.num_programs(0) // 2

    @pl.when(pid == 0)
    def _():
        fill_bias(start, bias, t)

    kt = k[0].astype(F32).T.astype(BF)
    gsf = gs[...].astype(F32)
    prod = (gsf * sent[...].astype(F32)).T
    d0 = jnp.sum(prod[0:hd], axis=0, keepdims=True)
    d1 = jnp.sum(prod[hd:], axis=0, keepdims=True)
    hsum[0] = jnp.concatenate([d0, d1], axis=0)
    ga = (gsf * scale[...]).astype(BF)
    gk[...] = jnp.zeros_like(gk)
    gv[...] = jnp.zeros_like(gv)
    for i in range(t // QB):
        k0, k1 = key_range(i)
        qs = slice(i * QB, (i + 1) * QB)
        qm = (both_heads(q[0, qs, :], hd) * (hd**-0.5)).astype(BF)
        gm = both_heads(ga[qs, :], hd)
        st = dot(k[0, k0:k1, :], qm, 1, 1) + bias[i, 0 : k1 - k0, :]
        ls = jnp.concatenate([lse[0, 0:1, qs], lse[0, 1:2, qs]], axis=1)
        dd = jnp.concatenate([d0[:, qs], d1[:, qs]], axis=1)
        pt = jnp.exp(st - ls)
        gp = dot(v[0, k0:k1, :], gm, 1, 1)
        ds = (pt * (gp - dd)).astype(BF)
        gv[k0:k1, :] += dot(pt.astype(BF), gm, 1, 0)
        gk[k0:k1, :] += dot(ds, qm, 1, 0)
        gq = dot(kt[:, k0:k1], ds, 1, 0) * (hd**-0.5)
        gqt[:, qs] = jnp.concatenate([gq[0:hd, 0:QB], gq[hd:, QB:]], axis=0)

    def put(out):
        out[0] = gqt[...].T.astype(BF)
        out[1] = gk[...].astype(BF)
        out[2] = gv[...].astype(BF)

    pl.when(pid < half)(lambda: put(send))
    pl.when(pid >= half)(lambda: put(keep))


def attn_bwd_call(idx, qkv, gs, sent, lse, start, scale):
    _, t, d = qkv.shape
    pairs = d // 128
    half = pairs // 2

    def at(i, s):
        return jnp.where(i < half, i + (1 - s[1]) * half, i - half + s[1] * half)

    part = lambda j: pl.BlockSpec((1, t, 128), lambda i, s: (j, 0, at(i, s)))
    flat = pl.BlockSpec((t, 128), lambda i, s: (0, at(i, s)))
    return call(
        attn_bwd_kernel,
        (pairs,),
        1,
        [
            part(0),
            part(1),
            part(2),
            flat,
            flat,
            pl.BlockSpec((1, 2, t), lambda i, s: (at(i, s), 0, 0)),
            const_spec((1, t)),
            pl.BlockSpec((1, 128), lambda i, s: (0, at(i, s))),
        ],
        [
            pl.BlockSpec((3, t, 128), lambda i, s: (0, 0, jnp.minimum(i, half - 1))),
            pl.BlockSpec((3, t, 128), lambda i, s: (0, 0, jnp.maximum(i - half, 0))),
            pl.BlockSpec((1, 2, t), lambda i, s: (at(i, s), 0, 0)),
        ],
        [
            struct((3, t, d // 2), BF),
            struct((3, t, d // 2), BF),
            struct((pairs, 2, t), F32),
        ],
        [
            pltpu.VMEM((t // QB, QB + REACH, 2 * QB), F32),
            pltpu.VMEM((t, 128), F32),
            pltpu.VMEM((t, 128), F32),
            pltpu.VMEM((128, t), F32),
        ],
        cost(t * d * t * 5, 16 * t * d, t * t * 8),
    )(idx, qkv, qkv, qkv, gs, sent, lse, start, scale)


def ffn_block(i, s):
    return (i % 2) * 2 + jnp.where(i < 2, 1 - s[1], s[1])


def ffn_fwd_kernel(
    s, sent, x, wo, g, b, w1, mg, mb, n1, s1, n2, s2, ffn_in, slope, nmid, smid, send, keep, act, tot
):
    i = pl.program_id(0)
    blocks = pl.num_programs(0) // 2
    width = blocks * act.shape[2]

    @pl.when(i == 0)
    def _():
        n, inv = ln_stats(dot(sent[...], wo[...], 1, 0))
        n1[...] = n
        s1[...] = inv
        hidden = x[...].astype(F32) + n * g[1:2, :] + b[1:2, :]
        n, inv = ln_stats(hidden)
        n2[...] = n
        s2[...] = inv
        ffn_in[...] = (n * g[2:3, :] + b[2:3, :]).astype(BF)
        tot[...] = jnp.zeros_like(tot)

    @pl.when(i < blocks)
    def _():
        f = dot(ffn_in[...], w1[...], 1, 0)
        phi = 0.5 + 0.5 * lax.erf(f * (0.5**0.5))
        a = f * phi
        slope[0] = (phi + f * (jnp.exp(-0.5 * f * f) * 0.3989422804014327)).astype(BF)
        act[i] = a
        tot[...] += jnp.sum(a, axis=-1, keepdims=True)

    @pl.when(i == blocks)
    def _():
        mean = tot[...] * (1.0 / width)
        sq = jnp.zeros_like(mean)
        for j in range(4):
            c = act[j] - mean
            act[j] = c
            sq += jnp.sum(c * c, axis=-1, keepdims=True)
        smid[...] = lax.rsqrt(sq * (1.0 / width) + EPS)

    @pl.when(i >= blocks)
    def _():
        n = act[i - blocks] * smid[...]
        nmid[0] = n.astype(BF)
        m = (n * mg[...] + mb[...]).astype(BF)

        @pl.when(i < blocks + blocks // 2)
        def _():
            send[0] = m

        @pl.when(i >= blocks + blocks // 2)
        def _():
            keep[0] = m


def ffn_fwd_call(idx, sent, x, wo, g, b, w1, mg, mb):
    t, d = x.shape
    ff = w1.shape[1]
    bw = ff // 4
    first = lambda i: jnp.minimum(i, 3)
    second = lambda i: jnp.maximum(i - 4, 0)
    vec = pl.BlockSpec((1, bw), lambda i, s: (0, ffn_block(second(i), s)))
    return call(
        ffn_fwd_kernel,
        (8,),
        1,
        [
            const_spec((t, d)),
            const_spec((t, d)),
            const_spec((d, d)),
            const_spec((3, d)),
            const_spec((3, d)),
            pl.BlockSpec((d, bw), lambda i, s: (0, ffn_block(first(i), s))),
            vec,
            vec,
        ],
        [
            const_spec((t, d)),
            const_spec((t, 1)),
            const_spec((t, d)),
            const_spec((t, 1)),
            const_spec((t, d)),
            pl.BlockSpec((1, t, bw), lambda i, s: (first(i), 0, 0)),
            pl.BlockSpec((1, t, bw), lambda i, s: (second(i), 0, 0)),
            const_spec((t, 1)),
            pl.BlockSpec((1, t, bw), lambda i, s: (jnp.clip(i - 4, 0, 1), 0, 0)),
            pl.BlockSpec((1, t, bw), lambda i, s: (jnp.clip(i - 6, 0, 1), 0, 0)),
        ],
        [
            struct((t, d), F32),
            struct((t, 1), F32),
            struct((t, d), F32),
            struct((t, 1), F32),
            struct((t, d), BF),
            struct((4, t, bw), BF),
            struct((4, t, bw), BF),
            struct((t, 1), F32),
            struct((2, t, bw), BF),
            struct((2, t, bw), BF),
        ],
        [pltpu.VMEM((4, t, bw), F32), pltpu.VMEM((t, 1), F32)],
        cost(t * d * (d + ff), 2 * d * (d + ff) + 30 * t * d, 2 * t * ff),
    )(idx, sent, x, wo, g, b, w1, mg, mb)


def out_kernel(s, send, keep, w2, x, n1, g, b, out, acc):
    i = pl.program_id(0)

    @pl.when(i == 0)
    def _():
        acc[...] = x[...].astype(F32) + n1[...] * g[1:2, :] + b[1:2, :]

    @pl.when(i < 2)
    def _():
        acc[...] += dot(send[0], w2[...], 1, 0)

    @pl.when(i >= 2)
    def _():
        acc[...] += dot(keep[0], w2[...], 1, 0)

    @pl.when(i == 3)
    def _():
        out[...] = acc[...].astype(BF)


def out_call(idx, send, keep, w2, x, n1, g, b):
    t, d = x.shape
    ff = w2.shape[0]
    bw = ff // 4
    return call(
        out_kernel,
        (4,),
        1,
        [
            pl.BlockSpec((1, t, bw), lambda i, s: (jnp.clip(i, 0, 1), 0, 0)),
            pl.BlockSpec((1, t, bw), lambda i, s: (jnp.clip(i - 2, 0, 1), 0, 0)),
            pl.BlockSpec((bw, d), lambda i, s: (ffn_block(i, s), 0)),
            const_spec((t, d)),
            const_spec((t, d)),
            const_spec((3, d)),
            const_spec((3, d)),
        ],
        const_spec((t, d)),
        struct((t, d), BF),
        [pltpu.VMEM((t, d), F32)],
        cost(t * d * ff, 2 * d * ff + 16 * t * d),
    )(idx, send, keep, w2, x, n1, g, b)


def ffn_bwd_kernel(
    s, cot, w2, mg, nmid, smid, slope, w1, n1, s1, n2, s2, g, wo,
    send, keep, ghid, gp_send, gp_keep, gsent, gmg, gmb, gn, bn, ebuf, ta, tan, acc,
):
    i = pl.program_id(0)
    blocks = pl.num_programs(0) // 2
    width = blocks * ebuf.shape[2]

    @pl.when(i == 0)
    def _():
        ta[...] = jnp.zeros_like(ta)
        tan[...] = jnp.zeros_like(tan)
        acc[...] = jnp.zeros_like(acc)

    @pl.when(i < blocks)
    def _():
        e = dot(cot[...], w2[...], 1, 1)
        n = nmid[0].astype(F32)
        gmg[...] = colsum(e * n)
        gmb[...] = colsum(e)
        a = e * mg[...]
        ebuf[i] = a
        ta[...] += jnp.sum(a, axis=-1, keepdims=True)
        tan[...] += jnp.sum(a * n, axis=-1, keepdims=True)

    @pl.when(i >= blocks)
    def _():
        n = nmid[0].astype(F32)
        a = ebuf[i - blocks] - ta[...] * (1.0 / width) - n * (tan[...] * (1.0 / width))
        gf = (a * smid[...] * slope[0].astype(F32)).astype(BF)

        @pl.when(i < blocks + blocks // 2)
        def _():
            send[0] = gf

        @pl.when(i >= blocks + blocks // 2)
        def _():
            keep[0] = gf

        acc[...] += dot(gf, w1[...], 1, 1)

    @pl.when(i == 2 * blocks - 1)
    def _():
        e = acc[...]
        n = n2[...]
        gn[1:2, :] = colsum(e * n)
        bn[1:2, :] = colsum(e)
        gh = cot[...].astype(F32) + ln_back(e, g[2:3, :], n, s2[...])
        ghid[...] = gh
        n = n1[...]
        gn[0:1, :] = colsum(gh * n)
        bn[0:1, :] = colsum(gh)
        gp = ln_back(gh, g[1:2, :], n, s1[...]).astype(BF)
        gsent[...] = dot(gp, wo[...], 1, 1).astype(BF)
        h = gp.shape[1] // 2

        @pl.when(s[1] == 0)
        def _():
            gp_keep[...] = gp[:, :h]
            gp_send[...] = gp[:, h:]

        @pl.when(s[1] == 1)
        def _():
            gp_keep[...] = gp[:, h:]
            gp_send[...] = gp[:, :h]


def ffn_bwd_call(idx, cot, w2, mg, nmid, smid, slope, w1, n1, s1, n2, s2, g, wo):
    t, d = cot.shape
    ff = w1.shape[1]
    bw = ff // 4
    first = lambda i: jnp.minimum(i, 3)
    second = lambda i: jnp.maximum(i - 4, 0)
    vec = pl.BlockSpec((1, bw), lambda i, s: (0, ffn_block(first(i), s)))
    return call(
        ffn_bwd_kernel,
        (8,),
        1,
        [
            const_spec((t, d)),
            pl.BlockSpec((bw, d), lambda i, s: (ffn_block(first(i), s), 0)),
            vec,
            pl.BlockSpec((1, t, bw), lambda i, s: (i % 4, 0, 0)),
            const_spec((t, 1)),
            pl.BlockSpec((1, t, bw), lambda i, s: (second(i), 0, 0)),
            pl.BlockSpec((d, bw), lambda i, s: (0, ffn_block(second(i), s))),
            const_spec((t, d)),
            const_spec((t, 1)),
            const_spec((t, d)),
            const_spec((t, 1)),
            const_spec((3, d)),
            const_spec((d, d)),
        ],
        [
            pl.BlockSpec((1, t, bw), lambda i, s: (jnp.clip(i - 4, 0, 1), 0, 0)),
            pl.BlockSpec((1, t, bw), lambda i, s: (jnp.clip(i - 6, 0, 1), 0, 0)),
            const_spec((t, d)),
            const_spec((t, d // 2)),
            const_spec((t, d // 2)),
            const_spec((t, d)),
            vec,
            vec,
            const_spec((2, d)),
            const_spec((2, d)),
        ],
        [
            struct((2, t, bw), BF),
            struct((2, t, bw), BF),
            struct((t, d), F32),
            struct((t, d // 2), BF),
            struct((t, d // 2), BF),
            struct((t, d), BF),
            struct((1, ff), F32),
            struct((1, ff), F32),
            struct((2, d), F32),
            struct((2, d), F32),
        ],
        [
            pltpu.VMEM((4, t, bw), F32),
            pltpu.VMEM((t, 1), F32),
            pltpu.VMEM((t, 1), F32),
            pltpu.VMEM((t, d), F32),
        ],
        cost(t * d * (d + 2 * ff), 2 * d * (d + 2 * ff) + 40 * t * d),
    )(idx, cot, w2, mg, nmid, smid, slope, w1, n1, s1, n2, s2, g, wo)


def in_bwd_kernel(s, send, keep, w, x, ghid, g, gx, gn, bn, acc):
    i = pl.program_id(0)

    @pl.when(i == 0)
    def _():
        acc[...] = jnp.zeros_like(acc)

    @pl.when(i < 3)
    def _():
        acc[...] += dot(send[0], w[...], 1, 1)

    @pl.when(i >= 3)
    def _():
        acc[...] += dot(keep[0], w[...], 1, 1)

    @pl.when(i == 5)
    def _():
        e = acc[...]
        n, inv = ln_stats(x[...].astype(F32))
        gn[...] = colsum(e * n)
        bn[...] = colsum(e)
        gx[...] = ghid[...] + ln_back(e, g[0:1, :], n, inv)


def in_bwd_call(idx, send, keep, w, x, ghid, g):
    t, d = x.shape
    h = d // 2
    return call(
        in_bwd_kernel,
        (6,),
        1,
        [
            pl.BlockSpec((1, t, h), lambda i, s: (jnp.minimum(i, 2), 0, 0)),
            pl.BlockSpec((1, t, h), lambda i, s: (jnp.maximum(i - 3, 0), 0, 0)),
            pl.BlockSpec((d, h), lambda i, s: (0, (i % 3) * 2 + jnp.where(i < 3, 1 - s[1], s[1]))),
            const_spec((t, d)),
            const_spec((t, d)),
            const_spec((3, d)),
        ],
        [const_spec((t, d)), const_spec((1, d)), const_spec((1, d))],
        [struct((t, d), F32), struct((1, d), F32), struct((1, d), F32)],
        [pltpu.VMEM((t, d), F32)],
        cost(3 * t * d * d, 6 * d * d + 24 * t * d),
    )(idx, send, keep, w, x, ghid, g)


def wgrad_kernel(s, *refs):
    ops, (send, keep) = refs[:-2], refs[-2:]
    i = pl.program_id(0)
    get = lambda r: r[...].reshape(r.shape[-2:])

    def chunk(at):
        a0, a1, b0, b1 = [get(r) for r in ops[4 * at : 4 * at + 4]]
        v = (dot(a0, b0, 0, 0) + dot(a1, b1, 0, 0)).astype(BF)

        @pl.when(i % 2 == 0)
        def _():
            send[0] = v

        @pl.when(i % 2 == 1)
        def _():
            keep[0] = v

    k = i // 2
    pl.when(k < 4)(lambda: chunk(0))
    pl.when((k >= 4) & (k < 8))(lambda: chunk(1))
    pl.when(k == 8)(lambda: chunk(2))
    pl.when(k > 8)(lambda: chunk(3))


def wgrad_call(idx, mid, cot, ffn_in, gf, sent, gp, normed, gq):
    t, d = cot[0].shape
    h = d // 2

    def spec(shape, at, lo, hi):
        def index(i, s):
            i = jnp.clip(i, 2 * lo, 2 * hi + 1)
            x = jnp.where(i % 2 == 0, 1 - s[0], s[0])
            return at(i // 2 - lo, x)

        return pl.BlockSpec(shape, index)

    pair = lambda *a: [spec(*a)] * 2
    specs = (
        pair((1, t, h), lambda k, x: (x, 0, k // 2), 0, 3)
        + pair((t, h), lambda k, x: (0, k % 2), 0, 3)
        + pair((t, h), lambda k, x: (0, x), 4, 7)
        + pair((1, t, h), lambda k, x: (k // 2, 0, k % 2), 4, 7)
        + pair((t, h), lambda k, x: (0, x), 8, 8)
        + pair((t, h), lambda k, x: (0, 0), 8, 8)
        + pair((t, h), lambda k, x: (0, x), 9, 11)
        + pair((1, t, h), lambda k, x: (k, 0, 0), 9, 11)
    )
    out = lambda o: pl.BlockSpec((1, h, h), lambda i, s: (jnp.clip((i - o) // 2, 0, 11), 0, 0))
    return call(
        wgrad_kernel,
        (24,),
        1,
        specs,
        [pl.BlockSpec((1, h, h), lambda i, s: (i // 2, 0, 0))] * 2,
        [struct((12, h, h), BF)] * 2,
        [],
        cost(48 * t * h * h, 48 * t * h * 2),
    )(idx, *mid, *cot, *ffn_in, *gf, *sent, *gp, *normed, *gq)


def factors_of(n):
    out, want, rest = [2], 2, n // 2
    while rest > 1:
        f = min(want, rest)
        out.append(f)
        rest //= f
        want *= 2
    return out


def reduce_kernel(factors, send, keep, small, out, small_out, *scr):
    n_rs = len(factors)
    chunks, rows, cols = send.shape
    me = lax.axis_index("rows")
    ctx = lax.axis_index("ctx")
    fs = [2] + factors[1:]
    strides, st = [0], 2
    for f in factors[1:]:
        strides.append(st)
        st *= f
    size = [rows]
    for f in fs[1:]:
        size.append(size[-1] // f)
    pos = [ctx] + [lax.rem(me // strides[i], fs[i]) for i in range(1, n_rs)]
    off = [0]
    for i in range(1, n_rs):
        off.append(off[-1] + pos[i] * size[i])
    bits = []
    b = 1
    while b < lax.axis_size("rows"):
        bits.append(b)
        b *= 2

    def peer(i, j):
        if i == 0:
            return (me, 1 - ctx)
        return (me + ((pos[i] ^ j) - pos[i]) * strides[i], ctx)

    core = lax.rem(me, 2)
    sibling = (me + 1 - 2 * core, ctx)

    def bit_peer(b):
        return (me + b - 2 * b * lax.rem(me // b, 2), ctx)

    scr = list(scr)
    acc = scr.pop(0)
    gath = scr.pop(0)
    recv = [gath] + [scr.pop(0) for _ in range(1, n_rs)]
    small_acc, small_recv = scr.pop(0), scr.pop(0)
    rs_s = [scr.pop(0) for _ in range(n_rs)]
    rs_r = [scr.pop(0) for _ in range(n_rs)]
    ag_s = [None] + [scr.pop(0) for _ in range(1, n_rs)]
    ag_r = [None] + [scr.pop(0) for _ in range(1, n_rs)]
    core_s, core_r, loc, small_s, small_r = scr

    def part(at, n):
        return pl.ds(at if isinstance(at, int) else pl.multiple_of(at, 16), n)

    def rs_copy(i, k, j):
        if i == 0:
            src, dst = send.at[k], gath.at[k]
        else:
            src = acc.at[k, part(off[i - 1] + (pos[i] ^ j) * size[i], size[i])]
            dst = recv[i].at[k, j - 1]
        return pltpu.make_async_remote_copy(
            src, dst, rs_s[i].at[k, j - 1], rs_r[i].at[k, j - 1],
            device_id=peer(i, j), device_id_type=pl.DeviceIdType.MESH,
        )

    def ag_copy(i, k, j, arriving):
        at = off[i - 1] + (pos[i] ^ j) * size[i] if arriving else off[i]
        ref = gath.at[k, part(at, size[i])]
        return pltpu.make_async_remote_copy(
            ref, ref, ag_s[i].at[k, j - 1], ag_r[i].at[k, j - 1],
            device_id=peer(i, j), device_id_type=pl.DeviceIdType.MESH,
        )

    def core_copy(k, arriving):
        to = 1 - core if arriving else core
        return pltpu.make_async_remote_copy(
            gath.at[k], out.at[k, to], core_s.at[k], core_r.at[k],
            device_id=sibling, device_id_type=pl.DeviceIdType.MESH,
        )

    def own_copy(k):
        return pltpu.make_async_copy(gath.at[k], out.at[k, core], loc.at[k])

    def reduce_stage(i, k):
        for j in range(1, fs[i]):
            rs_copy(i, k, j).wait_recv()
        here = part(off[i], size[i])
        if i == 0:
            v = keep[k].astype(F32) + gath[k].astype(F32)
        else:
            v = acc[k, here].astype(F32)
            for j in range(1, fs[i]):
                v = v + recv[i][k, j - 1].astype(F32)
        if i + 1 < n_rs:
            acc[k, here] = v.astype(BF)
            for j in range(1, fs[i + 1]):
                rs_copy(i + 1, k, j).start()
        else:
            gath[k, here] = v.astype(BF)
            for j in range(1, fs[i]):
                ag_copy(i, k, j, False).start()

    def gather_stage(i, k):
        for j in range(1, fs[i]):
            ag_copy(i, k, j, True).wait_recv()
        if i > 1:
            for j in range(1, fs[i - 1]):
                ag_copy(i - 1, k, j, False).start()
        else:
            core_copy(k, False).start()
            own_copy(k).start()

    def small_copy(i):
        to = (me, 1 - ctx) if i == 0 else bit_peer(bits[i - 1])
        return pltpu.make_async_remote_copy(
            small_acc.at[i], small_recv.at[i], small_s.at[i], small_r.at[i],
            device_id=to, device_id_type=pl.DeviceIdType.MESH,
        )

    peers = [(me, 1 - ctx), sibling]
    for i in range(1, n_rs):
        peers += [peer(i, j) for j in range(1, fs[i])]
    barrier = pltpu.get_barrier_semaphore()
    for p in peers:
        pl.semaphore_signal(barrier, inc=1, device_id=p, device_id_type=pl.DeviceIdType.MESH)
    pl.semaphore_wait(barrier, len(peers))

    small_acc[0] = small[...]
    small_copy(0).start()

    def first(k, _):
        rs_copy(0, k, 1).start()
        return 0

    lax.fori_loop(0, chunks, first, 0)

    lanes = 2 * n_rs - 1
    steps = [functools.partial(reduce_stage, i) for i in range(n_rs)]
    steps += [functools.partial(gather_stage, i) for i in range(n_rs - 1, 0, -1)]

    def step(t, _):
        for lag in range(lanes - 1, -1, -1):
            k = t - lag

            @pl.when((k >= 0) & (k < chunks))
            def _(k=k, lag=lag):
                steps[lag](k)

        for i in range(len(bits) + 1):

            @pl.when(t == i)
            def _(i=i):
                small_copy(i).wait_recv()
                if i < len(bits):
                    small_acc[i + 1] = small_acc[i] + small_recv[i]
                    small_copy(i + 1).start()
                else:
                    small_out[...] = small_acc[i] + small_recv[i]

        return 0

    lax.fori_loop(0, chunks + lanes - 1, step, 0)

    def last(k, _):
        for i in range(n_rs):
            for j in range(1, fs[i]):
                rs_copy(i, k, j).wait_send()
                if i > 0:
                    ag_copy(i, k, j, False).wait_send()
        core_copy(k, False).wait_send()
        core_copy(k, True).wait_recv()
        own_copy(k).wait()
        return 0

    lax.fori_loop(0, chunks, last, 0)
    for i in range(len(bits) + 1):
        small_copy(i).wait_send()


def reduce_call(send, keep, small, factors):
    chunks, rows, cols = send.shape
    n = 1
    for f in factors:
        n *= f
    fs = [2] + factors[1:]
    levels = 1
    while n > 1:
        levels += 1
        n //= 2
    size, recv = rows, []
    for f in fs[1:]:
        size //= f
        recv.append(pltpu.VMEM((chunks, f - 1, size, cols), BF))
    dma = lambda *shape: pltpu.SemaphoreType.DMA(shape)
    per = lambda k: [dma(chunks, f - 1) for f in fs[k:]]
    return pl.pallas_call(
        functools.partial(reduce_kernel, factors),
        in_specs=[
            pl.BlockSpec(memory_space=pl.ANY),
            pl.BlockSpec(memory_space=pltpu.VMEM),
            pl.BlockSpec(memory_space=pltpu.VMEM),
        ],
        out_specs=[pl.BlockSpec(memory_space=pl.ANY), pl.BlockSpec(memory_space=pltpu.VMEM)],
        out_shape=[struct((chunks, 2, rows, cols), BF), struct(small.shape, F32)],
        scratch_shapes=[pltpu.VMEM((chunks, rows, cols), BF)] * 2
        + recv
        + [pltpu.VMEM((levels,) + small.shape, F32)] * 2
        + per(0) + per(0) + per(1) + per(1)
        + [dma(chunks), dma(chunks), dma(chunks), dma(levels), dma(levels)],
        compiler_params=pltpu.CompilerParams(
            collective_id=0, has_side_effects=True, vmem_limit_bytes=60 * 2**20
        ),
    )(send, keep, small)


def sum_over_devices(send, keep, small, factors):
    chunks, rows, cols = send.shape
    pieces = 1
    for f in factors[1:]:
        pieces *= f
    r = max(rows, 16 * pieces)
    flat = lambda v: v if r == rows else v.reshape(chunks, r, rows * cols // r)
    got, small = reduce_call(flat(send), flat(keep), small, factors)
    return got.reshape(chunks, 2, rows, cols), small


def finish_kernel(s, got, g2, g1, go, gq):
    k = pl.program_id(0) // 2
    v = got[0, 0].astype(F32)

    def put(out):
        out[...] = v

    pl.when(k < 4)(lambda: put(g2))
    pl.when((k >= 4) & (k < 8))(lambda: put(g1))
    pl.when(k == 8)(lambda: put(go))
    pl.when(k > 8)(lambda: put(gq))


def finish_call(idx, got, ff, d):
    h = d // 2

    def spec(lo, hi, at):
        def index(i, s):
            i = jnp.clip(i, 2 * lo, 2 * hi + 1)
            return at(i // 2 - lo, i % 2)

        return pl.BlockSpec((h, h), index)

    return call(
        finish_kernel,
        (24,),
        1,
        [pl.BlockSpec((1, 1, h, h), lambda i, s: (i // 2, i % 2, 0, 0))],
        [
            spec(0, 3, lambda k, c: (c * 2 + k // 2, k % 2)),
            spec(4, 7, lambda k, c: (0, ((k // 2) * 2 + c) * 2 + k % 2)),
            spec(8, 8, lambda k, c: (0, c)),
            spec(9, 11, lambda k, c: (0, k * 2 + c)),
        ],
        [struct((ff // 2, d), F32), struct((h, ff), F32), struct((h, d), F32), struct((h, 3 * d), F32)],
        [],
        cost(0, 24 * h * h * 6),
    )(idx, got)


def swap(v, stride, n):
    return lax.ppermute(v, "rows", [(i, i ^ stride) for i in range(n)])


def swap_ctx(v):
    return lax.ppermute(v, "ctx", [(0, 1), (1, 0)])


def local(
    tokens, cotangent, w_qkv, w_out, w_fc1, w_fc2, norm_gain, norm_bias, mid_gain, mid_bias, head_scale, doc_lengths
):
    n = lax.axis_size("rows")
    factors = factors_of(n)
    d = tokens.shape[2]
    ff = w_fc1.shape[1]
    heads = head_scale.shape[0]
    ctx = lax.axis_index("ctx")
    row = lax.axis_index("rows")
    places = []
    rest = row
    for f in factors:
        places.append(rest % f)
        rest = rest // f
    idx = jnp.stack([ctx] + places).astype(jnp.int32)

    def whole_row(v):
        mine = lax.dynamic_index_in_dim(v, ctx, 0, False)
        got = swap_ctx(lax.dynamic_index_in_dim(v, 1 - ctx, 0, False))
        lo = jnp.where(ctx == 0, mine, got)
        hi = jnp.where(ctx == 0, got, mine)
        return jnp.concatenate([lo, hi], axis=0)

    x = whole_row(tokens)
    cot = whole_row(cotangent)
    t = x.shape[0]
    lengths = lax.dynamic_index_in_dim(doc_lengths, ctx, 0, False)
    at = jnp.arange(t, dtype=jnp.int32)
    start = jnp.zeros((t,), jnp.int32)
    bound = jnp.zeros((), jnp.int32)
    for i in range(lengths.shape[0]):
        bound = bound + lengths[i]
        start = jnp.where(at >= bound, bound, start)
    start = start[None, :]
    scale = jnp.repeat(head_scale, d // heads)[None, :]
    mg, mb = mid_gain[None, :], mid_bias[None, :]

    core = lambda v: (v, swap(v, 1, n))
    normed, qkv = qkv_call(idx, x, w_qkv, norm_gain[0:1], norm_bias[0:1])
    sent, lse = attn_fwd_call(idx, qkv, start, scale)
    n1, s1, n2, s2, ffn_in, slope, nmid, smid, mid_send, mid_keep = ffn_fwd_call(
        idx, sent, x, w_out, norm_gain, norm_bias, w_fc1, mg, mb
    )
    mid_pair = (mid_keep, swap(mid_send, 1, n))
    cot_pair = core(cot)
    gf_send, gf_keep, ghid, gp_send, gp_keep, gsent, gmg, gmb, gn12, bn12 = ffn_bwd_call(
        idx, cot, w_fc2, mg, nmid, smid, slope, w_fc1, n1, s1, n2, s2, norm_gain, w_out
    )
    gq_send, gq_keep, hsum = attn_bwd_call(idx, qkv, gsent, sent, lse, start, scale)
    gx, gn0, bn0 = in_bwd_call(idx, gq_send, gq_keep, w_qkv, x, ghid, norm_gain)
    out = out_call(idx, mid_send, mid_keep, w_fc2, x, n1, norm_gain, norm_bias)

    ghs = jnp.sum(hsum, axis=-1).reshape(-1) / head_scale
    small = jnp.concatenate(
        [jnp.concatenate([gn0, gn12]).reshape(-1), jnp.concatenate([bn0, bn12]).reshape(-1), gmg[0], gmb[0], ghs]
    )
    pad = -small.shape[0] % 1024
    small = jnp.pad(small, (0, pad)).reshape(-1, 128)
    send, keep = wgrad_call(
        idx,
        mid_pair,
        cot_pair,
        core(ffn_in),
        (gf_keep, swap(gf_send, 1, n)),
        core(sent),
        (gp_keep, swap(gp_send, 1, n)),
        core(normed),
        (gq_keep, swap(gq_send, 1, n)),
    )
    got, small = sum_over_devices(send, keep, small, factors)
    small = small.reshape(-1)
    g2, g1, go, gq = finish_call(idx, got, ff, d)

    def take(v, axis):
        size = v.shape[axis] // 2
        return lax.dynamic_slice_in_dim(v, ctx * size, size, axis)

    gn = take(small[: 3 * d].reshape(3, d), 1)
    bn = take(small[3 * d : 6 * d].reshape(3, d), 1)
    gmg = take(small[6 * d : 6 * d + ff], 0)
    gmb = take(small[6 * d + ff : 6 * d + 2 * ff], 0)
    ghs = take(small[6 * d + 2 * ff : 6 * d + 2 * ff + heads], 0)

    def halves(v):
        seg = t // 2
        mine = lax.dynamic_slice_in_dim(v, ctx * seg, seg, 0)
        other = lax.dynamic_slice_in_dim(v, (1 - ctx) * seg, seg, 0)
        got = swap_ctx(other.astype(BF)).astype(v.dtype)
        lo = jnp.where(ctx == 0, mine, got)
        hi = jnp.where(ctx == 0, got, mine)
        return jnp.stack([lo, hi])

    return (halves(out), halves(gx), gq, go, g1, g2, gn, bn, gmg, gmb, ghs)


def solution(mesh):
    rows = P("rows", "ctx", None)
    in_specs = (rows, rows) + (P(),) * 9 + (P("rows", None),)
    ctx0 = P("ctx", None)
    out_specs = (rows, rows, ctx0, ctx0, ctx0, ctx0, P(None, "ctx"), P(None, "ctx"), P("ctx"), P("ctx"), P("ctx"))
    return jax.shard_map(local, mesh=mesh, in_specs=in_specs, out_specs=out_specs, check_vma=False)
```

```python
import functools

import jax
import jax.numpy as jnp
from jax import lax
from jax.experimental import pallas as pl
from jax.experimental.pallas import tpu as pltpu
from jax.sharding import PartitionSpec as P

EPS = 1e-05
MASKED = -1e30
BF = jnp.bfloat16
F32 = jnp.float32
REACH = 256
QB = 128


def dot(a, b, ca, cb):
    return lax.dot_general(a, b, (((ca,), (cb,)), ((), ())), preferred_element_type=F32)


def ln_stats(v):
    mean = jnp.mean(v, axis=-1, keepdims=True)
    cen = v - mean
    inv = lax.rsqrt(jnp.mean(cen * cen, axis=-1, keepdims=True) + EPS)
    return cen * inv, inv


def ln_back(e, gain, n, inv):
    a = e * gain
    return inv * (
        a - jnp.mean(a, axis=-1, keepdims=True) - n * jnp.mean(a * n, axis=-1, keepdims=True)
    )


def colsum(v):
    return jnp.sum(v, axis=0, keepdims=True)


def struct(shape, dtype):
    return jax.ShapeDtypeStruct(shape, dtype)


def key_range(i):
    return max(0, i * QB - REACH), (i + 1) * QB


def fill_bias(start, bias, t):
    for i in range(t // QB):
        k0, k1 = key_range(i)
        u = lax.broadcasted_iota(jnp.int32, (k1 - k0, QB), 0) + k0
        q = lax.broadcasted_iota(jnp.int32, (k1 - k0, QB), 1) + i * QB
        first = start[:, i * QB : (i + 1) * QB]
        ok = (u >= first) & (u <= q)
        one = jnp.where(ok, 0.0, MASKED).astype(F32)
        bias[i, 0 : k1 - k0, 0:QB] = one
        bias[i, 0 : k1 - k0, QB : 2 * QB] = one


def both_heads(v, hd):
    lane = lax.broadcasted_iota(jnp.int32, v.shape, 1)
    zero = jnp.zeros_like(v)
    return jnp.concatenate([jnp.where(lane < hd, v, zero), jnp.where(lane < hd, zero, v)], axis=0)


def put_chunk(ref, k, v):
    h, c = v.shape[0], ref.shape[2]
    for m in range(v.shape[1] // c):
        ref[k, m * h : (m + 1) * h, :] = v[:, m * c : (m + 1) * c]


PRE = 3
CHUNKS = 12
F_Q1, F_Q2, F_AT, F_FC, F_NM, F_B1, F_A, F_O, F_B2, F_END = 0, 3, 6, 14, 18, 22, 26, 30, 34, 38
MESH = pl.DeviceIdType.MESH


def remote(src, dst, ss, rs, to):
    return pltpu.make_async_remote_copy(src, dst, ss, rs, device_id=to, device_id_type=MESH)


def head_lanes(scale, pair, shape, hd):
    lane = lax.broadcasted_iota(jnp.int32, shape, 1)
    return jnp.where(lane < hd, scale[2 * pair], scale[2 * pair + 1])


def front_kernel(lengths, scale, gain, offset, mg, mb, h_tok, h_cot, h_wqkv, h_wo, h_w1, h_w2,
                 o_x, o_nrm, o_qkv, o_sent, lse, o_ffn, o_gf, o_gp, o_gs, o_gh, o_out, o_keep, o_last, pre, small,
                 wb, wo, xb, cotb, nrm, qkvb, sent, bias, act, mid, nmid, gfb, r_mid, r_cot, n1, n2, hid, acc, ffn,
                 sendw, keepw, s1, s2, smid, ta, tb, wsem, lsem, osem, ss, rs):
    tick = pl.program_id(0)
    me = lax.axis_index("rows")
    ctx = lax.axis_index("ctx")
    core = lax.rem(me, 2)
    sibling = (me + 1 - 2 * core, ctx)
    other_ctx = (me, 1 - ctx)
    t, d = xb.shape
    seg = t // 2
    blocks = act.shape[0]
    width = blocks * act.shape[2]
    h = d // 2

    def rows_of(c):
        return pl.ds(pl.multiple_of(c * seg, seg), seg)

    def w_copy(ref, i):
        return pltpu.make_async_copy(ref, wb.at[lax.rem(i, 3)], wsem.at[lax.rem(i, 3)])

    def col(ref, i):
        return ref.at[:, pl.ds(pl.multiple_of(i * d, d), d)]

    def row(ref, i):
        return ref.at[pl.ds(pl.multiple_of(i * d, d), d), :]

    def w_start(i):
        pl.when(i < 6)(lambda: w_copy(col(h_wqkv, lax.rem(i, 3)), i).start())
        pl.when((i >= 6) & (i < 10))(lambda: w_copy(col(h_w1, i - 6), i).start())
        pl.when((i >= 10) & (i < 18))(lambda: w_copy(row(h_w2, lax.rem(i - 10, 4)), i).start())
        pl.when((i >= 18) & (i < 22))(lambda: w_copy(col(h_w1, i - 18), i).start())

    def w_next(i):
        w_copy(row(h_w2, 0), i).wait()
        w_start(i + 2)
        return wb.at[lax.rem(i, 3)]

    def tok_copy():
        return remote(h_tok.at[1 - ctx], xb.at[rows_of(ctx)], ss.at[0], rs.at[0], other_ctx)

    def cot_copy():
        return remote(h_cot.at[1 - ctx], cotb.at[rows_of(ctx)], ss.at[1], rs.at[1], other_ctx)

    def cot_core():
        return remote(cotb, r_cot, ss.at[2], rs.at[2], sibling)

    def mid_core(i):
        return remote(mid.at[2 * i + 1 - core], r_mid.at[i], ss.at[3 + i], rs.at[3 + i], sibling)

    def pre_copy(k):
        return remote(sendw.at[k], pre.at[k], ss.at[5 + k], rs.at[5 + k], other_ctx)

    def load_copy(j):
        src, dst = [(h_tok.at[ctx], xb.at[rows_of(ctx)]), (h_cot.at[ctx], cotb.at[rows_of(ctx)]), (h_wo, wo)][j]
        return pltpu.make_async_copy(src, dst, lsem.at[j])

    outs = [(xb, o_x), (nrm, o_nrm), (qkvb, o_qkv), (sent, o_sent), (ffn, o_ffn), (qkvb.at[0], o_gp), (qkvb.at[1], o_gs),
            (hid, o_gh), (qkvb.at[2], o_out), (keepw, o_keep), (sendw.at[pl.ds(PRE, 1)], o_last), (gfb, o_gf)]

    def out_copy(j):
        return pltpu.make_async_copy(outs[j][0], outs[j][1], osem.at[j])

    @pl.when(tick == 0)
    def _():
        barrier = pltpu.get_barrier_semaphore()
        for p in (other_ctx, sibling):
            pl.semaphore_signal(barrier, inc=1, device_id=p, device_id_type=MESH)
        load_copy(0).start()
        w_start(0)
        w_start(1)
        load_copy(1).start()
        load_copy(2).start()
        pl.semaphore_wait(barrier, 2)
        tok_copy().start()
        cot_copy().start()
        small[...] = jnp.zeros_like(small)
        at = lax.broadcasted_iota(jnp.int32, (1, t), 1)
        start = jnp.zeros((1, t), jnp.int32)
        bound = jnp.int32(0)
        for i in range(lengths.shape[1]):
            bound = bound + lengths[ctx, i]
            start = jnp.where(at >= bound, bound, start)
        fill_bias(start, bias, t)
        load_copy(0).wait()

    @pl.when(tick == F_Q2)
    def _():
        tok_copy().wait_recv()
        out_copy(0).start()

    for own in (True, False):
        first = F_Q1 if own else F_Q2
        here = rows_of(ctx if own else 1 - ctx)

        @pl.when(tick == first)
        def _(here=here):
            n, _ = ln_stats(xb[here, :].astype(F32))
            nrm[here, :] = (n * gain[0:1, :] + offset[0:1, :]).astype(BF)

        @pl.when((tick >= first) & (tick < first + 3))
        def _(here=here, first=first):
            w = w_next(tick)
            qkvb[tick - first, here, :] = dot(nrm[here, :], w[...], 1, 0).astype(BF)

    @pl.when(tick == F_AT)
    def _():
        out_copy(1).start()
        out_copy(2).start()
        cot_copy().wait_recv()
        load_copy(1).wait()
        cot_core().start()

    @pl.when((tick >= F_AT) & (tick < F_FC))
    def _():
        pair = tick - F_AT
        hd = 64
        at = pl.ds(pl.multiple_of(pair * 128, 128), 128)
        vt = qkvb[2, :, at].astype(F32).T.astype(BF)
        sc = head_lanes(scale, pair, (1, 128), hd)
        for i in range(t // QB):
            k0, k1 = key_range(i)
            qs = slice(i * QB, (i + 1) * QB)
            qm = (both_heads(qkvb[0, qs, at], hd) * (hd**-0.5)).astype(BF)
            st = dot(qkvb[1, k0:k1, at], qm, 1, 1) + bias[i, 0 : k1 - k0, :]
            top = jnp.max(st, axis=0, keepdims=True)
            pt = jnp.exp(st - top)
            total = jnp.sum(pt, axis=0, keepdims=True)
            ot = dot(vt[:, k0:k1], pt.astype(BF), 1, 0) * (1.0 / total)
            o = jnp.concatenate([ot[0:hd, 0:QB], ot[hd:, QB:]], axis=0).T
            sent[qs, at] = (o * sc).astype(BF)
            ls = top + jnp.log(total)
            lse[pair, 0:1, qs] = ls[:, 0:QB]
            lse[pair, 1:2, qs] = ls[:, QB:]

    @pl.when(tick == F_FC)
    def _():
        out_copy(3).start()
        load_copy(2).wait()
        n, inv = ln_stats(dot(sent[...], wo[...], 1, 0))
        n1[...] = n
        s1[...] = inv
        hidden = xb[...].astype(F32) + n * gain[1:2, :] + offset[1:2, :]
        hid[...] = hidden
        n, inv = ln_stats(hidden)
        n2[...] = n
        s2[...] = inv
        ffn[...] = (n * gain[2:3, :] + offset[2:3, :]).astype(BF)
        ta[...] = jnp.zeros_like(ta)
        out_copy(4).start()

    @pl.when((tick >= F_FC) & (tick < F_NM))
    def _():
        i = tick - F_FC
        w = w_next(6 + i)
        f = dot(ffn[...], w[...], 1, 0)
        phi = 0.5 + 0.5 * lax.erf(f * (0.5**0.5))
        a = f * phi
        gfb[i] = (phi + f * (jnp.exp(-0.5 * f * f) * 0.3989422804014327)).astype(BF)
        act[i] = a
        ta[...] += jnp.sum(a, axis=-1, keepdims=True)

    @pl.when(tick == F_NM)
    def _():
        mean = ta[...] * (1.0 / width)
        sq = jnp.zeros_like(mean)
        for j in range(blocks):
            c = act[j] - mean
            act[j] = c
            sq += jnp.sum(c * c, axis=-1, keepdims=True)
        smid[...] = lax.rsqrt(sq * (1.0 / width) + EPS)
        ta[...] = jnp.zeros_like(ta)
        tb[...] = jnp.zeros_like(tb)

    @pl.when((tick >= F_NM) & (tick < F_B1))
    def _():
        i = tick - F_NM
        n = act[i] * smid[...]
        nmid[i] = n.astype(BF)
        vec = pl.ds(pl.multiple_of(i * d, d), d)
        mid[i] = (n * mg[:, vec] + mb[:, vec]).astype(BF)
        pl.when(lax.rem(i, 2) == 1 - core)(lambda: mid_core(i // 2).start())

    @pl.when(tick == F_B1)
    def _():
        out_copy(1).wait()
        out_copy(2).wait()

    @pl.when((tick >= F_B1) & (tick < F_A))
    def _():
        i = tick - F_B1
        w = w_next(10 + i)
        e = dot(cotb[...], w[...], 1, 1)
        n = nmid[i].astype(F32)
        vec = pl.ds(pl.multiple_of(i * d, d), d)
        small[pl.ds(6 + i, 1), :] = colsum(e * n)
        small[pl.ds(6 + blocks + i, 1), :] = colsum(e)
        a = e * mg[:, vec]
        act[i] = a
        ta[...] += jnp.sum(a, axis=-1, keepdims=True)
        tb[...] += jnp.sum(a * n, axis=-1, keepdims=True)

    @pl.when(tick == F_A)
    def _():
        cot_core().wait_recv()
        mid_core(0).wait_recv()
        mid_core(1).wait_recv()

    @pl.when((tick >= F_A) & (tick < F_O))
    def _():
        k = tick - F_A
        a_at = pl.ds(pl.multiple_of((k // 2) * h, h), h)
        b_at = pl.ds(pl.multiple_of(lax.rem(k, 2) * h, h), h)
        for far in (True, False):
            x = 1 - ctx if far else ctx
            v = dot(mid[2 * x + core, :, a_at], cotb[:, b_at], 0, 0) + dot(r_mid[x, :, a_at], r_cot[:, b_at], 0, 0)
            put_chunk(sendw if far else keepw, k, v.astype(BF))
            if far:
                pl.when(k < PRE)(lambda: pre_copy(k).start())

    @pl.when(tick == F_O)
    def _():
        out_copy(9).start()
        out_copy(10).start()

    @pl.when((tick >= F_O) & (tick < F_B2))
    def _():
        i = tick - F_O
        w = w_next(14 + i)
        hid[...] += dot(mid[i], w[...], 1, 0)

    @pl.when(tick == F_B2 - 1)
    def _():
        qkvb[2] = hid[...].astype(BF)
        out_copy(8).start()

    @pl.when((tick >= F_B2) & (tick < F_END))
    def _():
        i = tick - F_B2
        w = w_next(18 + i)
        n = nmid[i].astype(F32)
        a = act[i] - ta[...] * (1.0 / width) - n * (tb[...] * (1.0 / width))
        gf = (a * smid[...] * gfb[i].astype(F32)).astype(BF)
        gfb[i] = gf
        v = dot(gf, w[...], 1, 1)

        @pl.when(i == 0)
        def _():
            acc[...] = v

        @pl.when(i > 0)
        def _():
            acc[...] += v

    @pl.when(tick == F_END - 1)
    def _():
        out_copy(11).start()
        e = acc[...]
        n = n2[...]
        small[2:3, :] = colsum(e * n)
        small[5:6, :] = colsum(e)
        gh = cotb[...].astype(F32) + ln_back(e, gain[2:3, :], n, s2[...])
        hid[...] = gh
        out_copy(7).start()
        n = n1[...]
        small[1:2, :] = colsum(gh * n)
        small[4:5, :] = colsum(gh)
        gp = ln_back(gh, gain[1:2, :], n, s1[...]).astype(BF)
        qkvb[0] = gp
        out_copy(5).start()
        qkvb[1] = dot(gp, wo[...], 1, 1).astype(BF)
        out_copy(6).start()
        for j in (0, 3, 4, 5, 6, 7, 8, 9, 10, 11):
            out_copy(j).wait()
        tok_copy().wait_send()
        cot_copy().wait_send()
        cot_core().wait_send()
        mid_core(0).wait_send()
        mid_core(1).wait_send()
        for k in range(PRE):
            pre_copy(k).wait()


def front_call(rows, cols, lengths, scale, gain, offset, mg, mb, tok, cot, wqkv, wo, w1, w2):
    seg, d = tok.shape[1:]
    t = 2 * seg
    ff = w1.shape[1]
    blocks = ff // d
    pairs = d // 128
    any_ = pl.BlockSpec(memory_space=pl.ANY)
    smem = pl.BlockSpec(memory_space=pltpu.SMEM)
    whole = lambda shape: pl.BlockSpec(shape, lambda i: (0,) * len(shape))
    vm = lambda *shape: pltpu.VMEM(shape, BF)
    vf = lambda *shape: pltpu.VMEM(shape, F32)
    dma = lambda n: pltpu.SemaphoreType.DMA((n,))
    small = (6 + 2 * blocks + 2, d)
    td = struct((t, d), BF)
    return pl.pallas_call(
        front_kernel,
        grid=(F_END,),
        in_specs=[smem, smem, whole((3, d)), whole((3, d)), whole((1, ff)), whole((1, ff))] + [any_] * 6,
        out_specs=[any_] * 4 + [whole((pairs, 2, t))] + [any_] * 9 + [whole(small)],
        out_shape=[
            td, td, struct((3, t, d), BF), td, struct((pairs, 2, t), F32), td, struct((blocks, t, d), BF), td, td,
            struct((t, d), F32), td, struct((4, rows, cols), BF), struct((1, rows, cols), BF),
            struct((PRE, rows, cols), BF), struct(small, F32),
        ],
        scratch_shapes=[
            vm(3, d, d), vm(d, d), vm(t, d), vm(t, d), vm(t, d), vm(3, t, d), vm(t, d), vf(t // QB, QB + REACH, 2 * QB),
            vf(blocks, t, d), vm(blocks, t, d), vm(blocks, t, d), vm(blocks, t, d), vm(2, t, d), vm(t, d),
            vf(t, d), vf(t, d), vf(t, d), vf(t, d), vm(t, d), vm(4, rows, cols), vm(4, rows, cols),
            vf(t, 1), vf(t, 1), vf(t, 1), vf(t, 1), vf(t, 1), dma(3), dma(3), dma(12), dma(8), dma(8),
        ],
        compiler_params=pltpu.CompilerParams(collective_id=1, has_side_effects=True, vmem_limit_bytes=60 * 2**20),
    )(lengths, scale, gain, offset, mg, mb, tok, cot, wqkv, wo, w1, w2)


def factors_of(n):
    out, want, rest = [2], 2, n // 2
    while rest > 1:
        f = min(want, rest)
        out.append(f)
        rest //= f
        want *= 2
    return out


T_ATT, T_WO, T_W1, T_WQ, T_IN, T_TAIL = 0, 8, 9, 13, 16, 22


DEPTH = 2
EVENT_TICKS = (0, 1, 2, 3, 8, 10, 12, 14, 16, 18, 20)


def event_at(i):
    done = jnp.maximum(i - T_TAIL, 0)
    for at in EVENT_TICKS:
        done = done + jnp.where(i > at, 1, 0)
    return done


def tick_count(n_events):
    return T_TAIL + n_events - len(EVENT_TICKS)


def main_kernel(factors, lengths, scale, q, k, v, gs, sn, lse, wq, gain,
                h_sent, h_ffn, h_gf, h_gp, h_nrm, h_last, h_keep, h_pre, h_x, h_ghid, h_small, h_out,
                out, gx_own, gx_got, small_out, out_got, *scr):
    tick = pl.program_id(0)
    n_rs = len(factors)
    chunks, rows, cols = out.shape[0], out.shape[2], out.shape[3]
    t, d = h_sent.shape
    hd2 = d // 2
    me = lax.axis_index("rows")
    ctx = lax.axis_index("ctx")
    fs = [2] + factors[1:]
    strides, st = [0], 2
    for f in factors[1:]:
        strides.append(st)
        st *= f
    size = [rows]
    for f in fs[1:]:
        size.append(size[-1] // f)
    pos = [ctx] + [lax.rem(me // strides[i], fs[i]) for i in range(1, n_rs)]
    off = [0]
    for i in range(1, n_rs):
        off.append(off[-1] + pos[i] * size[i])
    bits = []
    b = 1
    while b < lax.axis_size("rows"):
        bits.append(b)
        b *= 2

    def peer(i, j):
        if i == 0:
            return (me, 1 - ctx)
        return (me + ((pos[i] ^ j) - pos[i]) * strides[i], ctx)

    core = lax.rem(me, 2)
    sibling = (me + 1 - 2 * core, ctx)
    other_ctx = (me, 1 - ctx)

    def bit_peer(b):
        return (me + b - 2 * b * lax.rem(me // b, 2), ctx)

    scr = list(scr)
    take = lambda n: [scr.pop(0) for _ in range(n)]
    sendb, acc, gath = take(3)
    recv = [gath] + take(n_rs - 1)
    small_acc, small_recv = take(2)
    o_sent, o_ffn, o_gf, o_gp, o_nrm = take(5)
    r_sent, r_ffn, r_gf, r_gp, r_nrm, r_gq = take(6)
    gall, bias, gk, gv, gqt, xb, gh, gn_acc, gx_send = take(9)
    rs_s, rs_r = take(n_rs), take(n_rs)
    ag_s, ag_r = [None] + take(n_rs - 1), [None] + take(n_rs - 1)
    core_s, core_r, loc, small_s, small_r, swap_s, swap_r, load, gx_s, gx_r = take(10)

    def part(at, n):
        return pl.ds(at if isinstance(at, int) else pl.multiple_of(at, 16), n)

    def rs_copy(i, c, j):
        if i == 0:
            src, dst = sendb.at[c - PRE], gath.at[c]
        else:
            src = acc.at[c, part(off[i - 1] + (pos[i] ^ j) * size[i], size[i])]
            dst = recv[i].at[c, j - 1]
        return remote(src, dst, rs_s[i].at[c, j - 1], rs_r[i].at[c, j - 1], peer(i, j))

    def ag_copy(i, c, j, arriving):
        at = off[i - 1] + (pos[i] ^ j) * size[i] if arriving else off[i]
        ref = gath.at[c, part(at, size[i])]
        return remote(ref, ref, ag_s[i].at[c, j - 1], ag_r[i].at[c, j - 1], peer(i, j))

    def core_copy(c, arriving):
        to = 1 - core if arriving else core
        return remote(gath.at[c], out.at[c, to], core_s.at[c], core_r.at[c], sibling)

    def own_copy(c):
        return pltpu.make_async_copy(gath.at[c], out.at[c, core], loc.at[c])

    def reduce_stage(i, c):
        if i == 0:
            @pl.when(c >= PRE)
            def _():
                rs_copy(0, c, 1).wait_recv()
        else:
            for j in range(1, fs[i]):
                rs_copy(i, c, j).wait_recv()
        here = part(off[i], size[i])
        val = acc[c, here].astype(F32)
        if i == 0:
            val = val + gath[c].astype(F32)
        else:
            for j in range(1, fs[i]):
                val = val + recv[i][c, j - 1].astype(F32)
        if i + 1 < n_rs:
            acc[c, here] = val.astype(BF)
            for j in range(1, fs[i + 1]):
                rs_copy(i + 1, c, j).start()
        else:
            gath[c, here] = val.astype(BF)
            for j in range(1, fs[i]):
                ag_copy(i, c, j, False).start()

    def gather_stage(i, c):
        for j in range(1, fs[i]):
            ag_copy(i, c, j, True).wait_recv()
        if i > 1:
            for j in range(1, fs[i - 1]):
                ag_copy(i - 1, c, j, False).start()
        else:
            core_copy(c, False).start()
            own_copy(c).start()

    def small_copy(i):
        to = other_ctx if i == 0 else bit_peer(bits[i - 1])
        return remote(small_acc.at[i], small_recv.at[i], small_s.at[i], small_r.at[i], to)

    mine = pl.ds(pl.multiple_of(core * hd2, hd2), hd2)
    theirs = pl.ds(pl.multiple_of((1 - core) * hd2, hd2), hd2)
    swaps = [(h_sent, r_sent), (h_gp.at[:, theirs], r_gp), (h_ffn, r_ffn), (h_gf.at[1 - core], r_gf.at[0]), (h_nrm, r_nrm),
             (h_gf.at[3 - core], r_gf.at[1])]
    loads = [(h_sent, o_sent), (h_gp.at[:, mine], o_gp), (h_ffn, o_ffn), (h_gf.at[core], o_gf.at[0]), (h_nrm, o_nrm),
             (h_x, xb), (h_ghid, gh), (h_small, small_acc.at[0]), (h_last.at[0], sendb.at[0]),
             (h_keep, acc.at[pl.ds(0, 4)]), (h_pre, gath.at[pl.ds(0, PRE)]), (h_gf.at[2 + core], o_gf.at[1])]

    def swap_copy(j):
        return remote(swaps[j][0], swaps[j][1], swap_s.at[j], swap_r.at[j], sibling)

    def gq_copy():
        return remote(gall.at[1 - core], r_gq, swap_s.at[6], swap_r.at[6], sibling)

    def load_copy(j):
        return pltpu.make_async_copy(loads[j][0], loads[j][1], load.at[j])

    seg = t // 2

    def rows_of(c):
        return pl.ds(pl.multiple_of(c * seg, seg), seg)

    def gx_copy():
        return remote(gx_send, gx_got, gx_s.at[0], gx_r.at[0], other_ctx)

    def out_copy():
        return remote(h_out.at[rows_of(1 - ctx)], out_got, gx_s.at[1], gx_r.at[1], other_ctx)

    @pl.when(tick == 0)
    def _():
        peers = [other_ctx, sibling]
        for i in range(1, n_rs):
            peers += [peer(i, j) for j in range(1, fs[i])]
        barrier = pltpu.get_barrier_semaphore()
        for p in peers:
            pl.semaphore_signal(barrier, inc=1, device_id=p, device_id_type=MESH)
        for j in (10, 9, 8, 0, 1, 2, 3, 11, 4, 5, 6, 7):
            load_copy(j).start()
        pl.semaphore_wait(barrier, len(peers))
        for j in (0, 1, 2, 3, 5, 4):
            swap_copy(j).start()
        for j in (10, 9, 8):
            load_copy(j).wait()
        rs_copy(0, PRE, 1).start()
        out_copy().start()
        at = lax.broadcasted_iota(jnp.int32, (1, t), 1)
        start = jnp.zeros((1, t), jnp.int32)
        bound = jnp.int32(0)
        for i in range(lengths.shape[1]):
            bound = bound + lengths[ctx, i]
            start = jnp.where(at >= bound, bound, start)
        fill_bias(start, bias, t)
        load_copy(7).wait()

    @pl.when(tick < T_WO)
    def _():
        hd = q.shape[2] // 2
        kt = k[0].astype(F32).T.astype(BF)
        gsf = gs[...].astype(F32)
        prod = (gsf * sn[...].astype(F32)).T
        d0 = jnp.sum(prod[0:hd], axis=0, keepdims=True)
        d1 = jnp.sum(prod[hd:], axis=0, keepdims=True)
        lane = lax.broadcasted_iota(jnp.int32, (1, d), 1)
        h0 = jnp.sum(d0, axis=-1, keepdims=True)
        h1 = jnp.sum(d1, axis=-1, keepdims=True)
        small_acc[0, 14:15, :] += jnp.where(lane == 2 * tick, h0, 0.0) + jnp.where(lane == 2 * tick + 1, h1, 0.0)
        ga = (gsf * head_lanes(scale, tick, (1, 2 * hd), hd)).astype(BF)
        gk[...] = jnp.zeros_like(gk)
        gv[...] = jnp.zeros_like(gv)
        for i in range(t // QB):
            k0, k1 = key_range(i)
            qs = slice(i * QB, (i + 1) * QB)
            qm = (both_heads(q[0, qs, :], hd) * (hd**-0.5)).astype(BF)
            gm = both_heads(ga[qs, :], hd)
            sc = dot(k[0, k0:k1, :], qm, 1, 1) + bias[i, 0 : k1 - k0, :]
            ls = jnp.concatenate([lse[0, 0:1, qs], lse[0, 1:2, qs]], axis=1)
            dd = jnp.concatenate([d0[:, qs], d1[:, qs]], axis=1)
            pt = jnp.exp(sc - ls)
            gp = dot(v[0, k0:k1, :], gm, 1, 1)
            ds = (pt * (gp - dd)).astype(BF)
            gv[k0:k1, :] += dot(pt.astype(BF), gm, 1, 0)
            gk[k0:k1, :] += dot(ds, qm, 1, 0)
            gq = dot(kt[:, k0:k1], ds, 1, 0) * (hd**-0.5)
            gqt[:, qs] = jnp.concatenate([gq[0:hd, 0:QB], gq[hd:, QB:]], axis=0)
        half = tick // (T_WO // 2)
        at = pl.ds(pl.multiple_of(lax.rem(tick, T_WO // 2) * 128, 128), 128)
        gall[half, 0, :, at] = gqt[...].T.astype(BF)
        gall[half, 1, :, at] = gk[...].astype(BF)
        gall[half, 2, :, at] = gv[...].astype(BF)

    @pl.when(tick == T_WO - 1)
    def _():
        gq_copy().start()

    def wgrad(c, a0, a1, b0, b1):
        for far in (True, False):
            x = 1 - ctx if far else ctx
            val = (dot(a0(x), b0, 0, 0) + dot(a1(x), b1, 0, 0)).astype(BF)
            put_chunk(sendb if far else acc, c - PRE if far else c, val)
            if far:
                rs_copy(0, c, 1).start()

    def half_of(ref):
        return lambda x: ref[:, pl.ds(pl.multiple_of(x * hd2, 128), hd2)]

    @pl.when(tick == T_WO)
    def _():
        for j in (0, 1):
            load_copy(j).wait()
            swap_copy(j).wait_recv()
        wgrad(4, half_of(o_sent), half_of(r_sent), o_gp[...], r_gp[...])

    @pl.when(tick == T_W1)
    def _():
        for j in (2, 3):
            load_copy(j).wait()
            swap_copy(j).wait_recv()
        load_copy(11).wait()
        swap_copy(5).wait_recv()

    @pl.when((tick >= T_W1) & (tick < T_WQ))
    def _():
        c = tick - T_W1
        b = lambda ref: ref[c // 2, :, pl.ds(pl.multiple_of(lax.rem(c, 2) * hd2, 128), hd2)]
        wgrad(c + 5, half_of(o_ffn), half_of(r_ffn), b(o_gf), b(r_gf))

    @pl.when(tick == T_WQ)
    def _():
        load_copy(4).wait()
        swap_copy(4).wait_recv()
        gq_copy().wait_recv()

    @pl.when((tick >= T_WQ) & (tick < T_IN))
    def _():
        c = tick - T_WQ
        wgrad(c + 9, half_of(o_nrm), half_of(r_nrm), gall[core, c], r_gq[c])

    @pl.when((tick >= T_IN) & (tick < T_TAIL))
    def _():
        j = tick - T_IN
        val = dot(gall[lax.rem(j, 2), j // 2], wq[...], 1, 1)

        @pl.when(j == 0)
        def _():
            gn_acc[...] = val

        @pl.when(j > 0)
        def _():
            gn_acc[...] += val

    @pl.when(tick == T_TAIL - 1)
    def _():
        load_copy(5).wait()
        load_copy(6).wait()
        e = gn_acc[...]
        n, inv = ln_stats(xb[...].astype(F32))
        small_acc[0, 0:1, :] = colsum(e * n)
        small_acc[0, 3:4, :] = colsum(e)
        gh[...] += ln_back(e, gain[0:1, :], n, inv)
        gx_send[...] = gh[rows_of(1 - ctx), :].astype(BF)
        gx_copy().start()
        gx_own[...] = gh[rows_of(ctx), :]
        small_copy(0).start()

    def guarded(f, i, c):
        pl.when((c >= 0) & (c < chunks))(lambda: f(i, c))

    event = event_at(tick)
    fire = event_at(tick + 1) > event
    lanes = [(reduce_stage, i) for i in range(n_rs)] + [(gather_stage, i) for i in range(n_rs - 1, 0, -1)]

    @pl.when(fire)
    def _():
        for lag in range(len(lanes) - 1, -1, -1):
            f, i = lanes[lag]
            guarded(f, i, event - DEPTH * lag)

    for i in range(len(bits) + 1):

        @pl.when(tick == T_TAIL + 1 + i)
        def _(i=i):
            small_copy(i).wait_recv()
            if i < len(bits):
                small_acc[i + 1] = small_acc[i] + small_recv[i]
                small_copy(i + 1).start()
            else:
                small_out[...] = small_acc[i] + small_recv[i]

    @pl.when(tick == pl.num_programs(0) - 1)
    def _():
        def finish(c, _):
            for i in range(n_rs):
                for j in range(1, fs[i]):
                    if i == 0:
                        @pl.when(c >= PRE)
                        def _():
                            rs_copy(0, c, 1).wait_send()
                    else:
                        rs_copy(i, c, j).wait_send()
                        ag_copy(i, c, j, False).wait_send()
            core_copy(c, False).wait_send()
            core_copy(c, True).wait_recv()
            own_copy(c).wait()
            return 0

        lax.fori_loop(0, chunks, finish, 0)
        for i in range(len(bits) + 1):
            small_copy(i).wait_send()
        for j in range(6):
            swap_copy(j).wait_send()
        gq_copy().wait_send()
        gx_copy().wait()
        out_copy().wait()


def main_call(factors, rows, cols, lengths, scale, qkv, gsent, sent, lse, w_qkv, gain, ffn_in, gf, gp, normed, last,
              keep, pre, x, ghid, small, out):
    t, d = sent.shape
    h = d // 2
    n = 1
    for f in factors:
        n *= f
    fs = [2] + factors[1:]
    levels = 1
    while n > 1:
        levels += 1
        n //= 2
    size, recv = rows, []
    for f in fs[1:]:
        size //= f
        recv.append(pltpu.VMEM((CHUNKS, f - 1, size, cols), BF))
    dma = lambda *shape: pltpu.SemaphoreType.DMA(shape)
    per = lambda k: [dma(CHUNKS, f - 1) for f in fs[k:]]
    vm = lambda *shape: pltpu.VMEM(shape, BF)
    vf = lambda *shape: pltpu.VMEM(shape, F32)
    pair = lambda i: jnp.minimum(i, T_WO - 1)
    part = lambda j: pl.BlockSpec((1, t, 128), lambda i: (j, 0, pair(i)))
    flat = pl.BlockSpec((t, 128), lambda i: (0, pair(i)))
    whole = lambda shape: pl.BlockSpec(shape, lambda i: (0,) * len(shape))
    wcol = lambda i: jnp.clip(i - T_IN, 0, 5)
    any_ = pl.BlockSpec(memory_space=pl.ANY)
    lanes = 2 * len(fs) - 1
    events = CHUNKS + DEPTH * (lanes - 1)
    return pl.pallas_call(
        functools.partial(main_kernel, factors),
        grid=(tick_count(events),),
        in_specs=[
            pl.BlockSpec(memory_space=pltpu.SMEM), pl.BlockSpec(memory_space=pltpu.SMEM),
            part(0), part(1), part(2), flat, flat,
            pl.BlockSpec((1, 2, t), lambda i: (pair(i), 0, 0)),
            pl.BlockSpec((d, h), lambda i: (0, wcol(i))),
            whole((3, d)),
        ] + [any_] * 12,
        out_specs=[any_, whole((t // 2, d)), any_, whole(small.shape), any_],
        out_shape=[
            struct((CHUNKS, 2, rows, cols), BF), struct((t // 2, d), F32), struct((t // 2, d), BF), struct(small.shape, F32),
            struct((t // 2, d), BF),
        ],
        scratch_shapes=[vm(CHUNKS - PRE, rows, cols), vm(CHUNKS, rows, cols), vm(CHUNKS, rows, cols)]
        + recv
        + [vf(levels, *small.shape)] * 2
        + [vm(t, d), vm(t, d), vm(2, t, d), vm(t, h), vm(t, d)]
        + [vm(t, d), vm(t, d), vm(2, t, d), vm(t, h), vm(t, d), vm(3, t, h)]
        + [vm(2, 3, t, h), vf(t // QB, QB + REACH, 2 * QB), vf(t, 128), vf(t, 128), vf(128, t), vm(t, d), vf(t, d), vf(t, d),
           vm(t // 2, d)]
        + per(0) + per(0) + per(1) + per(1)
        + [dma(CHUNKS), dma(CHUNKS), dma(CHUNKS), dma(levels), dma(levels), dma(7), dma(7), dma(12), dma(2), dma(2)],
        compiler_params=pltpu.CompilerParams(collective_id=0, has_side_effects=True, vmem_limit_bytes=60 * 2**20),
    )(lengths, scale, qkv, qkv, qkv, gsent, sent, lse, w_qkv, gain,
      sent, ffn_in, gf, gp, normed, last, keep, pre, x, ghid, small, out)


def finish_kernel(got, g2, g1, go, gq):
    k = pl.program_id(0) // 2
    h = g2.shape[0]
    c = got.shape[3]

    def put(out):
        for m in range(h // c):
            out[:, m * c : (m + 1) * c] = got[0, 0, m * h : (m + 1) * h, :].astype(F32)

    pl.when(k < 4)(lambda: put(g2))
    pl.when(k == 4)(lambda: put(go))
    pl.when((k > 4) & (k < 9))(lambda: put(g1))
    pl.when(k > 8)(lambda: put(gq))


def finish_call(got, ff, d):
    h = d // 2
    rows, cols = got.shape[2:]

    def spec(lo, hi, at):
        def index(i):
            i = jnp.clip(i, 2 * lo, 2 * hi + 1)
            return at(i // 2 - lo, i % 2)

        return pl.BlockSpec((h, h), index)

    return pl.pallas_call(
        finish_kernel,
        grid=(24,),
        in_specs=[pl.BlockSpec((1, 1, rows, cols), lambda i: (i // 2, i % 2, 0, 0))],
        out_specs=[
            spec(0, 3, lambda k, c: (c * 2 + k // 2, k % 2)),
            spec(5, 8, lambda k, c: (0, ((k // 2) * 2 + c) * 2 + k % 2)),
            spec(4, 4, lambda k, c: (0, c)),
            spec(9, 11, lambda k, c: (0, k * 2 + c)),
        ],
        out_shape=[struct((ff // 2, d), F32), struct((h, ff), F32), struct((h, d), F32), struct((h, 3 * d), F32)],
        compiler_params=pltpu.CompilerParams(vmem_limit_bytes=60 * 2**20),
    )(got)


def local(
    tokens, cotangent, w_qkv, w_out, w_fc1, w_fc2, norm_gain, norm_bias, mid_gain, mid_bias, head_scale, doc_lengths
):
    n = lax.axis_size("rows")
    factors = factors_of(n)
    d = tokens.shape[2]
    ff = w_fc1.shape[1]
    heads = head_scale.shape[0]
    ctx = lax.axis_index("ctx")
    mg, mb = mid_gain[None, :], mid_bias[None, :]
    pieces = 1
    for f in factors[1:]:
        pieces *= f
    half = d // 2
    rows = max(half, 16 * pieces)
    cols = half * half // rows
    x, normed, qkv, sent, lse, ffn_in, gf, gp, gsent, ghid, out, keep, last, pre, small = front_call(
        rows, cols, doc_lengths, head_scale, norm_gain, norm_bias, mg, mb, tokens, cotangent, w_qkv, w_out, w_fc1, w_fc2
    )
    got, gx_own, gx_got, small, out_got = main_call(
        factors, rows, cols, doc_lengths, head_scale, qkv, gsent, sent, lse, w_qkv, norm_gain, ffn_in, gf, gp, normed, last,
        keep, pre, x, ghid, small, out,
    )
    g2, g1, go, gq = finish_call(got, ff, d)
    gx_got = gx_got.astype(F32)
    gx = jnp.stack([jnp.where(ctx == 0, gx_own, gx_got), jnp.where(ctx == 0, gx_got, gx_own)])

    def take(v, axis):
        size = v.shape[axis] // 2
        return lax.dynamic_slice_in_dim(v, ctx * size, size, axis)

    nm = ff // d
    gn = take(small[0:3], 1)
    bn = take(small[3:6], 1)
    gmg = take(small[6 : 6 + nm].reshape(-1), 0)
    gmb = take(small[6 + nm : 6 + 2 * nm].reshape(-1), 0)
    ghs = take(small[6 + 2 * nm, 0:heads] / head_scale, 0)

    seg = out_got.shape[0]
    out_own = lax.dynamic_slice_in_dim(out, ctx * seg, seg, 0)
    out = jnp.stack([jnp.where(ctx == 0, out_own, out_got), jnp.where(ctx == 0, out_got, out_own)])
    return (out, gx, gq, go, g1, g2, gn, bn, gmg, gmb, ghs)


def solution(mesh):
    rows = P("rows", "ctx", None)
    in_specs = (rows, rows) + (P(),) * 9 + (P("rows", None),)
    ctx0 = P("ctx", None)
    out_specs = (rows, rows, ctx0, ctx0, ctx0, ctx0, P(None, "ctx"), P(None, "ctx"), P("ctx"), P("ctx"), P("ctx"))
    return jax.shard_map(local, mesh=mesh, in_specs=in_specs, out_specs=out_specs, check_vma=False)
```

```python
import functools

import jax
import jax.numpy as jnp
from jax import lax
from jax.experimental import pallas as pl
from jax.experimental.pallas import tpu as pltpu
from jax.sharding import PartitionSpec as P

EPS = 1e-05
MASKED = -1e30
BF = jnp.bfloat16
F32 = jnp.float32
REACH = 256
QB = 128


def dot(a, b, ca, cb):
    return lax.dot_general(a, b, (((ca,), (cb,)), ((), ())), preferred_element_type=F32)


def ln_stats(v):
    mean = jnp.mean(v, axis=-1, keepdims=True)
    cen = v - mean
    inv = lax.rsqrt(jnp.mean(cen * cen, axis=-1, keepdims=True) + EPS)
    return cen * inv, inv


def ln_back(e, gain, n, inv):
    a = e * gain
    return inv * (
        a - jnp.mean(a, axis=-1, keepdims=True) - n * jnp.mean(a * n, axis=-1, keepdims=True)
    )


def colsum(v):
    return jnp.sum(v, axis=0, keepdims=True)


def struct(shape, dtype):
    return jax.ShapeDtypeStruct(shape, dtype)


def key_range(i):
    return max(0, i * QB - REACH), (i + 1) * QB


def fill_bias(start, bias, t):
    for i in range(t // QB):
        k0, k1 = key_range(i)
        u = lax.broadcasted_iota(jnp.int32, (k1 - k0, QB), 0) + k0
        q = lax.broadcasted_iota(jnp.int32, (k1 - k0, QB), 1) + i * QB
        first = start[:, i * QB : (i + 1) * QB]
        ok = (u >= first) & (u <= q)
        one = jnp.where(ok, 0.0, MASKED).astype(F32)
        bias[i, 0 : k1 - k0, 0:QB] = one
        bias[i, 0 : k1 - k0, QB : 2 * QB] = one


def both_heads(v, hd):
    lane = lax.broadcasted_iota(jnp.int32, v.shape, 1)
    zero = jnp.zeros_like(v)
    return jnp.concatenate([jnp.where(lane < hd, v, zero), jnp.where(lane < hd, zero, v)], axis=0)


def put_chunk(ref, k, v):
    h, c = v.shape[0], ref.shape[2]
    groups = ref.shape[1] // h
    for j in range(SUB):
        for m in range(groups):
            at = (j * groups + m) * c
            ref[SUB * k + j, m * h : (m + 1) * h, :] = v[:, at : at + c]


BLOCKS = 12
SUB = 2
CHUNKS = BLOCKS * SUB
PRE = 3 * SUB
F_Q1, F_Q2, F_AT, F_FC, F_NM, F_A, F_B1, F_O, F_B2, F_END = 0, 3, 6, 14, 18, 22, 26, 30, 34, 38
MESH = pl.DeviceIdType.MESH


def remote(src, dst, ss, rs, to):
    return pltpu.make_async_remote_copy(src, dst, ss, rs, device_id=to, device_id_type=MESH)


def head_lanes(scale, pair, shape, hd):
    lane = lax.broadcasted_iota(jnp.int32, shape, 1)
    return jnp.where(lane < hd, scale[2 * pair], scale[2 * pair + 1])


def front_kernel(lengths, scale, gain, offset, mg, mb, h_tok, h_cot, h_wqkv, h_wo, h_w1, h_w2,
                 o_x, o_nrm, o_qkv, o_sent, lse, o_ffn, o_gf, o_gp, o_gs, o_gh, o_out, o_keep, o_last, pre, small,
                 wb, wo, xb, cotb, nrm, qkvb, sent, bias, act, mid, nmid, gfb, r_mid, r_cot, n1, n2, hid, acc, ffn,
                 sendw, keepw, s1, s2, smid, ta, tb, wsem, lsem, osem, ss, rs):
    tick = pl.program_id(0)
    me = lax.axis_index("rows")
    ctx = lax.axis_index("ctx")
    core = lax.rem(me, 2)
    sibling = (me + 1 - 2 * core, ctx)
    other_ctx = (me, 1 - ctx)
    t, d = xb.shape
    seg = t // 2
    blocks = act.shape[0]
    width = blocks * act.shape[2]
    h = d // 2

    def rows_of(c):
        return pl.ds(pl.multiple_of(c * seg, seg), seg)

    def w_copy(ref, i):
        return pltpu.make_async_copy(ref, wb.at[lax.rem(i, 3)], wsem.at[lax.rem(i, 3)])

    def col(ref, i):
        return ref.at[:, pl.ds(pl.multiple_of(i * d, d), d)]

    def row(ref, i):
        return ref.at[pl.ds(pl.multiple_of(i * d, d), d), :]

    def w_start(i):
        pl.when(i < 6)(lambda: w_copy(col(h_wqkv, lax.rem(i, 3)), i).start())
        pl.when((i >= 6) & (i < 10))(lambda: w_copy(col(h_w1, i - 6), i).start())
        pl.when((i >= 10) & (i < 18))(lambda: w_copy(row(h_w2, lax.rem(i - 10, 4)), i).start())
        pl.when((i >= 18) & (i < 22))(lambda: w_copy(col(h_w1, i - 18), i).start())

    def w_next(i):
        w_copy(row(h_w2, 0), i).wait()
        w_start(i + 2)
        return wb.at[lax.rem(i, 3)]

    def tok_copy():
        return remote(h_tok.at[1 - ctx], xb.at[rows_of(ctx)], ss.at[0], rs.at[0], other_ctx)

    def cot_copy():
        return remote(h_cot.at[1 - ctx], cotb.at[rows_of(ctx)], ss.at[1], rs.at[1], other_ctx)

    def cot_core():
        return remote(cotb, r_cot, ss.at[2], rs.at[2], sibling)

    def mid_core(i):
        return remote(mid.at[2 * i + 1 - core], r_mid.at[i], ss.at[3 + i], rs.at[3 + i], sibling)

    def pre_copy(k):
        return remote(sendw.at[k], pre.at[k], ss.at[5 + k], rs.at[5 + k], other_ctx)

    def load_copy(j):
        src, dst = [(h_tok.at[ctx], xb.at[rows_of(ctx)]), (h_cot.at[ctx], cotb.at[rows_of(ctx)]), (h_wo, wo)][j]
        return pltpu.make_async_copy(src, dst, lsem.at[j])

    outs = [(xb, o_x), (nrm, o_nrm), (qkvb, o_qkv), (sent, o_sent), (ffn, o_ffn), (qkvb.at[0], o_gp), (qkvb.at[1], o_gs),
            (hid, o_gh), (qkvb.at[2], o_out), (keepw, o_keep), (sendw.at[pl.ds(PRE, 4 * SUB - PRE)], o_last), (gfb, o_gf)]

    def out_copy(j):
        return pltpu.make_async_copy(outs[j][0], outs[j][1], osem.at[j])

    @pl.when(tick == 0)
    def _():
        barrier = pltpu.get_barrier_semaphore()
        for p in (other_ctx, sibling):
            pl.semaphore_signal(barrier, inc=1, device_id=p, device_id_type=MESH)
        load_copy(0).start()
        w_start(0)
        w_start(1)
        load_copy(1).start()
        load_copy(2).start()
        pl.semaphore_wait(barrier, 2)
        tok_copy().start()
        cot_copy().start()
        small[...] = jnp.zeros_like(small)
        at = lax.broadcasted_iota(jnp.int32, (1, t), 1)
        start = jnp.zeros((1, t), jnp.int32)
        bound = jnp.int32(0)
        for i in range(lengths.shape[1]):
            bound = bound + lengths[ctx, i]
            start = jnp.where(at >= bound, bound, start)
        fill_bias(start, bias, t)
        load_copy(0).wait()

    @pl.when(tick == F_Q2)
    def _():
        tok_copy().wait_recv()
        out_copy(0).start()

    for own in (True, False):
        first = F_Q1 if own else F_Q2
        here = rows_of(ctx if own else 1 - ctx)

        @pl.when(tick == first)
        def _(here=here):
            n, _ = ln_stats(xb[here, :].astype(F32))
            nrm[here, :] = (n * gain[0:1, :] + offset[0:1, :]).astype(BF)

        @pl.when((tick >= first) & (tick < first + 3))
        def _(here=here, first=first):
            w = w_next(tick)
            qkvb[tick - first, here, :] = dot(nrm[here, :], w[...], 1, 0).astype(BF)

    @pl.when(tick == F_AT)
    def _():
        out_copy(1).start()
        out_copy(2).start()
        cot_copy().wait_recv()
        load_copy(1).wait()
        cot_core().start()

    @pl.when((tick >= F_AT) & (tick < F_FC))
    def _():
        pair = tick - F_AT
        hd = 64
        at = pl.ds(pl.multiple_of(pair * 128, 128), 128)
        vt = qkvb[2, :, at].astype(F32).T.astype(BF)
        sc = head_lanes(scale, pair, (1, 128), hd)
        for i in range(t // QB):
            k0, k1 = key_range(i)
            qs = slice(i * QB, (i + 1) * QB)
            qm = (both_heads(qkvb[0, qs, at], hd) * (hd**-0.5)).astype(BF)
            st = dot(qkvb[1, k0:k1, at], qm, 1, 1) + bias[i, 0 : k1 - k0, :]
            top = jnp.max(st, axis=0, keepdims=True)
            pt = jnp.exp(st - top)
            total = jnp.sum(pt, axis=0, keepdims=True)
            ot = dot(vt[:, k0:k1], pt.astype(BF), 1, 0) * (1.0 / total)
            o = jnp.concatenate([ot[0:hd, 0:QB], ot[hd:, QB:]], axis=0).T
            sent[qs, at] = (o * sc).astype(BF)
            ls = top + jnp.log(total)
            lse[pair, 0:1, qs] = ls[:, 0:QB]
            lse[pair, 1:2, qs] = ls[:, QB:]

    @pl.when(tick == F_FC)
    def _():
        out_copy(3).start()
        load_copy(2).wait()
        n, inv = ln_stats(dot(sent[...], wo[...], 1, 0))
        n1[...] = n
        s1[...] = inv
        hidden = xb[...].astype(F32) + n * gain[1:2, :] + offset[1:2, :]
        hid[...] = hidden
        n, inv = ln_stats(hidden)
        n2[...] = n
        s2[...] = inv
        ffn[...] = (n * gain[2:3, :] + offset[2:3, :]).astype(BF)
        ta[...] = jnp.zeros_like(ta)
        out_copy(4).start()

    @pl.when((tick >= F_FC) & (tick < F_NM))
    def _():
        i = tick - F_FC
        w = w_next(6 + i)
        f = dot(ffn[...], w[...], 1, 0)
        phi = 0.5 + 0.5 * lax.erf(f * (0.5**0.5))
        a = f * phi
        gfb[i] = (phi + f * (jnp.exp(-0.5 * f * f) * 0.3989422804014327)).astype(BF)
        act[i] = a
        ta[...] += jnp.sum(a, axis=-1, keepdims=True)

    @pl.when(tick == F_NM)
    def _():
        mean = ta[...] * (1.0 / width)
        sq = jnp.zeros_like(mean)
        for j in range(blocks):
            c = act[j] - mean
            act[j] = c
            sq += jnp.sum(c * c, axis=-1, keepdims=True)
        smid[...] = lax.rsqrt(sq * (1.0 / width) + EPS)
        ta[...] = jnp.zeros_like(ta)
        tb[...] = jnp.zeros_like(tb)

    @pl.when((tick >= F_NM) & (tick < F_B1))
    def _():
        j = tick - F_NM
        i = lax.rem(j, 2) * 2 + jnp.where(j < 2, 1 - core, core)
        n = act[i] * smid[...]
        nmid[i] = n.astype(BF)
        vec = pl.ds(pl.multiple_of(i * d, d), d)
        mid[i] = (n * mg[:, vec] + mb[:, vec]).astype(BF)
        pl.when(j < 2)(lambda: mid_core(j).start())

    @pl.when(tick == F_A)
    def _():
        out_copy(1).wait()
        out_copy(2).wait()

    @pl.when((tick >= F_B1) & (tick < F_O))
    def _():
        i = tick - F_B1
        w = w_next(10 + i)
        e = dot(cotb[...], w[...], 1, 1)
        n = nmid[i].astype(F32)
        vec = pl.ds(pl.multiple_of(i * d, d), d)
        small[pl.ds(6 + i, 1), :] = colsum(e * n)
        small[pl.ds(6 + blocks + i, 1), :] = colsum(e)
        a = e * mg[:, vec]
        act[i] = a
        ta[...] += jnp.sum(a, axis=-1, keepdims=True)
        tb[...] += jnp.sum(a * n, axis=-1, keepdims=True)

    @pl.when(tick == F_A)
    def _():
        cot_core().wait_recv()
        mid_core(0).wait_recv()
        mid_core(1).wait_recv()

    @pl.when((tick >= F_A) & (tick < F_B1))
    def _():
        k = tick - F_A
        a_at = pl.ds(pl.multiple_of((k // 2) * h, h), h)
        b_at = pl.ds(pl.multiple_of(lax.rem(k, 2) * h, h), h)
        for far in (True, False):
            x = 1 - ctx if far else ctx
            v = dot(mid[2 * x + core, :, a_at], cotb[:, b_at], 0, 0) + dot(r_mid[x, :, a_at], r_cot[:, b_at], 0, 0)
            put_chunk(sendw if far else keepw, k, v.astype(BF))
            if far:
                for j in range(SUB):
                    c = SUB * k + j
                    pl.when(c < PRE)(lambda c=c: pre_copy(c).start())

    @pl.when(tick == F_O)
    def _():
        out_copy(9).start()
        out_copy(10).start()

    @pl.when((tick >= F_O) & (tick < F_B2))
    def _():
        i = tick - F_O
        w = w_next(14 + i)
        hid[...] += dot(mid[i], w[...], 1, 0)

    @pl.when(tick == F_B2 - 1)
    def _():
        qkvb[2] = hid[...].astype(BF)
        out_copy(8).start()

    @pl.when((tick >= F_B2) & (tick < F_END))
    def _():
        i = tick - F_B2
        w = w_next(18 + i)
        n = nmid[i].astype(F32)
        a = act[i] - ta[...] * (1.0 / width) - n * (tb[...] * (1.0 / width))
        gf = (a * smid[...] * gfb[i].astype(F32)).astype(BF)
        gfb[i] = gf
        v = dot(gf, w[...], 1, 1)

        @pl.when(i == 0)
        def _():
            acc[...] = v

        @pl.when(i > 0)
        def _():
            acc[...] += v

    @pl.when(tick == F_END - 1)
    def _():
        out_copy(11).start()
        e = acc[...]
        n = n2[...]
        small[2:3, :] = colsum(e * n)
        small[5:6, :] = colsum(e)
        gh = cotb[...].astype(F32) + ln_back(e, gain[2:3, :], n, s2[...])
        hid[...] = gh
        out_copy(7).start()
        n = n1[...]
        small[1:2, :] = colsum(gh * n)
        small[4:5, :] = colsum(gh)
        gp = ln_back(gh, gain[1:2, :], n, s1[...]).astype(BF)
        qkvb[0] = gp
        out_copy(5).start()
        qkvb[1] = dot(gp, wo[...], 1, 1).astype(BF)
        out_copy(6).start()
        for j in (0, 3, 4, 5, 6, 7, 8, 9, 10, 11):
            out_copy(j).wait()
        tok_copy().wait_send()
        cot_copy().wait_send()
        cot_core().wait_send()
        mid_core(0).wait_send()
        mid_core(1).wait_send()
        for k in range(PRE):
            pre_copy(k).wait()


def front_call(rows, cols, lengths, scale, gain, offset, mg, mb, tok, cot, wqkv, wo, w1, w2):
    seg, d = tok.shape[1:]
    t = 2 * seg
    ff = w1.shape[1]
    blocks = ff // d
    pairs = d // 128
    any_ = pl.BlockSpec(memory_space=pl.ANY)
    smem = pl.BlockSpec(memory_space=pltpu.SMEM)
    whole = lambda shape: pl.BlockSpec(shape, lambda i: (0,) * len(shape))
    vm = lambda *shape: pltpu.VMEM(shape, BF)
    vf = lambda *shape: pltpu.VMEM(shape, F32)
    dma = lambda n: pltpu.SemaphoreType.DMA((n,))
    small = (6 + 2 * blocks + 2, d)
    td = struct((t, d), BF)
    return pl.pallas_call(
        front_kernel,
        grid=(F_END,),
        in_specs=[smem, smem, whole((3, d)), whole((3, d)), whole((1, ff)), whole((1, ff))] + [any_] * 6,
        out_specs=[any_] * 4 + [whole((pairs, 2, t))] + [any_] * 9 + [whole(small)],
        out_shape=[
            td, td, struct((3, t, d), BF), td, struct((pairs, 2, t), F32), td, struct((blocks, t, d), BF), td, td,
            struct((t, d), F32), td, struct((4 * SUB, rows, cols), BF), struct((4 * SUB - PRE, rows, cols), BF),
            struct((PRE, rows, cols), BF), struct(small, F32),
        ],
        scratch_shapes=[
            vm(3, d, d), vm(d, d), vm(t, d), vm(t, d), vm(t, d), vm(3, t, d), vm(t, d), vf(t // QB, QB + REACH, 2 * QB),
            vf(blocks, t, d), vm(blocks, t, d), vm(blocks, t, d), vm(blocks, t, d), vm(2, t, d), vm(t, d),
            vf(t, d), vf(t, d), vf(t, d), vf(t, d), vm(t, d), vm(4 * SUB, rows, cols), vm(4 * SUB, rows, cols),
            vf(t, 1), vf(t, 1), vf(t, 1), vf(t, 1), vf(t, 1), dma(3), dma(3), dma(12), dma(5 + PRE), dma(5 + PRE),
        ],
        compiler_params=pltpu.CompilerParams(collective_id=1, has_side_effects=True, vmem_limit_bytes=60 * 2**20),
    )(lengths, scale, gain, offset, mg, mb, tok, cot, wqkv, wo, w1, w2)


def factors_of(n):
    out = []
    while n > 1:
        out.append(2)
        n //= 2
    return out


T_ATT, T_WO, T_W1, T_WQ, T_IN, T_TAIL = 0, 8, 9, 13, 16, 22


def lags_of(n_rs):
    return (0,) + tuple(range(2, 2 * n_rs - 1)) + (2 * n_rs,)


T_OUT = 4


EVENT_TICKS = tuple(range(T_TAIL))
AHEAD = 16


def count_before(ticks, i):
    done = 0
    for at in sorted(set(ticks)):
        done = done + jnp.where(i > at, ticks.count(at), 0)
    return done


def event_ticks(n_events):
    more = n_events - len(EVENT_TICKS)
    return EVENT_TICKS + tuple(range(T_TAIL, T_TAIL + more))


def send_ticks(n_events):
    made = [0] * (4 * SUB - PRE)
    for at in tuple(range(T_WO, T_WO + 1)) + tuple(range(T_W1, T_WQ)) + tuple(range(T_WQ, T_IN)):
        made += [at] * SUB
    events = event_ticks(n_events)
    return tuple(max(at, events[max(PRE + j - AHEAD, 0)]) for j, at in enumerate(made))


def tick_count(n_events):
    return T_TAIL + max(n_events - len(EVENT_TICKS), 10)


def main_kernel(factors, lengths, scale, q, k, v, gs, sn, lse, wq, gain,
                h_sent, h_ffn, h_gf, h_gp, h_nrm, h_last, h_keep, h_pre, h_x, h_ghid, h_small, h_out,
                out, gx_own, gx_got, small_out, out_got, *scr):
    tick = pl.program_id(0)
    n_rs = len(factors)
    chunks, rows, cols = out.shape[0], out.shape[2], out.shape[3]
    t, d = h_sent.shape
    hd2 = d // 2
    me = lax.axis_index("rows")
    ctx = lax.axis_index("ctx")
    fs = [2] + factors[1:]
    strides, st = [0], 2
    for f in factors[1:]:
        strides.append(st)
        st *= f
    size = [rows]
    for f in fs[1:]:
        size.append(size[-1] // f)
    pos = [ctx] + [lax.rem(me // strides[i], fs[i]) for i in range(1, n_rs)]
    off = [0]
    for i in range(1, n_rs):
        off.append(off[-1] + pos[i] * size[i])
    bits = []
    b = 1
    while b < lax.axis_size("rows"):
        bits.append(b)
        b *= 2

    def peer(i, j):
        if i == 0:
            return (me, 1 - ctx)
        return (me + ((pos[i] ^ j) - pos[i]) * strides[i], ctx)

    core = lax.rem(me, 2)
    sibling = (me + 1 - 2 * core, ctx)
    other_ctx = (me, 1 - ctx)

    def bit_peer(b):
        return (me + b - 2 * b * lax.rem(me // b, 2), ctx)

    scr = list(scr)
    take = lambda n: [scr.pop(0) for _ in range(n)]
    sendb, acc, gath = take(3)
    recv = [gath] + take(n_rs - 1)
    small_acc, small_recv = take(2)
    o_sent, o_ffn, o_gf, o_gp, o_nrm = take(5)
    r_sent, r_ffn, r_gf, r_gp, r_nrm, r_gq = take(6)
    gall, bias, gk, gv, gqt, xb, gh, gn_acc, gx_send = take(9)
    rs_s, rs_r = take(n_rs), take(n_rs)
    ag_s, ag_r = [None] + take(n_rs - 1), [None] + take(n_rs - 1)
    core_s, core_r, loc, small_s, small_r, swap_s, swap_r, load, gx_s, gx_r = take(10)

    def part(at, n):
        return pl.ds(at if isinstance(at, int) else pl.multiple_of(at, 16), n)

    def rs_copy(i, c, j):
        if i == 0:
            src, dst = sendb.at[c - PRE], gath.at[c]
        else:
            src = acc.at[c, part(off[i - 1] + (pos[i] ^ j) * size[i], size[i])]
            dst = recv[i].at[c, j - 1]
        return remote(src, dst, rs_s[i].at[c, j - 1], rs_r[i].at[c, j - 1], peer(i, j))

    def ag_copy(i, c, j, arriving):
        at = off[i - 1] + (pos[i] ^ j) * size[i] if arriving else off[i]
        ref = gath.at[c, part(at, size[i])]
        return remote(ref, ref, ag_s[i].at[c, j - 1], ag_r[i].at[c, j - 1], peer(i, j))

    def core_copy(c, arriving):
        to = 1 - core if arriving else core
        return remote(gath.at[c], out.at[c, to], core_s.at[c], core_r.at[c], sibling)

    def own_copy(c):
        return pltpu.make_async_copy(gath.at[c], out.at[c, core], loc.at[c])

    def reduce_stage(i, c):
        if i == 0:
            @pl.when(c >= PRE)
            def _():
                rs_copy(0, c, 1).wait_recv()
        else:
            for j in range(1, fs[i]):
                rs_copy(i, c, j).wait_recv()
        here = part(off[i], size[i])
        val = acc[c, here].astype(F32)
        if i == 0:
            val = val + gath[c].astype(F32)
        else:
            for j in range(1, fs[i]):
                val = val + recv[i][c, j - 1].astype(F32)
        if i + 1 < n_rs:
            acc[c, here] = val.astype(BF)
            for j in range(1, fs[i + 1]):
                rs_copy(i + 1, c, j).start()
        else:
            gath[c, here] = val.astype(BF)
            for j in range(1, fs[i]):
                ag_copy(i, c, j, False).start()

    def gather_stage(i, c):
        for j in range(1, fs[i]):
            ag_copy(i, c, j, True).wait_recv()
        if i > 1:
            for j in range(1, fs[i - 1]):
                ag_copy(i - 1, c, j, False).start()
        else:
            core_copy(c, False).start()
            own_copy(c).start()

    def small_copy(i):
        to = other_ctx if i == 0 else bit_peer(bits[i - 1])
        return remote(small_acc.at[i], small_recv.at[i], small_s.at[i], small_r.at[i], to)

    mine = pl.ds(pl.multiple_of(core * hd2, hd2), hd2)
    theirs = pl.ds(pl.multiple_of((1 - core) * hd2, hd2), hd2)
    swaps = [(h_sent, r_sent), (h_gp.at[:, theirs], r_gp), (h_ffn, r_ffn), (h_gf.at[1 - core], r_gf.at[0]), (h_nrm, r_nrm),
             (h_gf.at[3 - core], r_gf.at[1])]
    loads = [(h_sent, o_sent), (h_gp.at[:, mine], o_gp), (h_ffn, o_ffn), (h_gf.at[core], o_gf.at[0]), (h_nrm, o_nrm),
             (h_x, xb), (h_ghid, gh), (h_small, small_acc.at[0]), (h_last, sendb.at[pl.ds(0, 4 * SUB - PRE)]),
             (h_keep, acc.at[pl.ds(0, 4 * SUB)]), (h_pre, gath.at[pl.ds(0, PRE)]), (h_gf.at[2 + core], o_gf.at[1])]

    def swap_copy(j):
        return remote(swaps[j][0], swaps[j][1], swap_s.at[j], swap_r.at[j], sibling)

    def gq_copy():
        return remote(gall.at[1 - core], r_gq, swap_s.at[6], swap_r.at[6], sibling)

    def load_copy(j):
        return pltpu.make_async_copy(loads[j][0], loads[j][1], load.at[j])

    seg = t // 2

    def rows_of(c):
        return pl.ds(pl.multiple_of(c * seg, seg), seg)

    def gx_copy():
        return remote(gx_send, gx_got, gx_s.at[0], gx_r.at[0], other_ctx)

    def out_copy():
        return remote(h_out.at[rows_of(1 - ctx)], out_got, gx_s.at[1], gx_r.at[1], other_ctx)

    @pl.when(tick == 0)
    def _():
        peers = [other_ctx, sibling]
        for i in range(1, n_rs):
            peers += [peer(i, j) for j in range(1, fs[i])]
        barrier = pltpu.get_barrier_semaphore()
        for p in peers:
            pl.semaphore_signal(barrier, inc=1, device_id=p, device_id_type=MESH)
        for j in (10, 9, 8, 0, 1, 2, 3, 11, 4, 5, 6, 7):
            load_copy(j).start()
        pl.semaphore_wait(barrier, len(peers))
        for j in (0, 1, 2, 3, 5, 4):
            swap_copy(j).start()
        for j in (10, 9, 8):
            load_copy(j).wait()
        at = lax.broadcasted_iota(jnp.int32, (1, t), 1)
        start = jnp.zeros((1, t), jnp.int32)
        bound = jnp.int32(0)
        for i in range(lengths.shape[1]):
            bound = bound + lengths[ctx, i]
            start = jnp.where(at >= bound, bound, start)
        fill_bias(start, bias, t)
        load_copy(7).wait()

    @pl.when(tick < T_WO)
    def _():
        hd = q.shape[2] // 2
        kt = k[0].astype(F32).T.astype(BF)
        gsf = gs[...].astype(F32)
        prod = (gsf * sn[...].astype(F32)).T
        d0 = jnp.sum(prod[0:hd], axis=0, keepdims=True)
        d1 = jnp.sum(prod[hd:], axis=0, keepdims=True)
        lane = lax.broadcasted_iota(jnp.int32, (1, d), 1)
        h0 = jnp.sum(d0, axis=-1, keepdims=True)
        h1 = jnp.sum(d1, axis=-1, keepdims=True)
        small_acc[0, 14:15, :] += (
            jnp.where(lane == 2 * tick, h0 / scale[2 * tick], 0.0)
            + jnp.where(lane == 2 * tick + 1, h1 / scale[2 * tick + 1], 0.0)
        )
        ga = (gsf * head_lanes(scale, tick, (1, 2 * hd), hd)).astype(BF)
        gk[...] = jnp.zeros_like(gk)
        gv[...] = jnp.zeros_like(gv)
        for i in range(t // QB):
            k0, k1 = key_range(i)
            qs = slice(i * QB, (i + 1) * QB)
            qm = (both_heads(q[0, qs, :], hd) * (hd**-0.5)).astype(BF)
            gm = both_heads(ga[qs, :], hd)
            sc = dot(k[0, k0:k1, :], qm, 1, 1) + bias[i, 0 : k1 - k0, :]
            ls = jnp.concatenate([lse[0, 0:1, qs], lse[0, 1:2, qs]], axis=1)
            dd = jnp.concatenate([d0[:, qs], d1[:, qs]], axis=1)
            pt = jnp.exp(sc - ls)
            gp = dot(v[0, k0:k1, :], gm, 1, 1)
            ds = (pt * (gp - dd)).astype(BF)
            gv[k0:k1, :] += dot(pt.astype(BF), gm, 1, 0)
            gk[k0:k1, :] += dot(ds, qm, 1, 0)
            gq = dot(kt[:, k0:k1], ds, 1, 0) * (hd**-0.5)
            gqt[:, qs] = jnp.concatenate([gq[0:hd, 0:QB], gq[hd:, QB:]], axis=0)
        half = tick // (T_WO // 2)
        at = pl.ds(pl.multiple_of(lax.rem(tick, T_WO // 2) * 128, 128), 128)
        gall[half, 0, :, at] = gqt[...].T.astype(BF)
        gall[half, 1, :, at] = gk[...].astype(BF)
        gall[half, 2, :, at] = gv[...].astype(BF)

    @pl.when(tick == T_WO - 1)
    def _():
        gq_copy().start()

    def wgrad(c, a0, a1, b0, b1):
        for far in (True, False):
            x = 1 - ctx if far else ctx
            val = (dot(a0(x), b0, 0, 0) + dot(a1(x), b1, 0, 0)).astype(BF)
            put_chunk(sendb if far else acc, c - PRE // SUB if far else c, val)

    def half_of(ref):
        return lambda x: ref[:, pl.ds(pl.multiple_of(x * hd2, 128), hd2)]

    @pl.when(tick == T_OUT)
    def _():
        out_copy().start()

    @pl.when(tick == T_WO)
    def _():
        for j in (0, 1):
            load_copy(j).wait()
            swap_copy(j).wait_recv()
        wgrad(4, half_of(o_sent), half_of(r_sent), o_gp[...], r_gp[...])

    @pl.when(tick == T_W1)
    def _():
        for j in (2, 3):
            load_copy(j).wait()
            swap_copy(j).wait_recv()
        load_copy(11).wait()
        swap_copy(5).wait_recv()

    @pl.when((tick >= T_W1) & (tick < T_WQ))
    def _():
        c = tick - T_W1
        b = lambda ref: ref[c // 2, :, pl.ds(pl.multiple_of(lax.rem(c, 2) * hd2, 128), hd2)]
        wgrad(c + 5, half_of(o_ffn), half_of(r_ffn), b(o_gf), b(r_gf))

    @pl.when(tick == T_WQ)
    def _():
        load_copy(4).wait()
        swap_copy(4).wait_recv()
        gq_copy().wait_recv()

    @pl.when((tick >= T_WQ) & (tick < T_IN))
    def _():
        c = tick - T_WQ
        wgrad(c + 9, half_of(o_nrm), half_of(r_nrm), gall[core, c], r_gq[c])

    @pl.when((tick >= T_IN) & (tick < T_TAIL))
    def _():
        j = tick - T_IN
        val = dot(gall[lax.rem(j, 2), j // 2], wq[...], 1, 1)

        @pl.when(j == 0)
        def _():
            gn_acc[...] = val

        @pl.when(j > 0)
        def _():
            gn_acc[...] += val

    @pl.when(tick == T_TAIL - 1)
    def _():
        load_copy(5).wait()
        load_copy(6).wait()
        e = gn_acc[...]
        n, inv = ln_stats(xb[...].astype(F32))
        small_acc[0, 0:1, :] = colsum(e * n)
        small_acc[0, 3:4, :] = colsum(e)
        gh[...] += ln_back(e, gain[0:1, :], n, inv)
        gx_send[...] = gh[rows_of(1 - ctx), :].astype(BF)
        gx_copy().start()
        gx_own[...] = gh[rows_of(ctx), :]
        small_copy(0).start()

    def guarded(f, i, c):
        pl.when((c >= 0) & (c < chunks))(lambda: f(i, c))

    lanes = [(reduce_stage, i) for i in range(n_rs)] + [(gather_stage, i) for i in range(n_rs - 1, 0, -1)]

    lags = lags_of(n_rs)
    n_events = chunks + lags[-1]
    sends = send_ticks(n_events)

    def send(c, _):
        rs_copy(0, c, 1).start()
        return 0

    lax.fori_loop(PRE + count_before(sends, tick), PRE + count_before(sends, tick + 1), send, 0)
    events = event_ticks(n_events)
    event = count_before(events, tick)

    @pl.when(count_before(events, tick + 1) > event)
    def _():
        for lag in range(len(lanes) - 1, -1, -1):
            f, i = lanes[lag]
            guarded(f, i, event - lags[lag])

    for i in range(len(bits) + 1):

        @pl.when(tick == T_TAIL + 1 + i)
        def _(i=i):
            small_copy(i).wait_recv()
            if i < len(bits):
                small_acc[i + 1] = small_acc[i] + small_recv[i]
                small_copy(i + 1).start()
            else:
                small_out[...] = small_acc[i] + small_recv[i]

    @pl.when(tick == pl.num_programs(0) - 1)
    def _():
        def finish(c, _):
            for i in range(n_rs):
                for j in range(1, fs[i]):
                    if i == 0:
                        @pl.when(c >= PRE)
                        def _():
                            rs_copy(0, c, 1).wait_send()
                    else:
                        rs_copy(i, c, j).wait_send()
                        ag_copy(i, c, j, False).wait_send()
            core_copy(c, False).wait_send()
            core_copy(c, True).wait_recv()
            own_copy(c).wait()
            return 0

        lax.fori_loop(0, chunks, finish, 0)
        for i in range(len(bits) + 1):
            small_copy(i).wait_send()
        for j in range(6):
            swap_copy(j).wait_send()
        gq_copy().wait_send()
        gx_copy().wait()
        out_copy().wait()


def main_call(factors, rows, cols, lengths, scale, qkv, gsent, sent, lse, w_qkv, gain, ffn_in, gf, gp, normed, last,
              keep, pre, x, ghid, small, out):
    t, d = sent.shape
    h = d // 2
    n = 1
    for f in factors:
        n *= f
    fs = [2] + factors[1:]
    levels = 1
    while n > 1:
        levels += 1
        n //= 2
    size, recv = rows, []
    for f in fs[1:]:
        size //= f
        recv.append(pltpu.VMEM((CHUNKS, f - 1, size, cols), BF))
    dma = lambda *shape: pltpu.SemaphoreType.DMA(shape)
    per = lambda k: [dma(CHUNKS, f - 1) for f in fs[k:]]
    vm = lambda *shape: pltpu.VMEM(shape, BF)
    vf = lambda *shape: pltpu.VMEM(shape, F32)
    pair = lambda i: jnp.minimum(i, T_WO - 1)
    part = lambda j: pl.BlockSpec((1, t, 128), lambda i: (j, 0, pair(i)))
    flat = pl.BlockSpec((t, 128), lambda i: (0, pair(i)))
    whole = lambda shape: pl.BlockSpec(shape, lambda i: (0,) * len(shape))
    wcol = lambda i: jnp.clip(i - T_IN, 0, 5)
    any_ = pl.BlockSpec(memory_space=pl.ANY)
    events = CHUNKS + lags_of(len(fs))[-1]
    return pl.pallas_call(
        functools.partial(main_kernel, factors),
        grid=(tick_count(events),),
        in_specs=[
            pl.BlockSpec(memory_space=pltpu.SMEM), pl.BlockSpec(memory_space=pltpu.SMEM),
            part(0), part(1), part(2), flat, flat,
            pl.BlockSpec((1, 2, t), lambda i: (pair(i), 0, 0)),
            pl.BlockSpec((d, h), lambda i: (0, wcol(i))),
            whole((3, d)),
        ] + [any_] * 12,
        out_specs=[any_, whole((t // 2, d)), any_, whole(small.shape), any_],
        out_shape=[
            struct((CHUNKS, 2, rows, cols), BF), struct((t // 2, d), F32), struct((t // 2, d), BF), struct(small.shape, F32),
            struct((t // 2, d), BF),
        ],
        scratch_shapes=[vm(CHUNKS - PRE, rows, cols), vm(CHUNKS, rows, cols), vm(CHUNKS, rows, cols)]
        + recv
        + [vf(levels, *small.shape)] * 2
        + [vm(t, d), vm(t, d), vm(2, t, d), vm(t, h), vm(t, d)]
        + [vm(t, d), vm(t, d), vm(2, t, d), vm(t, h), vm(t, d), vm(3, t, h)]
        + [vm(2, 3, t, h), vf(t // QB, QB + REACH, 2 * QB), vf(t, 128), vf(t, 128), vf(128, t), vm(t, d), vf(t, d), vf(t, d),
           vm(t // 2, d)]
        + per(0) + per(0) + per(1) + per(1)
        + [dma(CHUNKS), dma(CHUNKS), dma(CHUNKS), dma(levels), dma(levels), dma(7), dma(7), dma(12), dma(2), dma(2)],
        compiler_params=pltpu.CompilerParams(collective_id=0, has_side_effects=True, vmem_limit_bytes=60 * 2**20),
    )(lengths, scale, qkv, qkv, qkv, gsent, sent, lse, w_qkv, gain,
      sent, ffn_in, gf, gp, normed, last, keep, pre, x, ghid, small, out)


SLOTS = 8


def finish_kernel(small, got, gx_own, gx_got, own, away, out, gx, g2, g1, go, gq, gn, bn, gmg, gmb, ghs,
                  inb, outb, low, wide, isem, osem, sems):
    ctx = lax.axis_index("ctx")
    seg, d = gx_own.shape
    h = d // 2
    c = got.shape[3]
    blocks = (small.shape[0] - 8) // 2

    def copy(src, dst, j):
        return pltpu.make_async_copy(src, dst, sems.at[j])

    ins = [
        copy(gx_got, low.at[0], 0),
        copy(own.at[pl.ds(pl.multiple_of(ctx * seg, seg), seg)], low.at[1], 1),
        copy(away, low.at[2], 2),
        copy(gx_own, wide.at[1], 3),
    ]
    outs = [
        copy(wide.at[0], gx.at[1 - ctx], 4),
        copy(low.at[1], out.at[ctx], 5),
        copy(low.at[2], out.at[1 - ctx], 6),
        copy(wide.at[1], gx.at[ctx], 7),
    ]

    def place(i):
        k, core = i // 2, i % 2
        if k < 4:
            ref, r, col = g2, core * 2 + k // 2, k % 2
        elif k == 4:
            ref, r, col = go, 0, core
        elif k < 9:
            ref, r, col = g1, 0, (((k - 5) // 2) * 2 + core) * 2 + (k - 5) % 2
        else:
            ref, r, col = gq, 0, (k - 9) * 2 + core
        return ref.at[pl.ds(r * h, h), pl.ds(col * h, h)]

    def load(i):
        src = got.at[pl.ds(i // 2 * SUB, SUB), i % 2]
        return pltpu.make_async_copy(src, inb.at[i % SLOTS], isem.at[i % SLOTS])

    def store(i):
        return pltpu.make_async_copy(outb.at[i % SLOTS], place(i), osem.at[i % SLOTS])

    count = 2 * BLOCKS
    for i in range(SLOTS):
        load(i).start()
    for v in ins:
        v.start()
    half = pl.ds(pl.multiple_of(ctx * h, h), h)
    gn[...] = small[0:3, half]
    bn[...] = small[3:6, half]
    for j in range(blocks // 2):
        at = slice(j * d, (j + 1) * d)
        gmg[:, at] = small[pl.ds(6 + ctx * (blocks // 2) + j, 1), :]
        gmb[:, at] = small[pl.ds(6 + blocks + ctx * (blocks // 2) + j, 1), :]
    n = ghs.shape[1]
    row = small[6 + 2 * blocks : 7 + 2 * blocks, :]
    ghs[...] = jnp.where(ctx == 0, row[:, 0:n], row[:, n : 2 * n])
    for i in range(count):
        load(i).wait()
        if i >= SLOTS:
            store(i - SLOTS).wait()
        groups = h // c // SUB
        for j in range(SUB):
            for m in range(groups):
                at = (j * groups + m) * c
                outb[i % SLOTS, :, at : at + c] = inb[i % SLOTS, j, m * h : (m + 1) * h, :].astype(F32)
        store(i).start()
        if i + SLOTS < count:
            load(i + SLOTS).start()
        if i == SLOTS:
            for j in range(4):
                ins[j].wait()
                if j == 0:
                    wide[0] = low[0].astype(F32)
                outs[j].start()
    for i in range(count - SLOTS, count):
        store(i).wait()
    for v in outs:
        v.wait()


def finish_call(small, got, gx_own, gx_got, own, away, ff, heads):
    seg, d = gx_own.shape
    h = d // 2
    rows, cols = got.shape[2:]
    any_ = pl.BlockSpec(memory_space=pl.ANY)
    vmem = pl.BlockSpec(memory_space=pltpu.VMEM)
    dma = lambda n: pltpu.SemaphoreType.DMA((n,))
    return pl.pallas_call(
        finish_kernel,
        in_specs=[vmem] + [any_] * 5,
        out_specs=[any_] * 6 + [vmem] * 5,
        out_shape=[
            struct((2, seg, d), BF), struct((2, seg, d), F32), struct((ff // 2, d), F32), struct((h, ff), F32),
            struct((h, d), F32), struct((h, 3 * d), F32), struct((3, h), F32), struct((3, h), F32),
            struct((1, ff // 2), F32), struct((1, ff // 2), F32), struct((1, heads // 2), F32),
        ],
        scratch_shapes=[
            pltpu.VMEM((SLOTS, SUB, rows, cols), BF), pltpu.VMEM((SLOTS, h, h), F32),
            pltpu.VMEM((3, seg, d), BF), pltpu.VMEM((2, seg, d), F32), dma(SLOTS), dma(SLOTS), dma(8),
        ],
        compiler_params=pltpu.CompilerParams(vmem_limit_bytes=60 * 2**20),
    )(small, got, gx_own, gx_got, own, away)


def local(
    tokens, cotangent, w_qkv, w_out, w_fc1, w_fc2, norm_gain, norm_bias, mid_gain, mid_bias, head_scale, doc_lengths
):
    n = lax.axis_size("rows")
    factors = factors_of(n)
    d = tokens.shape[2]
    ff = w_fc1.shape[1]
    heads = head_scale.shape[0]
    mg, mb = mid_gain[None, :], mid_bias[None, :]
    pieces = 1
    for f in factors[1:]:
        pieces *= f
    half = d // 2
    rows = max(half, 16 * pieces)
    cols = half * half // rows // SUB
    x, normed, qkv, sent, lse, ffn_in, gf, gp, gsent, ghid, out, keep, last, pre, small = front_call(
        rows, cols, doc_lengths, head_scale, norm_gain, norm_bias, mg, mb, tokens, cotangent, w_qkv, w_out, w_fc1, w_fc2
    )
    got, gx_own, gx_got, small, out_got = main_call(
        factors, rows, cols, doc_lengths, head_scale, qkv, gsent, sent, lse, w_qkv, norm_gain, ffn_in, gf, gp, normed, last,
        keep, pre, x, ghid, small, out,
    )
    out, gx, g2, g1, go, gq, gn, bn, gmg, gmb, ghs = finish_call(small, got, gx_own, gx_got, out, out_got, ff, heads)
    return (out, gx, gq, go, g1, g2, gn, bn, gmg.reshape(-1), gmb.reshape(-1), ghs.reshape(-1))


def solution(mesh):
    rows = P("rows", "ctx", None)
    in_specs = (rows, rows) + (P(),) * 9 + (P("rows", None),)
    ctx0 = P("ctx", None)
    out_specs = (rows, rows, ctx0, ctx0, ctx0, ctx0, P(None, "ctx"), P(None, "ctx"), P("ctx"), P("ctx"), P("ctx"))
    return jax.shard_map(local, mesh=mesh, in_specs=in_specs, out_specs=out_specs, check_vma=False)
```

```python
import functools

import jax
import jax.numpy as jnp
from jax import lax
from jax.experimental import pallas as pl
from jax.experimental.pallas import tpu as pltpu
from jax.sharding import PartitionSpec as P

EPS = 1e-05
MASKED = -1e30
BF = jnp.bfloat16
F32 = jnp.float32
REACH = 256
QB = 128


def dot(a, b, ca, cb):
    return lax.dot_general(a, b, (((ca,), (cb,)), ((), ())), preferred_element_type=F32)


def ln_stats(v):
    mean = jnp.mean(v, axis=-1, keepdims=True)
    cen = v - mean
    inv = lax.rsqrt(jnp.mean(cen * cen, axis=-1, keepdims=True) + EPS)
    return cen * inv, inv


def ln_back(e, gain, n, inv):
    a = e * gain
    return inv * (
        a - jnp.mean(a, axis=-1, keepdims=True) - n * jnp.mean(a * n, axis=-1, keepdims=True)
    )


def colsum(v):
    return jnp.sum(v, axis=0, keepdims=True)


def struct(shape, dtype):
    return jax.ShapeDtypeStruct(shape, dtype)


def key_range(i):
    return max(0, i * QB - REACH), (i + 1) * QB


def fill_bias(start, bias, t):
    for i in range(t // QB):
        k0, k1 = key_range(i)
        u = lax.broadcasted_iota(jnp.int32, (k1 - k0, QB), 0) + k0
        q = lax.broadcasted_iota(jnp.int32, (k1 - k0, QB), 1) + i * QB
        first = start[:, i * QB : (i + 1) * QB]
        ok = (u >= first) & (u <= q)
        one = jnp.where(ok, 0.0, MASKED).astype(F32)
        bias[i, 0 : k1 - k0, 0:QB] = one
        bias[i, 0 : k1 - k0, QB : 2 * QB] = one


def both_heads(v, hd):
    lane = lax.broadcasted_iota(jnp.int32, v.shape, 1)
    zero = jnp.zeros_like(v)
    return jnp.concatenate([jnp.where(lane < hd, v, zero), jnp.where(lane < hd, zero, v)], axis=0)


def put_chunk(ref, k, v):
    h, c = v.shape[0], ref.shape[2]
    groups = ref.shape[1] // h
    for j in range(SUB):
        for m in range(groups):
            at = (j * groups + m) * c
            ref[SUB * k + j, m * h : (m + 1) * h, :] = v[:, at : at + c]


BLOCKS = 12
SUB = 2
CHUNKS = BLOCKS * SUB
PRE = 3 * SUB
F_Q1, F_Q2, F_AT, F_FC, F_NM, F_A, F_B1, F_O, F_B2, F_END = 0, 3, 6, 14, 18, 22, 26, 30, 34, 38
MESH = pl.DeviceIdType.MESH


def remote(src, dst, ss, rs, to):
    return pltpu.make_async_remote_copy(src, dst, ss, rs, device_id=to, device_id_type=MESH)


def head_lanes(scale, pair, shape, hd):
    lane = lax.broadcasted_iota(jnp.int32, shape, 1)
    return jnp.where(lane < hd, scale[2 * pair], scale[2 * pair + 1])


def front_kernel(lengths, scale, gain, offset, mg, mb, h_tok, h_cot, h_wqkv, h_wo, h_w1, h_w2,
                 o_x, o_nrm, o_qkv, o_sent, lse, o_ffn, o_gf, o_gp, o_gs, o_gh, o_out, o_keep, o_last, pre, small,
                 wb, wo, xb, cotb, nrm, qkvb, sent, bias, act, mid, nmid, gfb, r_mid, r_cot, n1, n2, hid, acc, ffn,
                 sendw, keepw, s1, s2, smid, ta, tb, wsem, lsem, osem, ss, rs):
    tick = pl.program_id(0)
    me = lax.axis_index("rows")
    ctx = lax.axis_index("ctx")
    core = lax.rem(me, 2)
    sibling = (me + 1 - 2 * core, ctx)
    other_ctx = (me, 1 - ctx)
    t, d = xb.shape
    seg = t // 2
    blocks = act.shape[0]
    width = blocks * act.shape[2]
    h = d // 2

    def rows_of(c):
        return pl.ds(pl.multiple_of(c * seg, seg), seg)

    def w_copy(ref, i):
        return pltpu.make_async_copy(ref, wb.at[lax.rem(i, 3)], wsem.at[lax.rem(i, 3)])

    def col(ref, i):
        return ref.at[:, pl.ds(pl.multiple_of(i * d, d), d)]

    def row(ref, i):
        return ref.at[pl.ds(pl.multiple_of(i * d, d), d), :]

    def w_start(i):
        pl.when(i < 6)(lambda: w_copy(col(h_wqkv, lax.rem(i, 3)), i).start())
        pl.when((i >= 6) & (i < 10))(lambda: w_copy(col(h_w1, i - 6), i).start())
        pl.when((i >= 10) & (i < 18))(lambda: w_copy(row(h_w2, lax.rem(i - 10, 4)), i).start())
        pl.when((i >= 18) & (i < 22))(lambda: w_copy(col(h_w1, i - 18), i).start())

    def w_next(i):
        w_copy(row(h_w2, 0), i).wait()
        w_start(i + 2)
        return wb.at[lax.rem(i, 3)]

    def tok_copy():
        return remote(h_tok.at[1 - ctx], xb.at[rows_of(ctx)], ss.at[0], rs.at[0], other_ctx)

    def cot_copy():
        return remote(h_cot.at[1 - ctx], cotb.at[rows_of(ctx)], ss.at[1], rs.at[1], other_ctx)

    def cot_core():
        return remote(cotb, r_cot, ss.at[2], rs.at[2], sibling)

    def mid_core(i):
        return remote(mid.at[2 * i + 1 - core], r_mid.at[i], ss.at[3 + i], rs.at[3 + i], sibling)

    def pre_copy(k):
        return remote(sendw.at[k], pre.at[k], ss.at[5 + k], rs.at[5 + k], other_ctx)

    def load_copy(j):
        src, dst = [(h_tok.at[ctx], xb.at[rows_of(ctx)]), (h_cot.at[ctx], cotb.at[rows_of(ctx)]), (h_wo, wo)][j]
        return pltpu.make_async_copy(src, dst, lsem.at[j])

    outs = [(xb, o_x), (nrm, o_nrm), (qkvb, o_qkv), (sent, o_sent), (ffn, o_ffn), (qkvb.at[0], o_gp), (qkvb.at[1], o_gs),
            (hid, o_gh), (qkvb.at[2], o_out), (keepw, o_keep), (sendw.at[pl.ds(PRE, 4 * SUB - PRE)], o_last), (gfb, o_gf)]

    def out_copy(j):
        return pltpu.make_async_copy(outs[j][0], outs[j][1], osem.at[j])

    @pl.when(tick == 0)
    def _():
        barrier = pltpu.get_barrier_semaphore()
        for p in (other_ctx, sibling):
            pl.semaphore_signal(barrier, inc=1, device_id=p, device_id_type=MESH)
        load_copy(0).start()
        w_start(0)
        w_start(1)
        load_copy(1).start()
        load_copy(2).start()
        pl.semaphore_wait(barrier, 2)
        tok_copy().start()
        cot_copy().start()
        small[...] = jnp.zeros_like(small)
        at = lax.broadcasted_iota(jnp.int32, (1, t), 1)
        start = jnp.zeros((1, t), jnp.int32)
        bound = jnp.int32(0)
        for i in range(lengths.shape[1]):
            bound = bound + lengths[ctx, i]
            start = jnp.where(at >= bound, bound, start)
        fill_bias(start, bias, t)
        load_copy(0).wait()

    @pl.when(tick == F_Q2)
    def _():
        tok_copy().wait_recv()
        out_copy(0).start()

    for own in (True, False):
        first = F_Q1 if own else F_Q2
        here = rows_of(ctx if own else 1 - ctx)

        @pl.when(tick == first)
        def _(here=here):
            n, _ = ln_stats(xb[here, :].astype(F32))
            nrm[here, :] = (n * gain[0:1, :] + offset[0:1, :]).astype(BF)

        @pl.when((tick >= first) & (tick < first + 3))
        def _(here=here, first=first):
            w = w_next(tick)
            qkvb[tick - first, here, :] = dot(nrm[here, :], w[...], 1, 0).astype(BF)

    @pl.when(tick == F_AT)
    def _():
        out_copy(1).start()
        out_copy(2).start()
        cot_copy().wait_recv()
        load_copy(1).wait()
        cot_core().start()

    @pl.when((tick >= F_AT) & (tick < F_FC))
    def _():
        pair = tick - F_AT
        hd = 64
        at = pl.ds(pl.multiple_of(pair * 128, 128), 128)
        vt = qkvb[2, :, at].astype(F32).T.astype(BF)
        sc = head_lanes(scale, pair, (1, 128), hd)
        for i in range(t // QB):
            k0, k1 = key_range(i)
            qs = slice(i * QB, (i + 1) * QB)
            qm = (both_heads(qkvb[0, qs, at], hd) * (hd**-0.5)).astype(BF)
            st = dot(qkvb[1, k0:k1, at], qm, 1, 1) + bias[i, 0 : k1 - k0, :]
            top = jnp.max(st, axis=0, keepdims=True)
            pt = jnp.exp(st - top)
            total = jnp.sum(pt, axis=0, keepdims=True)
            ot = dot(vt[:, k0:k1], pt.astype(BF), 1, 0) * (1.0 / total)
            o = jnp.concatenate([ot[0:hd, 0:QB], ot[hd:, QB:]], axis=0).T
            sent[qs, at] = (o * sc).astype(BF)
            ls = top + jnp.log(total)
            lse[pair, 0:1, qs] = ls[:, 0:QB]
            lse[pair, 1:2, qs] = ls[:, QB:]

    @pl.when(tick == F_FC)
    def _():
        out_copy(3).start()
        load_copy(2).wait()
        n, inv = ln_stats(dot(sent[...], wo[...], 1, 0))
        n1[...] = n
        s1[...] = inv
        hidden = xb[...].astype(F32) + n * gain[1:2, :] + offset[1:2, :]
        hid[...] = hidden
        n, inv = ln_stats(hidden)
        n2[...] = n
        s2[...] = inv
        ffn[...] = (n * gain[2:3, :] + offset[2:3, :]).astype(BF)
        ta[...] = jnp.zeros_like(ta)
        out_copy(4).start()

    @pl.when((tick >= F_FC) & (tick < F_NM))
    def _():
        i = tick - F_FC
        w = w_next(6 + i)
        f = dot(ffn[...], w[...], 1, 0)
        phi = 0.5 + 0.5 * lax.erf(f * (0.5**0.5))
        a = f * phi
        gfb[i] = (phi + f * (jnp.exp(-0.5 * f * f) * 0.3989422804014327)).astype(BF)
        act[i] = a
        ta[...] += jnp.sum(a, axis=-1, keepdims=True)

    @pl.when(tick == F_NM)
    def _():
        mean = ta[...] * (1.0 / width)
        sq = jnp.zeros_like(mean)
        for j in range(blocks):
            c = act[j] - mean
            act[j] = c
            sq += jnp.sum(c * c, axis=-1, keepdims=True)
        smid[...] = lax.rsqrt(sq * (1.0 / width) + EPS)
        ta[...] = jnp.zeros_like(ta)
        tb[...] = jnp.zeros_like(tb)

    @pl.when((tick >= F_NM) & (tick < F_B1))
    def _():
        j = tick - F_NM
        i = lax.rem(j, 2) * 2 + jnp.where(j < 2, 1 - core, core)
        n = act[i] * smid[...]
        nmid[i] = n.astype(BF)
        vec = pl.ds(pl.multiple_of(i * d, d), d)
        mid[i] = (n * mg[:, vec] + mb[:, vec]).astype(BF)
        pl.when(j < 2)(lambda: mid_core(j).start())

    @pl.when(tick == F_A)
    def _():
        out_copy(1).wait()
        out_copy(2).wait()

    @pl.when((tick >= F_B1) & (tick < F_O))
    def _():
        i = tick - F_B1
        w = w_next(10 + i)
        e = dot(cotb[...], w[...], 1, 1)
        n = nmid[i].astype(F32)
        vec = pl.ds(pl.multiple_of(i * d, d), d)
        small[pl.ds(6 + i, 1), :] = colsum(e * n)
        small[pl.ds(6 + blocks + i, 1), :] = colsum(e)
        a = e * mg[:, vec]
        act[i] = a
        ta[...] += jnp.sum(a, axis=-1, keepdims=True)
        tb[...] += jnp.sum(a * n, axis=-1, keepdims=True)

    @pl.when(tick == F_A)
    def _():
        cot_core().wait_recv()
        mid_core(0).wait_recv()
        mid_core(1).wait_recv()

    @pl.when((tick >= F_A) & (tick < F_B1))
    def _():
        k = tick - F_A
        a_at = pl.ds(pl.multiple_of((k // 2) * h, h), h)
        b_at = pl.ds(pl.multiple_of(lax.rem(k, 2) * h, h), h)
        for far in (True, False):
            x = 1 - ctx if far else ctx
            v = dot(mid[2 * x + core, :, a_at], cotb[:, b_at], 0, 0) + dot(r_mid[x, :, a_at], r_cot[:, b_at], 0, 0)
            put_chunk(sendw if far else keepw, k, v.astype(BF))
            if far:
                for j in range(SUB):
                    c = SUB * k + j
                    pl.when(c < PRE)(lambda c=c: pre_copy(c).start())

    @pl.when(tick == F_O)
    def _():
        out_copy(9).start()
        out_copy(10).start()

    @pl.when((tick >= F_O) & (tick < F_B2))
    def _():
        i = tick - F_O
        w = w_next(14 + i)
        hid[...] += dot(mid[i], w[...], 1, 0)

    @pl.when(tick == F_B2 - 1)
    def _():
        qkvb[2] = hid[...].astype(BF)
        out_copy(8).start()

    @pl.when((tick >= F_B2) & (tick < F_END))
    def _():
        i = tick - F_B2
        w = w_next(18 + i)
        n = nmid[i].astype(F32)
        a = act[i] - ta[...] * (1.0 / width) - n * (tb[...] * (1.0 / width))
        gf = (a * smid[...] * gfb[i].astype(F32)).astype(BF)
        gfb[i] = gf
        v = dot(gf, w[...], 1, 1)

        @pl.when(i == 0)
        def _():
            acc[...] = v

        @pl.when(i > 0)
        def _():
            acc[...] += v

    @pl.when(tick == F_END - 1)
    def _():
        out_copy(11).start()
        e = acc[...]
        n = n2[...]
        small[2:3, :] = colsum(e * n)
        small[5:6, :] = colsum(e)
        gh = cotb[...].astype(F32) + ln_back(e, gain[2:3, :], n, s2[...])
        hid[...] = gh
        out_copy(7).start()
        n = n1[...]
        small[1:2, :] = colsum(gh * n)
        small[4:5, :] = colsum(gh)
        gp = ln_back(gh, gain[1:2, :], n, s1[...]).astype(BF)
        qkvb[0] = gp
        out_copy(5).start()
        qkvb[1] = dot(gp, wo[...], 1, 1).astype(BF)
        out_copy(6).start()
        for j in (0, 3, 4, 5, 6, 7, 8, 9, 10, 11):
            out_copy(j).wait()
        tok_copy().wait_send()
        cot_copy().wait_send()
        cot_core().wait_send()
        mid_core(0).wait_send()
        mid_core(1).wait_send()
        for k in range(PRE):
            pre_copy(k).wait()


def front_call(rows, cols, lengths, scale, gain, offset, mg, mb, tok, cot, wqkv, wo, w1, w2):
    seg, d = tok.shape[1:]
    t = 2 * seg
    ff = w1.shape[1]
    blocks = ff // d
    pairs = d // 128
    any_ = pl.BlockSpec(memory_space=pl.ANY)
    smem = pl.BlockSpec(memory_space=pltpu.SMEM)
    whole = lambda shape: pl.BlockSpec(shape, lambda i: (0,) * len(shape))
    vm = lambda *shape: pltpu.VMEM(shape, BF)
    vf = lambda *shape: pltpu.VMEM(shape, F32)
    dma = lambda n: pltpu.SemaphoreType.DMA((n,))
    small = (6 + 2 * blocks + 2, d)
    td = struct((t, d), BF)
    return pl.pallas_call(
        front_kernel,
        grid=(F_END,),
        in_specs=[smem, smem, whole((3, d)), whole((3, d)), whole((1, ff)), whole((1, ff))] + [any_] * 6,
        out_specs=[any_] * 4 + [whole((pairs, 2, t))] + [any_] * 9 + [whole(small)],
        out_shape=[
            td, td, struct((3, t, d), BF), td, struct((pairs, 2, t), F32), td, struct((blocks, t, d), BF), td, td,
            struct((t, d), F32), td, struct((4 * SUB, rows, cols), BF), struct((4 * SUB - PRE, rows, cols), BF),
            struct((PRE, rows, cols), BF), struct(small, F32),
        ],
        scratch_shapes=[
            vm(3, d, d), vm(d, d), vm(t, d), vm(t, d), vm(t, d), vm(3, t, d), vm(t, d), vf(t // QB, QB + REACH, 2 * QB),
            vf(blocks, t, d), vm(blocks, t, d), vm(blocks, t, d), vm(blocks, t, d), vm(2, t, d), vm(t, d),
            vf(t, d), vf(t, d), vf(t, d), vf(t, d), vm(t, d), vm(4 * SUB, rows, cols), vm(4 * SUB, rows, cols),
            vf(t, 1), vf(t, 1), vf(t, 1), vf(t, 1), vf(t, 1), dma(3), dma(3), dma(12), dma(5 + PRE), dma(5 + PRE),
        ],
        compiler_params=pltpu.CompilerParams(collective_id=1, has_side_effects=True, vmem_limit_bytes=60 * 2**20),
    )(lengths, scale, gain, offset, mg, mb, tok, cot, wqkv, wo, w1, w2)


def factors_of(n):
    out = []
    while n > 1:
        out.append(2)
        n //= 2
    return out


ATT_TICKS = (0, 1, 2, 4, 5, 7, 8, 10)
WG_TICKS = (3, 6, 9, 11, 12, 13, 14, 15)
T_IN, T_TAIL = 16, 22


def lags_of(n_rs):
    return (0,) + tuple(range(2, 2 * n_rs - 1)) + (2 * n_rs,)


T_OUT = 26


EVENT_TICKS = tuple(range(T_TAIL))
AHEAD = 16


def count_before(ticks, i):
    done = 0
    for at in sorted(set(ticks)):
        done = done + jnp.where(i > at, ticks.count(at), 0)
    return done


def event_ticks(n_events):
    more = n_events - len(EVENT_TICKS)
    return EVENT_TICKS + tuple(range(T_TAIL, T_TAIL + more))


def send_ticks(n_events):
    made = [0] * (4 * SUB - PRE)
    for at in WG_TICKS:
        made += [at] * SUB
    events = event_ticks(n_events)
    return tuple(max(at, events[max(PRE + j - AHEAD, 0)]) for j, at in enumerate(made))


def tick_count(n_events):
    return T_TAIL + max(n_events - len(EVENT_TICKS), 10)


def main_kernel(factors, lengths, scale, q, k, v, gs, sn, lse, wq, gain,
                h_sent, h_ffn, h_gf, h_gp, h_nrm, h_last, h_keep, h_pre, h_x, h_ghid, h_small, h_out,
                out, gx_own, gx_got, small_out, out_got, *scr):
    tick = pl.program_id(0)
    n_rs = len(factors)
    chunks, rows, cols = out.shape[0], out.shape[2], out.shape[3]
    t, d = h_sent.shape
    hd2 = d // 2
    me = lax.axis_index("rows")
    ctx = lax.axis_index("ctx")
    fs = [2] + factors[1:]
    strides, st = [0], 2
    for f in factors[1:]:
        strides.append(st)
        st *= f
    size = [rows]
    for f in fs[1:]:
        size.append(size[-1] // f)
    pos = [ctx] + [lax.rem(me // strides[i], fs[i]) for i in range(1, n_rs)]
    off = [0]
    for i in range(1, n_rs):
        off.append(off[-1] + pos[i] * size[i])
    bits = []
    b = 1
    while b < lax.axis_size("rows"):
        bits.append(b)
        b *= 2

    def peer(i, j):
        if i == 0:
            return (me, 1 - ctx)
        return (me + ((pos[i] ^ j) - pos[i]) * strides[i], ctx)

    core = lax.rem(me, 2)
    sibling = (me + 1 - 2 * core, ctx)
    other_ctx = (me, 1 - ctx)

    def bit_peer(b):
        return (me + b - 2 * b * lax.rem(me // b, 2), ctx)

    scr = list(scr)
    take = lambda n: [scr.pop(0) for _ in range(n)]
    sendb, acc, gath = take(3)
    recv = [gath] + take(n_rs - 1)
    small_acc, small_recv = take(2)
    o_sent, o_ffn, o_gf, o_gp, o_nrm = take(5)
    r_sent, r_ffn, r_gf, r_gp, r_nrm, r_gq = take(6)
    gall, bias, gk, gv, gqt, xb, gh, gn_acc, gx_send = take(9)
    rs_s, rs_r = take(n_rs), take(n_rs)
    ag_s, ag_r = [None] + take(n_rs - 1), [None] + take(n_rs - 1)
    core_s, core_r, loc, small_s, small_r, swap_s, swap_r, load, gx_s, gx_r = take(10)

    def part(at, n):
        return pl.ds(at if isinstance(at, int) else pl.multiple_of(at, 16), n)

    def rs_copy(i, c, j):
        if i == 0:
            src, dst = sendb.at[c - PRE], gath.at[c]
        else:
            src = acc.at[c, part(off[i - 1] + (pos[i] ^ j) * size[i], size[i])]
            dst = recv[i].at[c, j - 1]
        return remote(src, dst, rs_s[i].at[c, j - 1], rs_r[i].at[c, j - 1], peer(i, j))

    def ag_copy(i, c, j, arriving):
        at = off[i - 1] + (pos[i] ^ j) * size[i] if arriving else off[i]
        ref = gath.at[c, part(at, size[i])]
        return remote(ref, ref, ag_s[i].at[c, j - 1], ag_r[i].at[c, j - 1], peer(i, j))

    def core_copy(c, arriving):
        to = 1 - core if arriving else core
        return remote(gath.at[c], out.at[c, to], core_s.at[c], core_r.at[c], sibling)

    def own_copy(c):
        return pltpu.make_async_copy(gath.at[c], out.at[c, core], loc.at[c])

    def reduce_stage(i, c):
        if i == 0:
            @pl.when(c >= PRE)
            def _():
                rs_copy(0, c, 1).wait_recv()
        else:
            for j in range(1, fs[i]):
                rs_copy(i, c, j).wait_recv()
        here = part(off[i], size[i])
        val = acc[c, here].astype(F32)
        if i == 0:
            val = val + gath[c].astype(F32)
        else:
            for j in range(1, fs[i]):
                val = val + recv[i][c, j - 1].astype(F32)
        if i + 1 < n_rs:
            acc[c, here] = val.astype(BF)
            for j in range(1, fs[i + 1]):
                rs_copy(i + 1, c, j).start()
        else:
            gath[c, here] = val.astype(BF)
            for j in range(1, fs[i]):
                ag_copy(i, c, j, False).start()

    def gather_stage(i, c):
        for j in range(1, fs[i]):
            ag_copy(i, c, j, True).wait_recv()
        if i > 1:
            for j in range(1, fs[i - 1]):
                ag_copy(i - 1, c, j, False).start()
        else:
            core_copy(c, False).start()
            own_copy(c).start()

    def small_copy(i):
        to = other_ctx if i == 0 else bit_peer(bits[i - 1])
        return remote(small_acc.at[i], small_recv.at[i], small_s.at[i], small_r.at[i], to)

    mine = pl.ds(pl.multiple_of(core * hd2, hd2), hd2)
    theirs = pl.ds(pl.multiple_of((1 - core) * hd2, hd2), hd2)
    swaps = [(h_sent, r_sent), (h_gp.at[:, theirs], r_gp), (h_ffn, r_ffn), (h_gf.at[1 - core], r_gf.at[0]), (h_nrm, r_nrm),
             (h_gf.at[3 - core], r_gf.at[1])]
    loads = [(h_sent, o_sent), (h_gp.at[:, mine], o_gp), (h_ffn, o_ffn), (h_gf.at[core], o_gf.at[0]), (h_nrm, o_nrm),
             (h_x, xb), (h_ghid, gh), (h_small, small_acc.at[0]), (h_last, sendb.at[pl.ds(0, 4 * SUB - PRE)]),
             (h_keep, acc.at[pl.ds(0, 4 * SUB)]), (h_pre, gath.at[pl.ds(0, PRE)]), (h_gf.at[2 + core], o_gf.at[1])]

    def swap_copy(j):
        return remote(swaps[j][0], swaps[j][1], swap_s.at[j], swap_r.at[j], sibling)

    def gq_copy():
        return remote(gall.at[1 - core], r_gq, swap_s.at[6], swap_r.at[6], sibling)

    def load_copy(j):
        return pltpu.make_async_copy(loads[j][0], loads[j][1], load.at[j])

    seg = t // 2

    def rows_of(c):
        return pl.ds(pl.multiple_of(c * seg, seg), seg)

    def gx_copy():
        return remote(gx_send, gx_got, gx_s.at[0], gx_r.at[0], other_ctx)

    def out_copy():
        return remote(h_out.at[rows_of(1 - ctx)], out_got, gx_s.at[1], gx_r.at[1], other_ctx)

    @pl.when(tick == 0)
    def _():
        peers = [other_ctx, sibling]
        for i in range(1, n_rs):
            peers += [peer(i, j) for j in range(1, fs[i])]
        barrier = pltpu.get_barrier_semaphore()
        for p in peers:
            pl.semaphore_signal(barrier, inc=1, device_id=p, device_id_type=MESH)
        for j in (10, 9, 8, 0, 1, 2, 3, 11, 4, 5, 6, 7):
            load_copy(j).start()
        pl.semaphore_wait(barrier, len(peers))
        for j in (0, 1, 2, 3, 5, 4):
            swap_copy(j).start()
        for j in (10, 9, 8):
            load_copy(j).wait()
        at = lax.broadcasted_iota(jnp.int32, (1, t), 1)
        start = jnp.zeros((1, t), jnp.int32)
        bound = jnp.int32(0)
        for i in range(lengths.shape[1]):
            bound = bound + lengths[ctx, i]
            start = jnp.where(at >= bound, bound, start)
        fill_bias(start, bias, t)
        load_copy(7).wait()

    pair = count_before(ATT_TICKS, tick)

    @pl.when(count_before(ATT_TICKS, tick + 1) > pair)
    def _():
        hd = q.shape[2] // 2
        kt = k[0].astype(F32).T.astype(BF)
        gsf = gs[...].astype(F32)
        prod = (gsf * sn[...].astype(F32)).T
        d0 = jnp.sum(prod[0:hd], axis=0, keepdims=True)
        d1 = jnp.sum(prod[hd:], axis=0, keepdims=True)
        lane = lax.broadcasted_iota(jnp.int32, (1, d), 1)
        h0 = jnp.sum(d0, axis=-1, keepdims=True)
        h1 = jnp.sum(d1, axis=-1, keepdims=True)
        small_acc[0, 14:15, :] += (
            jnp.where(lane == 2 * pair, h0 / scale[2 * pair], 0.0)
            + jnp.where(lane == 2 * pair + 1, h1 / scale[2 * pair + 1], 0.0)
        )
        ga = (gsf * head_lanes(scale, pair, (1, 2 * hd), hd)).astype(BF)
        gk[...] = jnp.zeros_like(gk)
        gv[...] = jnp.zeros_like(gv)
        for i in range(t // QB):
            k0, k1 = key_range(i)
            qs = slice(i * QB, (i + 1) * QB)
            qm = (both_heads(q[0, qs, :], hd) * (hd**-0.5)).astype(BF)
            gm = both_heads(ga[qs, :], hd)
            sc = dot(k[0, k0:k1, :], qm, 1, 1) + bias[i, 0 : k1 - k0, :]
            ls = jnp.concatenate([lse[0, 0:1, qs], lse[0, 1:2, qs]], axis=1)
            dd = jnp.concatenate([d0[:, qs], d1[:, qs]], axis=1)
            pt = jnp.exp(sc - ls)
            gp = dot(v[0, k0:k1, :], gm, 1, 1)
            ds = (pt * (gp - dd)).astype(BF)
            gv[k0:k1, :] += dot(pt.astype(BF), gm, 1, 0)
            gk[k0:k1, :] += dot(ds, qm, 1, 0)
            gq = dot(kt[:, k0:k1], ds, 1, 0) * (hd**-0.5)
            gqt[:, qs] = jnp.concatenate([gq[0:hd, 0:QB], gq[hd:, QB:]], axis=0)
        per_core = len(ATT_TICKS) // 2
        half = pair // per_core
        at = pl.ds(pl.multiple_of(lax.rem(pair, per_core) * 128, 128), 128)
        gall[half, 0, :, at] = gqt[...].T.astype(BF)
        gall[half, 1, :, at] = gk[...].astype(BF)
        gall[half, 2, :, at] = gv[...].astype(BF)

    @pl.when(tick == ATT_TICKS[-1])
    def _():
        gq_copy().start()

    def wgrad(c, a0, a1, b0, b1):
        for far in (True, False):
            x = 1 - ctx if far else ctx
            val = (dot(a0(x), b0, 0, 0) + dot(a1(x), b1, 0, 0)).astype(BF)
            put_chunk(sendb if far else acc, c - PRE // SUB if far else c, val)

    def half_of(ref):
        return lambda x: ref[:, pl.ds(pl.multiple_of(x * hd2, 128), hd2)]

    @pl.when(tick == T_OUT)
    def _():
        out_copy().start()
        gx_copy().start()

    @pl.when(tick == WG_TICKS[0])
    def _():
        for j in (0, 1):
            load_copy(j).wait()
            swap_copy(j).wait_recv()
        wgrad(4, half_of(o_sent), half_of(r_sent), o_gp[...], r_gp[...])

    @pl.when(tick == WG_TICKS[1])
    def _():
        for j in (2, 3):
            load_copy(j).wait()
            swap_copy(j).wait_recv()
        load_copy(11).wait()
        swap_copy(5).wait_recv()

    block = count_before(WG_TICKS, tick)
    makes = count_before(WG_TICKS, tick + 1) > block

    @pl.when(makes & (block >= 1) & (block < 5))
    def _():
        c = block - 1
        b = lambda ref: ref[c // 2, :, pl.ds(pl.multiple_of(lax.rem(c, 2) * hd2, 128), hd2)]
        wgrad(c + 5, half_of(o_ffn), half_of(r_ffn), b(o_gf), b(r_gf))

    @pl.when(tick == WG_TICKS[5])
    def _():
        load_copy(4).wait()
        swap_copy(4).wait_recv()
        gq_copy().wait_recv()

    @pl.when(makes & (block >= 5))
    def _():
        c = block - 5
        wgrad(c + 9, half_of(o_nrm), half_of(r_nrm), gall[core, c], r_gq[c])

    @pl.when((tick >= T_IN) & (tick < T_TAIL))
    def _():
        j = tick - T_IN
        val = dot(gall[lax.rem(j, 2), j // 2], wq[...], 1, 1)

        @pl.when(j == 0)
        def _():
            gn_acc[...] = val

        @pl.when(j > 0)
        def _():
            gn_acc[...] += val

    @pl.when(tick == T_TAIL - 1)
    def _():
        load_copy(5).wait()
        load_copy(6).wait()
        e = gn_acc[...]
        n, inv = ln_stats(xb[...].astype(F32))
        small_acc[0, 0:1, :] = colsum(e * n)
        small_acc[0, 3:4, :] = colsum(e)
        gh[...] += ln_back(e, gain[0:1, :], n, inv)
        gx_send[...] = gh[rows_of(1 - ctx), :].astype(BF)
        gx_own[...] = gh[rows_of(ctx), :]
        small_copy(0).start()

    def guarded(f, i, c):
        pl.when((c >= 0) & (c < chunks))(lambda: f(i, c))

    lanes = [(reduce_stage, i) for i in range(n_rs)] + [(gather_stage, i) for i in range(n_rs - 1, 0, -1)]

    lags = lags_of(n_rs)
    n_events = chunks + lags[-1]
    sends = send_ticks(n_events)

    def send(c, _):
        rs_copy(0, c, 1).start()
        return 0

    lax.fori_loop(PRE + count_before(sends, tick), PRE + count_before(sends, tick + 1), send, 0)
    events = event_ticks(n_events)
    event = count_before(events, tick)

    @pl.when(count_before(events, tick + 1) > event)
    def _():
        for lag in range(len(lanes) - 1, -1, -1):
            f, i = lanes[lag]
            guarded(f, i, event - lags[lag])

    for i in range(len(bits) + 1):

        @pl.when(tick == T_TAIL + 1 + i)
        def _(i=i):
            small_copy(i).wait_recv()
            if i < len(bits):
                small_acc[i + 1] = small_acc[i] + small_recv[i]
                small_copy(i + 1).start()
            else:
                small_out[...] = small_acc[i] + small_recv[i]

    @pl.when(tick == pl.num_programs(0) - 1)
    def _():
        def finish(c, _):
            for i in range(n_rs):
                for j in range(1, fs[i]):
                    if i == 0:
                        @pl.when(c >= PRE)
                        def _():
                            rs_copy(0, c, 1).wait_send()
                    else:
                        rs_copy(i, c, j).wait_send()
                        ag_copy(i, c, j, False).wait_send()
            core_copy(c, False).wait_send()
            core_copy(c, True).wait_recv()
            own_copy(c).wait()
            return 0

        lax.fori_loop(0, chunks, finish, 0)
        for i in range(len(bits) + 1):
            small_copy(i).wait_send()
        for j in range(6):
            swap_copy(j).wait_send()
        gq_copy().wait_send()
        gx_copy().wait()
        out_copy().wait()


def main_call(factors, rows, cols, lengths, scale, qkv, gsent, sent, lse, w_qkv, gain, ffn_in, gf, gp, normed, last,
              keep, pre, x, ghid, small, out):
    t, d = sent.shape
    h = d // 2
    n = 1
    for f in factors:
        n *= f
    fs = [2] + factors[1:]
    levels = 1
    while n > 1:
        levels += 1
        n //= 2
    size, recv = rows, []
    for f in fs[1:]:
        size //= f
        recv.append(pltpu.VMEM((CHUNKS, f - 1, size, cols), BF))
    dma = lambda *shape: pltpu.SemaphoreType.DMA(shape)
    per = lambda k: [dma(CHUNKS, f - 1) for f in fs[k:]]
    vm = lambda *shape: pltpu.VMEM(shape, BF)
    vf = lambda *shape: pltpu.VMEM(shape, F32)
    pair = lambda i: jnp.minimum(count_before(ATT_TICKS, i), len(ATT_TICKS) - 1)
    part = lambda j: pl.BlockSpec((1, t, 128), lambda i: (j, 0, pair(i)))
    flat = pl.BlockSpec((t, 128), lambda i: (0, pair(i)))
    whole = lambda shape: pl.BlockSpec(shape, lambda i: (0,) * len(shape))
    wcol = lambda i: jnp.clip(i - T_IN, 0, 5)
    any_ = pl.BlockSpec(memory_space=pl.ANY)
    events = CHUNKS + lags_of(len(fs))[-1]
    return pl.pallas_call(
        functools.partial(main_kernel, factors),
        grid=(tick_count(events),),
        in_specs=[
            pl.BlockSpec(memory_space=pltpu.SMEM), pl.BlockSpec(memory_space=pltpu.SMEM),
            part(0), part(1), part(2), flat, flat,
            pl.BlockSpec((1, 2, t), lambda i: (pair(i), 0, 0)),
            pl.BlockSpec((d, h), lambda i: (0, wcol(i))),
            whole((3, d)),
        ] + [any_] * 12,
        out_specs=[any_, whole((t // 2, d)), any_, whole(small.shape), any_],
        out_shape=[
            struct((CHUNKS, 2, rows, cols), BF), struct((t // 2, d), F32), struct((t // 2, d), BF), struct(small.shape, F32),
            struct((t // 2, d), BF),
        ],
        scratch_shapes=[vm(CHUNKS - PRE, rows, cols), vm(CHUNKS, rows, cols), vm(CHUNKS, rows, cols)]
        + recv
        + [vf(levels, *small.shape)] * 2
        + [vm(t, d), vm(t, d), vm(2, t, d), vm(t, h), vm(t, d)]
        + [vm(t, d), vm(t, d), vm(2, t, d), vm(t, h), vm(t, d), vm(3, t, h)]
        + [vm(2, 3, t, h), vf(t // QB, QB + REACH, 2 * QB), vf(t, 128), vf(t, 128), vf(128, t), vm(t, d), vf(t, d), vf(t, d),
           vm(t // 2, d)]
        + per(0) + per(0) + per(1) + per(1)
        + [dma(CHUNKS), dma(CHUNKS), dma(CHUNKS), dma(levels), dma(levels), dma(7), dma(7), dma(12), dma(2), dma(2)],
        compiler_params=pltpu.CompilerParams(collective_id=0, has_side_effects=True, vmem_limit_bytes=60 * 2**20),
    )(lengths, scale, qkv, qkv, qkv, gsent, sent, lse, w_qkv, gain,
      sent, ffn_in, gf, gp, normed, last, keep, pre, x, ghid, small, out)


SLOTS = 8


def finish_kernel(small, got, gx_own, gx_got, own, away, out, gx, g2, g1, go, gq, gn, bn, gmg, gmb, ghs,
                  inb, outb, low, wide, isem, osem, sems):
    ctx = lax.axis_index("ctx")
    seg, d = gx_own.shape
    h = d // 2
    c = got.shape[3]
    blocks = (small.shape[0] - 8) // 2

    def copy(src, dst, j):
        return pltpu.make_async_copy(src, dst, sems.at[j])

    ins = [
        copy(gx_got, low.at[0], 0),
        copy(own.at[pl.ds(pl.multiple_of(ctx * seg, seg), seg)], low.at[1], 1),
        copy(away, low.at[2], 2),
        copy(gx_own, wide.at[1], 3),
    ]
    outs = [
        copy(wide.at[0], gx.at[1 - ctx], 4),
        copy(low.at[1], out.at[ctx], 5),
        copy(low.at[2], out.at[1 - ctx], 6),
        copy(wide.at[1], gx.at[ctx], 7),
    ]

    def place(i):
        k, core = i // 2, i % 2
        if k < 4:
            ref, r, col = g2, core * 2 + k // 2, k % 2
        elif k == 4:
            ref, r, col = go, 0, core
        elif k < 9:
            ref, r, col = g1, 0, (((k - 5) // 2) * 2 + core) * 2 + (k - 5) % 2
        else:
            ref, r, col = gq, 0, (k - 9) * 2 + core
        return ref.at[pl.ds(r * h, h), pl.ds(col * h, h)]

    def load(i):
        src = got.at[pl.ds(i // 2 * SUB, SUB), i % 2]
        return pltpu.make_async_copy(src, inb.at[i % SLOTS], isem.at[i % SLOTS])

    def store(i):
        return pltpu.make_async_copy(outb.at[i % SLOTS], place(i), osem.at[i % SLOTS])

    count = 2 * BLOCKS
    for i in range(SLOTS):
        load(i).start()
    for v in ins:
        v.start()
    half = pl.ds(pl.multiple_of(ctx * h, h), h)
    gn[...] = small[0:3, half]
    bn[...] = small[3:6, half]
    for j in range(blocks // 2):
        at = slice(j * d, (j + 1) * d)
        gmg[:, at] = small[pl.ds(6 + ctx * (blocks // 2) + j, 1), :]
        gmb[:, at] = small[pl.ds(6 + blocks + ctx * (blocks // 2) + j, 1), :]
    n = ghs.shape[1]
    row = small[6 + 2 * blocks : 7 + 2 * blocks, :]
    ghs[...] = jnp.where(ctx == 0, row[:, 0:n], row[:, n : 2 * n])
    for i in range(count):
        load(i).wait()
        if i >= SLOTS:
            store(i - SLOTS).wait()
        groups = h // c // SUB
        for j in range(SUB):
            for m in range(groups):
                at = (j * groups + m) * c
                outb[i % SLOTS, :, at : at + c] = inb[i % SLOTS, j, m * h : (m + 1) * h, :].astype(F32)
        store(i).start()
        if i + SLOTS < count:
            load(i + SLOTS).start()
        if i == SLOTS:
            for j in range(4):
                ins[j].wait()
                if j == 0:
                    wide[0] = low[0].astype(F32)
                outs[j].start()
    for i in range(count - SLOTS, count):
        store(i).wait()
    for v in outs:
        v.wait()


def finish_call(small, got, gx_own, gx_got, own, away, ff, heads):
    seg, d = gx_own.shape
    h = d // 2
    rows, cols = got.shape[2:]
    any_ = pl.BlockSpec(memory_space=pl.ANY)
    vmem = pl.BlockSpec(memory_space=pltpu.VMEM)
    dma = lambda n: pltpu.SemaphoreType.DMA((n,))
    return pl.pallas_call(
        finish_kernel,
        in_specs=[vmem] + [any_] * 5,
        out_specs=[any_] * 6 + [vmem] * 5,
        out_shape=[
            struct((2, seg, d), BF), struct((2, seg, d), F32), struct((ff // 2, d), F32), struct((h, ff), F32),
            struct((h, d), F32), struct((h, 3 * d), F32), struct((3, h), F32), struct((3, h), F32),
            struct((1, ff // 2), F32), struct((1, ff // 2), F32), struct((1, heads // 2), F32),
        ],
        scratch_shapes=[
            pltpu.VMEM((SLOTS, SUB, rows, cols), BF), pltpu.VMEM((SLOTS, h, h), F32),
            pltpu.VMEM((3, seg, d), BF), pltpu.VMEM((2, seg, d), F32), dma(SLOTS), dma(SLOTS), dma(8),
        ],
        compiler_params=pltpu.CompilerParams(vmem_limit_bytes=60 * 2**20),
    )(small, got, gx_own, gx_got, own, away)


def local(
    tokens, cotangent, w_qkv, w_out, w_fc1, w_fc2, norm_gain, norm_bias, mid_gain, mid_bias, head_scale, doc_lengths
):
    n = lax.axis_size("rows")
    factors = factors_of(n)
    d = tokens.shape[2]
    ff = w_fc1.shape[1]
    heads = head_scale.shape[0]
    mg, mb = mid_gain[None, :], mid_bias[None, :]
    pieces = 1
    for f in factors[1:]:
        pieces *= f
    half = d // 2
    rows = max(half, 16 * pieces)
    cols = half * half // rows // SUB
    x, normed, qkv, sent, lse, ffn_in, gf, gp, gsent, ghid, out, keep, last, pre, small = front_call(
        rows, cols, doc_lengths, head_scale, norm_gain, norm_bias, mg, mb, tokens, cotangent, w_qkv, w_out, w_fc1, w_fc2
    )
    got, gx_own, gx_got, small, out_got = main_call(
        factors, rows, cols, doc_lengths, head_scale, qkv, gsent, sent, lse, w_qkv, norm_gain, ffn_in, gf, gp, normed, last,
        keep, pre, x, ghid, small, out,
    )
    out, gx, g2, g1, go, gq, gn, bn, gmg, gmb, ghs = finish_call(small, got, gx_own, gx_got, out, out_got, ff, heads)
    return (out, gx, gq, go, g1, g2, gn, bn, gmg.reshape(-1), gmb.reshape(-1), ghs.reshape(-1))


def solution(mesh):
    rows = P("rows", "ctx", None)
    in_specs = (rows, rows) + (P(),) * 9 + (P("rows", None),)
    ctx0 = P("ctx", None)
    out_specs = (rows, rows, ctx0, ctx0, ctx0, ctx0, P(None, "ctx"), P(None, "ctx"), P("ctx"), P("ctx"), P("ctx"))
    return jax.shard_map(local, mesh=mesh, in_specs=in_specs, out_specs=out_specs, check_vma=False)
```

```python
import functools

import jax
import jax.numpy as jnp
from jax import lax
from jax.experimental import pallas as pl
from jax.experimental.pallas import tpu as pltpu
from jax.sharding import PartitionSpec as P

EPS = 1e-05
MASKED = -1e30
BF = jnp.bfloat16
F32 = jnp.float32
REACH = 256
QB = 128


def dot(a, b, ca, cb):
    return lax.dot_general(a, b, (((ca,), (cb,)), ((), ())), preferred_element_type=F32)


def ln_stats(v):
    mean = jnp.mean(v, axis=-1, keepdims=True)
    cen = v - mean
    inv = lax.rsqrt(jnp.mean(cen * cen, axis=-1, keepdims=True) + EPS)
    return cen * inv, inv


def ln_back(e, gain, n, inv):
    a = e * gain
    return inv * (
        a - jnp.mean(a, axis=-1, keepdims=True) - n * jnp.mean(a * n, axis=-1, keepdims=True)
    )


def colsum(v):
    return jnp.sum(v, axis=0, keepdims=True)


def struct(shape, dtype):
    return jax.ShapeDtypeStruct(shape, dtype)


def key_range(i):
    return max(0, i * QB - REACH), (i + 1) * QB


def fill_bias(start, bias, t):
    for i in range(t // QB):
        k0, k1 = key_range(i)
        u = lax.broadcasted_iota(jnp.int32, (k1 - k0, QB), 0) + k0
        q = lax.broadcasted_iota(jnp.int32, (k1 - k0, QB), 1) + i * QB
        first = start[:, i * QB : (i + 1) * QB]
        ok = (u >= first) & (u <= q)
        one = jnp.where(ok, 0.0, MASKED).astype(F32)
        bias[i, 0 : k1 - k0, 0:QB] = one
        bias[i, 0 : k1 - k0, QB : 2 * QB] = one


def both_heads(v, hd):
    lane = lax.broadcasted_iota(jnp.int32, v.shape, 1)
    zero = jnp.zeros_like(v)
    return jnp.concatenate([jnp.where(lane < hd, v, zero), jnp.where(lane < hd, zero, v)], axis=0)


def put_chunk(ref, k, v):
    h, c = v.shape[0], ref.shape[2]
    groups = ref.shape[1] // h
    for j in range(SUB):
        for m in range(groups):
            at = (j * groups + m) * c
            ref[SUB * k + j, m * h : (m + 1) * h, :] = v[:, at : at + c]


BLOCKS = 12
SUB = 2
CHUNKS = BLOCKS * SUB
PRE = 2 * SUB
F_Q1, F_Q2, F_AT, F_FC, F_NM, F_A, F_B1, F_O, F_B2, F_END = 0, 3, 6, 10, 14, 18, 22, 26, 30, 34
MESH = pl.DeviceIdType.MESH


def remote(src, dst, ss, rs, to):
    return pltpu.make_async_remote_copy(src, dst, ss, rs, device_id=to, device_id_type=MESH)


def head_lanes(scale, pair, shape, hd):
    lane = lax.broadcasted_iota(jnp.int32, shape, 1)
    return jnp.where(lane < hd, scale[2 * pair], scale[2 * pair + 1])


def front_kernel(lengths, scale, gain, offset, mg, mb, h_tok, h_cot, h_wqkv, h_wo, h_w1, h_w2,
                 o_x, o_nrm, o_qkv, o_sent, lse, o_ffn, o_gf, o_gp, o_gs, o_gh, o_out, o_keep, o_last, pre, small,
                 wb, wo, xb, cotb, nrm, qkvb, sent, bias, act, mid, nmid, gfb, r_mid, r_cot, n1, n2, hid, acc, ffn,
                 sendw, keepw, s1, s2, smid, ta, tb, wsem, lsem, osem, ss, rs):
    tick = pl.program_id(0)
    me = lax.axis_index("rows")
    ctx = lax.axis_index("ctx")
    core = lax.rem(me, 2)
    sibling = (me + 1 - 2 * core, ctx)
    other_ctx = (me, 1 - ctx)
    t, d = xb.shape
    seg = t // 2
    blocks = act.shape[0]
    width = blocks * act.shape[2]
    h = d // 2

    def rows_of(c):
        return pl.ds(pl.multiple_of(c * seg, seg), seg)

    def w_copy(ref, i):
        return pltpu.make_async_copy(ref, wb.at[lax.rem(i, 3)], wsem.at[lax.rem(i, 3)])

    def col(ref, i):
        return ref.at[:, pl.ds(pl.multiple_of(i * d, d), d)]

    def row(ref, i):
        return ref.at[pl.ds(pl.multiple_of(i * d, d), d), :]

    def w_start(i):
        pl.when(i < 6)(lambda: w_copy(col(h_wqkv, lax.rem(i, 3)), i).start())
        pl.when((i >= 6) & (i < 10))(lambda: w_copy(col(h_w1, i - 6), i).start())
        pl.when((i >= 10) & (i < 18))(lambda: w_copy(row(h_w2, lax.rem(i - 10, 4)), i).start())
        pl.when((i >= 18) & (i < 22))(lambda: w_copy(col(h_w1, i - 18), i).start())

    def w_next(i):
        w_copy(row(h_w2, 0), i).wait()
        w_start(i + 2)
        return wb.at[lax.rem(i, 3)]

    def tok_copy():
        return remote(h_tok.at[1 - ctx], xb.at[rows_of(ctx)], ss.at[0], rs.at[0], other_ctx)

    def cot_copy():
        return remote(h_cot.at[1 - ctx], cotb.at[rows_of(ctx)], ss.at[1], rs.at[1], other_ctx)

    def cot_core():
        return remote(cotb, r_cot, ss.at[2], rs.at[2], sibling)

    def mid_core(i):
        return remote(mid.at[2 * i + 1 - core], r_mid.at[i], ss.at[3 + i], rs.at[3 + i], sibling)

    def pre_copy(k):
        return remote(sendw.at[k], pre.at[k], ss.at[5 + k], rs.at[5 + k], other_ctx)

    def load_copy(j):
        src, dst = [(h_tok.at[ctx], xb.at[rows_of(ctx)]), (h_cot.at[ctx], cotb.at[rows_of(ctx)]), (h_wo, wo)][j]
        return pltpu.make_async_copy(src, dst, lsem.at[j])

    outs = [(xb, o_x), (nrm, o_nrm), (qkvb, o_qkv), (sent, o_sent), (ffn, o_ffn), (qkvb.at[0], o_gp), (qkvb.at[1], o_gs),
            (hid, o_gh), (qkvb.at[2], o_out), (keepw, o_keep), (sendw.at[pl.ds(PRE, 4 * SUB - PRE)], o_last), (gfb, o_gf)]

    def out_copy(j):
        return pltpu.make_async_copy(outs[j][0], outs[j][1], osem.at[j])

    @pl.when(tick == 0)
    def _():
        barrier = pltpu.get_barrier_semaphore()
        for p in (other_ctx, sibling):
            pl.semaphore_signal(barrier, inc=1, device_id=p, device_id_type=MESH)
        load_copy(0).start()
        w_start(0)
        w_start(1)
        load_copy(1).start()
        load_copy(2).start()
        pl.semaphore_wait(barrier, 2)
        tok_copy().start()
        cot_copy().start()
        small[...] = jnp.zeros_like(small)
        at = lax.broadcasted_iota(jnp.int32, (1, t), 1)
        start = jnp.zeros((1, t), jnp.int32)
        bound = jnp.int32(0)
        for i in range(lengths.shape[1]):
            bound = bound + lengths[ctx, i]
            start = jnp.where(at >= bound, bound, start)
        fill_bias(start, bias, t)
        load_copy(0).wait()

    @pl.when(tick == F_Q2)
    def _():
        tok_copy().wait_recv()
        out_copy(0).start()

    for own in (True, False):
        first = F_Q1 if own else F_Q2
        here = rows_of(ctx if own else 1 - ctx)

        @pl.when(tick == first)
        def _(here=here):
            n, _ = ln_stats(xb[here, :].astype(F32))
            nrm[here, :] = (n * gain[0:1, :] + offset[0:1, :]).astype(BF)

        @pl.when((tick >= first) & (tick < first + 3))
        def _(here=here, first=first):
            w = w_next(tick)
            qkvb[tick - first, here, :] = dot(nrm[here, :], w[...], 1, 0).astype(BF)

    @pl.when(tick == F_AT)
    def _():
        out_copy(1).start()
        out_copy(2).start()
        cot_copy().wait_recv()
        load_copy(1).wait()
        cot_core().start()

    @pl.when((tick >= F_AT) & (tick < F_FC))
    def _():
        hd = 64
        for pair in (2 * (tick - F_AT), 2 * (tick - F_AT) + 1):
            at = pl.ds(pl.multiple_of(pair * 128, 128), 128)
            vt = qkvb[2, :, at].astype(F32).T.astype(BF)
            sc = head_lanes(scale, pair, (1, 128), hd)
            for i in range(t // QB):
                k0, k1 = key_range(i)
                qs = slice(i * QB, (i + 1) * QB)
                qm = (both_heads(qkvb[0, qs, at], hd) * (hd**-0.5)).astype(BF)
                st = dot(qkvb[1, k0:k1, at], qm, 1, 1) + bias[i, 0 : k1 - k0, :]
                top = jnp.max(st, axis=0, keepdims=True)
                pt = jnp.exp(st - top)
                total = jnp.sum(pt, axis=0, keepdims=True)
                ot = dot(vt[:, k0:k1], pt.astype(BF), 1, 0) * (1.0 / total)
                o = jnp.concatenate([ot[0:hd, 0:QB], ot[hd:, QB:]], axis=0).T
                sent[qs, at] = (o * sc).astype(BF)
                ls = top + jnp.log(total)
                lse[pair, 0:1, qs] = ls[:, 0:QB]
                lse[pair, 1:2, qs] = ls[:, QB:]

    @pl.when(tick == F_FC)
    def _():
        out_copy(3).start()
        load_copy(2).wait()
        n, inv = ln_stats(dot(sent[...], wo[...], 1, 0))
        n1[...] = n
        s1[...] = inv
        hidden = xb[...].astype(F32) + n * gain[1:2, :] + offset[1:2, :]
        hid[...] = hidden
        n, inv = ln_stats(hidden)
        n2[...] = n
        s2[...] = inv
        ffn[...] = (n * gain[2:3, :] + offset[2:3, :]).astype(BF)
        ta[...] = jnp.zeros_like(ta)
        out_copy(4).start()

    @pl.when((tick >= F_FC) & (tick < F_NM))
    def _():
        i = tick - F_FC
        w = w_next(6 + i)
        f = dot(ffn[...], w[...], 1, 0)
        phi = 0.5 + 0.5 * lax.erf(f * (0.5**0.5))
        a = f * phi
        gfb[i] = (phi + f * (jnp.exp(-0.5 * f * f) * 0.3989422804014327)).astype(BF)
        act[i] = a
        ta[...] += jnp.sum(a, axis=-1, keepdims=True)

    @pl.when(tick == F_NM)
    def _():
        mean = ta[...] * (1.0 / width)
        sq = jnp.zeros_like(mean)
        for j in range(blocks):
            c = act[j] - mean
            act[j] = c
            sq += jnp.sum(c * c, axis=-1, keepdims=True)
        smid[...] = lax.rsqrt(sq * (1.0 / width) + EPS)
        ta[...] = jnp.zeros_like(ta)
        tb[...] = jnp.zeros_like(tb)

    @pl.when((tick >= F_NM) & (tick < F_B1))
    def _():
        j = tick - F_NM
        i = lax.rem(j, 2) * 2 + jnp.where(j < 2, 1 - core, core)
        n = act[i] * smid[...]
        nmid[i] = n.astype(BF)
        vec = pl.ds(pl.multiple_of(i * d, d), d)
        mid[i] = (n * mg[:, vec] + mb[:, vec]).astype(BF)
        pl.when(j < 2)(lambda: mid_core(j).start())

    @pl.when(tick == F_A)
    def _():
        out_copy(1).wait()
        out_copy(2).wait()

    @pl.when((tick >= F_B1) & (tick < F_O))
    def _():
        i = tick - F_B1
        w = w_next(10 + i)
        e = dot(cotb[...], w[...], 1, 1)
        n = nmid[i].astype(F32)
        vec = pl.ds(pl.multiple_of(i * d, d), d)
        small[pl.ds(6 + i, 1), :] = colsum(e * n)
        small[pl.ds(6 + blocks + i, 1), :] = colsum(e)
        a = e * mg[:, vec]
        act[i] = a
        ta[...] += jnp.sum(a, axis=-1, keepdims=True)
        tb[...] += jnp.sum(a * n, axis=-1, keepdims=True)

    @pl.when(tick == F_A)
    def _():
        cot_core().wait_recv()
        mid_core(0).wait_recv()
        mid_core(1).wait_recv()

    @pl.when((tick >= F_A) & (tick < F_B1))
    def _():
        k = tick - F_A
        a_at = pl.ds(pl.multiple_of((k // 2) * h, h), h)
        b_at = pl.ds(pl.multiple_of(lax.rem(k, 2) * h, h), h)
        for far in (True, False):
            x = 1 - ctx if far else ctx
            v = dot(mid[2 * x + core, :, a_at], cotb[:, b_at], 0, 0) + dot(r_mid[x, :, a_at], r_cot[:, b_at], 0, 0)
            put_chunk(sendw if far else keepw, k, v.astype(BF))
            if far:
                for j in range(SUB):
                    c = SUB * k + j
                    pl.when(c < PRE)(lambda c=c: pre_copy(c).start())

    @pl.when(tick == F_O)
    def _():
        out_copy(9).start()
        out_copy(10).start()

    @pl.when((tick >= F_O) & (tick < F_B2))
    def _():
        i = tick - F_O
        w = w_next(14 + i)
        hid[...] += dot(mid[i], w[...], 1, 0)

    @pl.when(tick == F_B2 - 1)
    def _():
        qkvb[2] = hid[...].astype(BF)
        out_copy(8).start()

    @pl.when((tick >= F_B2) & (tick < F_END))
    def _():
        i = tick - F_B2
        w = w_next(18 + i)
        n = nmid[i].astype(F32)
        a = act[i] - ta[...] * (1.0 / width) - n * (tb[...] * (1.0 / width))
        gf = (a * smid[...] * gfb[i].astype(F32)).astype(BF)
        gfb[i] = gf
        v = dot(gf, w[...], 1, 1)

        @pl.when(i == 0)
        def _():
            acc[...] = v

        @pl.when(i > 0)
        def _():
            acc[...] += v

    @pl.when(tick == F_END - 1)
    def _():
        out_copy(11).start()
        e = acc[...]
        n = n2[...]
        small[2:3, :] = colsum(e * n)
        small[5:6, :] = colsum(e)
        gh = cotb[...].astype(F32) + ln_back(e, gain[2:3, :], n, s2[...])
        hid[...] = gh
        out_copy(7).start()
        n = n1[...]
        small[1:2, :] = colsum(gh * n)
        small[4:5, :] = colsum(gh)
        gp = ln_back(gh, gain[1:2, :], n, s1[...]).astype(BF)
        qkvb[0] = gp
        out_copy(5).start()
        qkvb[1] = dot(gp, wo[...], 1, 1).astype(BF)
        out_copy(6).start()
        for j in (0, 3, 4, 5, 6, 7, 8, 9, 10, 11):
            out_copy(j).wait()
        tok_copy().wait_send()
        cot_copy().wait_send()
        cot_core().wait_send()
        mid_core(0).wait_send()
        mid_core(1).wait_send()
        for k in range(PRE):
            pre_copy(k).wait()


def front_call(rows, cols, lengths, scale, gain, offset, mg, mb, tok, cot, wqkv, wo, w1, w2):
    seg, d = tok.shape[1:]
    t = 2 * seg
    ff = w1.shape[1]
    blocks = ff // d
    pairs = d // 128
    any_ = pl.BlockSpec(memory_space=pl.ANY)
    smem = pl.BlockSpec(memory_space=pltpu.SMEM)
    whole = lambda shape: pl.BlockSpec(shape, lambda i: (0,) * len(shape))
    vm = lambda *shape: pltpu.VMEM(shape, BF)
    vf = lambda *shape: pltpu.VMEM(shape, F32)
    dma = lambda n: pltpu.SemaphoreType.DMA((n,))
    small = (6 + 2 * blocks + 2, d)
    td = struct((t, d), BF)
    return pl.pallas_call(
        front_kernel,
        grid=(F_END,),
        in_specs=[smem, smem, whole((3, d)), whole((3, d)), whole((1, ff)), whole((1, ff))] + [any_] * 6,
        out_specs=[any_] * 4 + [whole((pairs, 2, t))] + [any_] * 9 + [whole(small)],
        out_shape=[
            td, td, struct((3, t, d), BF), td, struct((pairs, 2, t), F32), td, struct((blocks, t, d), BF), td, td,
            struct((t, d), F32), td, struct((4 * SUB, rows, cols), BF), struct((4 * SUB - PRE, rows, cols), BF),
            struct((PRE, rows, cols), BF), struct(small, F32),
        ],
        scratch_shapes=[
            vm(3, d, d), vm(d, d), vm(t, d), vm(t, d), vm(t, d), vm(3, t, d), vm(t, d), vf(t // QB, QB + REACH, 2 * QB),
            vf(blocks, t, d), vm(blocks, t, d), vm(blocks, t, d), vm(blocks, t, d), vm(2, t, d), vm(t, d),
            vf(t, d), vf(t, d), vf(t, d), vf(t, d), vm(t, d), vm(4 * SUB, rows, cols), vm(4 * SUB, rows, cols),
            vf(t, 1), vf(t, 1), vf(t, 1), vf(t, 1), vf(t, 1), dma(3), dma(3), dma(12), dma(5 + PRE), dma(5 + PRE),
        ],
        compiler_params=pltpu.CompilerParams(collective_id=1, has_side_effects=True, vmem_limit_bytes=60 * 2**20),
    )(lengths, scale, gain, offset, mg, mb, tok, cot, wqkv, wo, w1, w2)


def factors_of(n):
    out = []
    while n > 1:
        out.append(2)
        n //= 2
    return out


ATT_TICKS = (0, 1, 2, 4, 5, 7, 8, 10)
WG_TICKS = (3, 6, 9, 11, 12, 13, 14, 15)
T_IN, T_TAIL = 16, 22


def lags_of(n_rs):
    return (0,) + tuple(range(2, 2 * n_rs - 1)) + (2 * n_rs,)


T_OUT = 25


EVENT_TICKS = tuple(range(T_TAIL))
AHEAD = 16


def count_before(ticks, i):
    done = 0
    for at in sorted(set(ticks)):
        done = done + jnp.where(i > at, ticks.count(at), 0)
    return done


def event_ticks(n_events):
    more = n_events - len(EVENT_TICKS)
    return EVENT_TICKS + tuple(range(T_TAIL, T_TAIL + more))


def send_ticks(n_events):
    made = [0] * (4 * SUB - PRE)
    for at in WG_TICKS:
        made += [at] * SUB
    events = event_ticks(n_events)
    return tuple(max(at, events[max(PRE + j - AHEAD, 0)]) for j, at in enumerate(made))


def tick_count(n_events):
    return T_TAIL + max(n_events - len(EVENT_TICKS), 10)


def main_kernel(factors, lengths, scale, q, k, v, gs, sn, lse, wq, gain,
                h_sent, h_ffn, h_gf, h_gp, h_nrm, h_last, h_keep, h_pre, h_x, h_ghid, h_small, h_out,
                out, gx_own, gx_got, small_out, out_got, *scr):
    tick = pl.program_id(0)
    n_rs = len(factors)
    chunks, rows, cols = out.shape[0], out.shape[2], out.shape[3]
    t, d = h_sent.shape
    hd2 = d // 2
    me = lax.axis_index("rows")
    ctx = lax.axis_index("ctx")
    fs = [2] + factors[1:]
    strides, st = [0], 2
    for f in factors[1:]:
        strides.append(st)
        st *= f
    size = [rows]
    for f in fs[1:]:
        size.append(size[-1] // f)
    pos = [ctx] + [lax.rem(me // strides[i], fs[i]) for i in range(1, n_rs)]
    off = [0]
    for i in range(1, n_rs):
        off.append(off[-1] + pos[i] * size[i])
    bits = []
    b = 1
    while b < lax.axis_size("rows"):
        bits.append(b)
        b *= 2

    def peer(i, j):
        if i == 0:
            return (me, 1 - ctx)
        return (me + ((pos[i] ^ j) - pos[i]) * strides[i], ctx)

    core = lax.rem(me, 2)
    sibling = (me + 1 - 2 * core, ctx)
    other_ctx = (me, 1 - ctx)

    def bit_peer(b):
        return (me + b - 2 * b * lax.rem(me // b, 2), ctx)

    scr = list(scr)
    take = lambda n: [scr.pop(0) for _ in range(n)]
    sendb, acc, gath = take(3)
    recv = [gath] + take(n_rs - 1)
    small_acc, small_recv = take(2)
    o_sent, o_ffn, o_gf, o_gp, o_nrm = take(5)
    r_sent, r_ffn, r_gf, r_gp, r_nrm, r_gq = take(6)
    gall, bias, gk, gv, gqt, xb, gh, gn_acc, gx_send = take(9)
    rs_s, rs_r = take(n_rs), take(n_rs)
    ag_s, ag_r = [None] + take(n_rs - 1), [None] + take(n_rs - 1)
    core_s, core_r, loc, small_s, small_r, swap_s, swap_r, load, gx_s, gx_r = take(10)

    def part(at, n):
        return pl.ds(at if isinstance(at, int) else pl.multiple_of(at, 16), n)

    def rs_copy(i, c, j):
        if i == 0:
            src, dst = sendb.at[c - PRE], gath.at[c]
        else:
            src = acc.at[c, part(off[i - 1] + (pos[i] ^ j) * size[i], size[i])]
            dst = recv[i].at[c, j - 1]
        return remote(src, dst, rs_s[i].at[c, j - 1], rs_r[i].at[c, j - 1], peer(i, j))

    def ag_copy(i, c, j, arriving):
        at = off[i - 1] + (pos[i] ^ j) * size[i] if arriving else off[i]
        ref = gath.at[c, part(at, size[i])]
        return remote(ref, ref, ag_s[i].at[c, j - 1], ag_r[i].at[c, j - 1], peer(i, j))

    def core_copy(c, arriving):
        to = 1 - core if arriving else core
        return remote(gath.at[c], out.at[c, to], core_s.at[c], core_r.at[c], sibling)

    def own_copy(c):
        return pltpu.make_async_copy(gath.at[c], out.at[c, core], loc.at[c])

    def reduce_stage(i, c):
        if i == 0:
            @pl.when(c >= PRE)
            def _():
                rs_copy(0, c, 1).wait_recv()
        else:
            for j in range(1, fs[i]):
                rs_copy(i, c, j).wait_recv()
        here = part(off[i], size[i])
        val = acc[c, here].astype(F32)
        if i == 0:
            val = val + gath[c].astype(F32)
        else:
            for j in range(1, fs[i]):
                val = val + recv[i][c, j - 1].astype(F32)
        if i + 1 < n_rs:
            acc[c, here] = val.astype(BF)
            for j in range(1, fs[i + 1]):
                rs_copy(i + 1, c, j).start()
        else:
            gath[c, here] = val.astype(BF)
            for j in range(1, fs[i]):
                ag_copy(i, c, j, False).start()

    def gather_stage(i, c):
        for j in range(1, fs[i]):
            ag_copy(i, c, j, True).wait_recv()
        if i > 1:
            for j in range(1, fs[i - 1]):
                ag_copy(i - 1, c, j, False).start()
        else:
            core_copy(c, False).start()
            own_copy(c).start()

    def small_copy(i):
        to = other_ctx if i == 0 else bit_peer(bits[i - 1])
        return remote(small_acc.at[i], small_recv.at[i], small_s.at[i], small_r.at[i], to)

    mine = pl.ds(pl.multiple_of(core * hd2, hd2), hd2)
    theirs = pl.ds(pl.multiple_of((1 - core) * hd2, hd2), hd2)
    swaps = [(h_sent, r_sent), (h_gp.at[:, theirs], r_gp), (h_ffn, r_ffn), (h_gf.at[1 - core], r_gf.at[0]), (h_nrm, r_nrm),
             (h_gf.at[3 - core], r_gf.at[1])]
    loads = [(h_sent, o_sent), (h_gp.at[:, mine], o_gp), (h_ffn, o_ffn), (h_gf.at[core], o_gf.at[0]), (h_nrm, o_nrm),
             (h_x, xb), (h_ghid, gh), (h_small, small_acc.at[0]), (h_last, sendb.at[pl.ds(0, 4 * SUB - PRE)]),
             (h_keep, acc.at[pl.ds(0, 4 * SUB)]), (h_pre, gath.at[pl.ds(0, PRE)]), (h_gf.at[2 + core], o_gf.at[1])]

    def swap_copy(j):
        return remote(swaps[j][0], swaps[j][1], swap_s.at[j], swap_r.at[j], sibling)

    def gq_copy():
        return remote(gall.at[1 - core], r_gq, swap_s.at[6], swap_r.at[6], sibling)

    def load_copy(j):
        return pltpu.make_async_copy(loads[j][0], loads[j][1], load.at[j])

    seg = t // 2

    def rows_of(c):
        return pl.ds(pl.multiple_of(c * seg, seg), seg)

    def gx_copy():
        return remote(gx_send, gx_got, gx_s.at[0], gx_r.at[0], other_ctx)

    def out_copy():
        return remote(h_out.at[rows_of(1 - ctx)], out_got, gx_s.at[1], gx_r.at[1], other_ctx)

    @pl.when(tick == 0)
    def _():
        peers = [other_ctx, sibling]
        for i in range(1, n_rs):
            peers += [peer(i, j) for j in range(1, fs[i])]
        barrier = pltpu.get_barrier_semaphore()
        for p in peers:
            pl.semaphore_signal(barrier, inc=1, device_id=p, device_id_type=MESH)
        for j in (10, 9, 8, 0, 1, 2, 3, 11, 4, 5, 6, 7):
            load_copy(j).start()
        pl.semaphore_wait(barrier, len(peers))
        for j in (0, 1, 2, 3, 5, 4):
            swap_copy(j).start()
        for j in (10, 9, 8):
            load_copy(j).wait()
        at = lax.broadcasted_iota(jnp.int32, (1, t), 1)
        start = jnp.zeros((1, t), jnp.int32)
        bound = jnp.int32(0)
        for i in range(lengths.shape[1]):
            bound = bound + lengths[ctx, i]
            start = jnp.where(at >= bound, bound, start)
        fill_bias(start, bias, t)
        load_copy(7).wait()

    pair = count_before(ATT_TICKS, tick)

    @pl.when(count_before(ATT_TICKS, tick + 1) > pair)
    def _():
        hd = q.shape[2] // 2
        kt = k[0].astype(F32).T.astype(BF)
        gsf = gs[...].astype(F32)
        prod = (gsf * sn[...].astype(F32)).T
        d0 = jnp.sum(prod[0:hd], axis=0, keepdims=True)
        d1 = jnp.sum(prod[hd:], axis=0, keepdims=True)
        lane = lax.broadcasted_iota(jnp.int32, (1, d), 1)
        h0 = jnp.sum(d0, axis=-1, keepdims=True)
        h1 = jnp.sum(d1, axis=-1, keepdims=True)
        small_acc[0, 14:15, :] += (
            jnp.where(lane == 2 * pair, h0 / scale[2 * pair], 0.0)
            + jnp.where(lane == 2 * pair + 1, h1 / scale[2 * pair + 1], 0.0)
        )
        ga = (gsf * head_lanes(scale, pair, (1, 2 * hd), hd)).astype(BF)
        gk[...] = jnp.zeros_like(gk)
        gv[...] = jnp.zeros_like(gv)
        for i in range(t // QB):
            k0, k1 = key_range(i)
            qs = slice(i * QB, (i + 1) * QB)
            qm = (both_heads(q[0, qs, :], hd) * (hd**-0.5)).astype(BF)
            gm = both_heads(ga[qs, :], hd)
            sc = dot(k[0, k0:k1, :], qm, 1, 1) + bias[i, 0 : k1 - k0, :]
            ls = jnp.concatenate([lse[0, 0:1, qs], lse[0, 1:2, qs]], axis=1)
            dd = jnp.concatenate([d0[:, qs], d1[:, qs]], axis=1)
            pt = jnp.exp(sc - ls)
            gp = dot(v[0, k0:k1, :], gm, 1, 1)
            ds = (pt * (gp - dd)).astype(BF)
            gv[k0:k1, :] += dot(pt.astype(BF), gm, 1, 0)
            gk[k0:k1, :] += dot(ds, qm, 1, 0)
            gq = dot(kt[:, k0:k1], ds, 1, 0) * (hd**-0.5)
            gqt[:, qs] = jnp.concatenate([gq[0:hd, 0:QB], gq[hd:, QB:]], axis=0)
        per_core = len(ATT_TICKS) // 2
        half = pair // per_core
        at = pl.ds(pl.multiple_of(lax.rem(pair, per_core) * 128, 128), 128)
        gall[half, 0, :, at] = gqt[...].T.astype(BF)
        gall[half, 1, :, at] = gk[...].astype(BF)
        gall[half, 2, :, at] = gv[...].astype(BF)

    @pl.when(tick == ATT_TICKS[-1])
    def _():
        gq_copy().start()

    def wgrad(c, a0, a1, b0, b1):
        for far in (True, False):
            x = 1 - ctx if far else ctx
            val = (dot(a0(x), b0, 0, 0) + dot(a1(x), b1, 0, 0)).astype(BF)
            put_chunk(sendb if far else acc, c - PRE // SUB if far else c, val)

    def half_of(ref):
        return lambda x: ref[:, pl.ds(pl.multiple_of(x * hd2, 128), hd2)]

    @pl.when(tick == T_OUT)
    def _():
        out_copy().start()
        gx_copy().start()

    @pl.when(tick == WG_TICKS[0])
    def _():
        for j in (0, 1):
            load_copy(j).wait()
            swap_copy(j).wait_recv()
        wgrad(4, half_of(o_sent), half_of(r_sent), o_gp[...], r_gp[...])

    @pl.when(tick == WG_TICKS[1])
    def _():
        for j in (2, 3):
            load_copy(j).wait()
            swap_copy(j).wait_recv()
        load_copy(11).wait()
        swap_copy(5).wait_recv()

    block = count_before(WG_TICKS, tick)
    makes = count_before(WG_TICKS, tick + 1) > block

    @pl.when(makes & (block >= 1) & (block < 5))
    def _():
        c = block - 1
        b = lambda ref: ref[c // 2, :, pl.ds(pl.multiple_of(lax.rem(c, 2) * hd2, 128), hd2)]
        wgrad(c + 5, half_of(o_ffn), half_of(r_ffn), b(o_gf), b(r_gf))

    @pl.when(tick == WG_TICKS[5])
    def _():
        load_copy(4).wait()
        swap_copy(4).wait_recv()
        gq_copy().wait_recv()

    @pl.when(makes & (block >= 5))
    def _():
        c = block - 5
        wgrad(c + 9, half_of(o_nrm), half_of(r_nrm), gall[core, c], r_gq[c])

    @pl.when((tick >= T_IN) & (tick < T_TAIL))
    def _():
        j = tick - T_IN
        val = dot(gall[lax.rem(j, 2), j // 2], wq[...], 1, 1)

        @pl.when(j == 0)
        def _():
            gn_acc[...] = val

        @pl.when(j > 0)
        def _():
            gn_acc[...] += val

    @pl.when(tick == T_TAIL - 1)
    def _():
        load_copy(5).wait()
        load_copy(6).wait()
        e = gn_acc[...]
        n, inv = ln_stats(xb[...].astype(F32))
        small_acc[0, 0:1, :] = colsum(e * n)
        small_acc[0, 3:4, :] = colsum(e)
        gh[...] += ln_back(e, gain[0:1, :], n, inv)
        gx_send[...] = gh[rows_of(1 - ctx), :].astype(BF)
        gx_own[...] = gh[rows_of(ctx), :]
        small_copy(0).start()

    def guarded(f, i, c):
        pl.when((c >= 0) & (c < chunks))(lambda: f(i, c))

    lanes = [(reduce_stage, i) for i in range(n_rs)] + [(gather_stage, i) for i in range(n_rs - 1, 0, -1)]

    lags = lags_of(n_rs)
    n_events = chunks + lags[-1]
    sends = send_ticks(n_events)

    def send(c, _):
        rs_copy(0, c, 1).start()
        return 0

    lax.fori_loop(PRE + count_before(sends, tick), PRE + count_before(sends, tick + 1), send, 0)
    events = event_ticks(n_events)
    event = count_before(events, tick)

    @pl.when(count_before(events, tick + 1) > event)
    def _():
        for lag in range(len(lanes) - 1, -1, -1):
            f, i = lanes[lag]
            guarded(f, i, event - lags[lag])

    for i in range(len(bits) + 1):

        @pl.when(tick == T_TAIL + 1 + i)
        def _(i=i):
            small_copy(i).wait_recv()
            if i < len(bits):
                small_acc[i + 1] = small_acc[i] + small_recv[i]
                small_copy(i + 1).start()
            else:
                small_out[...] = small_acc[i] + small_recv[i]

    @pl.when(tick == pl.num_programs(0) - 1)
    def _():
        def finish(c, _):
            for i in range(n_rs):
                for j in range(1, fs[i]):
                    if i == 0:
                        @pl.when(c >= PRE)
                        def _():
                            rs_copy(0, c, 1).wait_send()
                    else:
                        rs_copy(i, c, j).wait_send()
                        ag_copy(i, c, j, False).wait_send()
            core_copy(c, False).wait_send()
            core_copy(c, True).wait_recv()
            own_copy(c).wait()
            return 0

        lax.fori_loop(0, chunks, finish, 0)
        for i in range(len(bits) + 1):
            small_copy(i).wait_send()
        for j in range(6):
            swap_copy(j).wait_send()
        gq_copy().wait_send()
        gx_copy().wait()
        out_copy().wait()


def main_call(factors, rows, cols, lengths, scale, qkv, gsent, sent, lse, w_qkv, gain, ffn_in, gf, gp, normed, last,
              keep, pre, x, ghid, small, out):
    t, d = sent.shape
    h = d // 2
    n = 1
    for f in factors:
        n *= f
    fs = [2] + factors[1:]
    levels = 1
    while n > 1:
        levels += 1
        n //= 2
    size, recv = rows, []
    for f in fs[1:]:
        size //= f
        recv.append(pltpu.VMEM((CHUNKS, f - 1, size, cols), BF))
    dma = lambda *shape: pltpu.SemaphoreType.DMA(shape)
    per = lambda k: [dma(CHUNKS, f - 1) for f in fs[k:]]
    vm = lambda *shape: pltpu.VMEM(shape, BF)
    vf = lambda *shape: pltpu.VMEM(shape, F32)
    pair = lambda i: jnp.minimum(count_before(ATT_TICKS, i), len(ATT_TICKS) - 1)
    part = lambda j: pl.BlockSpec((1, t, 128), lambda i: (j, 0, pair(i)))
    flat = pl.BlockSpec((t, 128), lambda i: (0, pair(i)))
    whole = lambda shape: pl.BlockSpec(shape, lambda i: (0,) * len(shape))
    wcol = lambda i: jnp.clip(i - T_IN, 0, 5)
    any_ = pl.BlockSpec(memory_space=pl.ANY)
    events = CHUNKS + lags_of(len(fs))[-1]
    return pl.pallas_call(
        functools.partial(main_kernel, factors),
        grid=(tick_count(events),),
        in_specs=[
            pl.BlockSpec(memory_space=pltpu.SMEM), pl.BlockSpec(memory_space=pltpu.SMEM),
            part(0), part(1), part(2), flat, flat,
            pl.BlockSpec((1, 2, t), lambda i: (pair(i), 0, 0)),
            pl.BlockSpec((d, h), lambda i: (0, wcol(i))),
            whole((3, d)),
        ] + [any_] * 12,
        out_specs=[any_, whole((t // 2, d)), any_, whole(small.shape), any_],
        out_shape=[
            struct((CHUNKS, 2, rows, cols), BF), struct((t // 2, d), F32), struct((t // 2, d), BF), struct(small.shape, F32),
            struct((t // 2, d), BF),
        ],
        scratch_shapes=[vm(CHUNKS - PRE, rows, cols), vm(CHUNKS, rows, cols), vm(CHUNKS, rows, cols)]
        + recv
        + [vf(levels, *small.shape)] * 2
        + [vm(t, d), vm(t, d), vm(2, t, d), vm(t, h), vm(t, d)]
        + [vm(t, d), vm(t, d), vm(2, t, d), vm(t, h), vm(t, d), vm(3, t, h)]
        + [vm(2, 3, t, h), vf(t // QB, QB + REACH, 2 * QB), vf(t, 128), vf(t, 128), vf(128, t), vm(t, d), vf(t, d), vf(t, d),
           vm(t // 2, d)]
        + per(0) + per(0) + per(1) + per(1)
        + [dma(CHUNKS), dma(CHUNKS), dma(CHUNKS), dma(levels), dma(levels), dma(7), dma(7), dma(12), dma(2), dma(2)],
        compiler_params=pltpu.CompilerParams(collective_id=0, has_side_effects=True, vmem_limit_bytes=60 * 2**20),
    )(lengths, scale, qkv, qkv, qkv, gsent, sent, lse, w_qkv, gain,
      sent, ffn_in, gf, gp, normed, last, keep, pre, x, ghid, small, out)


SLOTS = 8


def finish_kernel(small, got, gx_own, gx_got, own, away, out, gx, g2, g1, go, gq, gn, bn, gmg, gmb, ghs,
                  inb, outb, low, wide, isem, osem, sems):
    ctx = lax.axis_index("ctx")
    seg, d = gx_own.shape
    h = d // 2
    c = got.shape[3]
    blocks = (small.shape[0] - 8) // 2

    def copy(src, dst, j):
        return pltpu.make_async_copy(src, dst, sems.at[j])

    ins = [
        copy(gx_got, low.at[0], 0),
        copy(own.at[pl.ds(pl.multiple_of(ctx * seg, seg), seg)], low.at[1], 1),
        copy(away, low.at[2], 2),
        copy(gx_own, wide.at[1], 3),
    ]
    outs = [
        copy(wide.at[0], gx.at[1 - ctx], 4),
        copy(low.at[1], out.at[ctx], 5),
        copy(low.at[2], out.at[1 - ctx], 6),
        copy(wide.at[1], gx.at[ctx], 7),
    ]

    def place(i):
        k, core = i // 2, i % 2
        if k < 4:
            ref, r, col = g2, core * 2 + k // 2, k % 2
        elif k == 4:
            ref, r, col = go, 0, core
        elif k < 9:
            ref, r, col = g1, 0, (((k - 5) // 2) * 2 + core) * 2 + (k - 5) % 2
        else:
            ref, r, col = gq, 0, (k - 9) * 2 + core
        return ref.at[pl.ds(r * h, h), pl.ds(col * h, h)]

    def load(i):
        src = got.at[pl.ds(i // 2 * SUB, SUB), i % 2]
        return pltpu.make_async_copy(src, inb.at[i % SLOTS], isem.at[i % SLOTS])

    def store(i):
        return pltpu.make_async_copy(outb.at[i % SLOTS], place(i), osem.at[i % SLOTS])

    count = 2 * BLOCKS
    for i in range(SLOTS):
        load(i).start()
    for v in ins:
        v.start()
    half = pl.ds(pl.multiple_of(ctx * h, h), h)
    gn[...] = small[0:3, half]
    bn[...] = small[3:6, half]
    for j in range(blocks // 2):
        at = slice(j * d, (j + 1) * d)
        gmg[:, at] = small[pl.ds(6 + ctx * (blocks // 2) + j, 1), :]
        gmb[:, at] = small[pl.ds(6 + blocks + ctx * (blocks // 2) + j, 1), :]
    n = ghs.shape[1]
    row = small[6 + 2 * blocks : 7 + 2 * blocks, :]
    ghs[...] = jnp.where(ctx == 0, row[:, 0:n], row[:, n : 2 * n])
    for i in range(count):
        load(i).wait()
        if i >= SLOTS:
            store(i - SLOTS).wait()
        groups = h // c // SUB
        for j in range(SUB):
            for m in range(groups):
                at = (j * groups + m) * c
                outb[i % SLOTS, :, at : at + c] = inb[i % SLOTS, j, m * h : (m + 1) * h, :].astype(F32)
        store(i).start()
        if i + SLOTS < count:
            load(i + SLOTS).start()
        if i == SLOTS:
            for j in range(4):
                ins[j].wait()
                if j == 0:
                    wide[0] = low[0].astype(F32)
                outs[j].start()
    for i in range(count - SLOTS, count):
        store(i).wait()
    for v in outs:
        v.wait()


def finish_call(small, got, gx_own, gx_got, own, away, ff, heads):
    seg, d = gx_own.shape
    h = d // 2
    rows, cols = got.shape[2:]
    any_ = pl.BlockSpec(memory_space=pl.ANY)
    vmem = pl.BlockSpec(memory_space=pltpu.VMEM)
    dma = lambda n: pltpu.SemaphoreType.DMA((n,))
    return pl.pallas_call(
        finish_kernel,
        in_specs=[vmem] + [any_] * 5,
        out_specs=[any_] * 6 + [vmem] * 5,
        out_shape=[
            struct((2, seg, d), BF), struct((2, seg, d), F32), struct((ff // 2, d), F32), struct((h, ff), F32),
            struct((h, d), F32), struct((h, 3 * d), F32), struct((3, h), F32), struct((3, h), F32),
            struct((1, ff // 2), F32), struct((1, ff // 2), F32), struct((1, heads // 2), F32),
        ],
        scratch_shapes=[
            pltpu.VMEM((SLOTS, SUB, rows, cols), BF), pltpu.VMEM((SLOTS, h, h), F32),
            pltpu.VMEM((3, seg, d), BF), pltpu.VMEM((2, seg, d), F32), dma(SLOTS), dma(SLOTS), dma(8),
        ],
        compiler_params=pltpu.CompilerParams(vmem_limit_bytes=60 * 2**20),
    )(small, got, gx_own, gx_got, own, away)


def local(
    tokens, cotangent, w_qkv, w_out, w_fc1, w_fc2, norm_gain, norm_bias, mid_gain, mid_bias, head_scale, doc_lengths
):
    n = lax.axis_size("rows")
    factors = factors_of(n)
    d = tokens.shape[2]
    ff = w_fc1.shape[1]
    heads = head_scale.shape[0]
    mg, mb = mid_gain[None, :], mid_bias[None, :]
    pieces = 1
    for f in factors[1:]:
        pieces *= f
    half = d // 2
    rows = max(half, 16 * pieces)
    cols = half * half // rows // SUB
    x, normed, qkv, sent, lse, ffn_in, gf, gp, gsent, ghid, out, keep, last, pre, small = front_call(
        rows, cols, doc_lengths, head_scale, norm_gain, norm_bias, mg, mb, tokens, cotangent, w_qkv, w_out, w_fc1, w_fc2
    )
    got, gx_own, gx_got, small, out_got = main_call(
        factors, rows, cols, doc_lengths, head_scale, qkv, gsent, sent, lse, w_qkv, norm_gain, ffn_in, gf, gp, normed, last,
        keep, pre, x, ghid, small, out,
    )
    out, gx, g2, g1, go, gq, gn, bn, gmg, gmb, ghs = finish_call(small, got, gx_own, gx_got, out, out_got, ff, heads)
    return (out, gx, gq, go, g1, g2, gn, bn, gmg.reshape(-1), gmb.reshape(-1), ghs.reshape(-1))


def solution(mesh):
    rows = P("rows", "ctx", None)
    in_specs = (rows, rows) + (P(),) * 9 + (P("rows", None),)
    ctx0 = P("ctx", None)
    out_specs = (rows, rows, ctx0, ctx0, ctx0, ctx0, P(None, "ctx"), P(None, "ctx"), P("ctx"), P("ctx"), P("ctx"))
    return jax.shard_map(local, mesh=mesh, in_specs=in_specs, out_specs=out_specs, check_vma=False)
```

```python
import functools

import jax
import jax.numpy as jnp
from jax import lax
from jax.experimental import pallas as pl
from jax.experimental.pallas import tpu as pltpu
from jax.sharding import PartitionSpec as P

EPS = 1e-05
MASKED = -1e30
BF = jnp.bfloat16
F32 = jnp.float32
REACH = 256
QB = 128


def dot(a, b, ca, cb):
    return lax.dot_general(a, b, (((ca,), (cb,)), ((), ())), preferred_element_type=F32)


def ln_stats(v):
    mean = jnp.mean(v, axis=-1, keepdims=True)
    cen = v - mean
    inv = lax.rsqrt(jnp.mean(cen * cen, axis=-1, keepdims=True) + EPS)
    return cen * inv, inv


def ln_back(e, gain, n, inv):
    a = e * gain
    return inv * (
        a - jnp.mean(a, axis=-1, keepdims=True) - n * jnp.mean(a * n, axis=-1, keepdims=True)
    )


def colsum(v):
    return jnp.sum(v, axis=0, keepdims=True)


def struct(shape, dtype):
    return jax.ShapeDtypeStruct(shape, dtype)


def key_range(i):
    return max(0, i * QB - REACH), (i + 1) * QB


def fill_bias(start, bias, t):
    for i in range(t // QB):
        k0, k1 = key_range(i)
        u = lax.broadcasted_iota(jnp.int32, (k1 - k0, QB), 0) + k0
        q = lax.broadcasted_iota(jnp.int32, (k1 - k0, QB), 1) + i * QB
        first = start[:, i * QB : (i + 1) * QB]
        ok = (u >= first) & (u <= q)
        one = jnp.where(ok, 0.0, MASKED).astype(F32)
        bias[i, 0 : k1 - k0, 0:QB] = one
        bias[i, 0 : k1 - k0, QB : 2 * QB] = one


def both_heads(v, hd):
    lane = lax.broadcasted_iota(jnp.int32, v.shape, 1)
    zero = jnp.zeros_like(v)
    return jnp.concatenate([jnp.where(lane < hd, v, zero), jnp.where(lane < hd, zero, v)], axis=0)


def put_chunk(ref, k, v):
    h, c = v.shape[0], ref.shape[2]
    groups = ref.shape[1] // h
    for j in range(SUB):
        for m in range(groups):
            at = (j * groups + m) * c
            ref[SUB * k + j, m * h : (m + 1) * h, :] = v[:, at : at + c]


BLOCKS = 12
SUB = 2
CHUNKS = BLOCKS * SUB
PRE = 2 * SUB
F_Q1, F_Q2, F_AT, F_FC, F_NM, F_A, F_B1, F_O, F_B2, F_END = 0, 3, 6, 10, 14, 18, 22, 26, 30, 34
MESH = pl.DeviceIdType.MESH


def remote(src, dst, ss, rs, to):
    return pltpu.make_async_remote_copy(src, dst, ss, rs, device_id=to, device_id_type=MESH)


def head_lanes(scale, pair, shape, hd):
    lane = lax.broadcasted_iota(jnp.int32, shape, 1)
    return jnp.where(lane < hd, scale[2 * pair], scale[2 * pair + 1])


def front_kernel(lengths, scale, gain, offset, mg, mb, h_tok, h_cot, h_wqkv, h_wo, h_w1, h_w2,
                 o_x, o_nrm, o_qkv, o_sent, lse, o_ffn, o_gf, o_gp, o_gs, o_gh, o_out, o_keep, o_last, pre, small,
                 wb, wo, xb, cotb, nrm, qkvb, sent, bias, act, mid, nmid, gfb, r_mid, r_cot, n1, n2, hid, acc, ffn,
                 sendw, keepw, s1, s2, smid, ta, tb, wsem, lsem, osem, ss, rs):
    tick = pl.program_id(0)
    me = lax.axis_index("rows")
    ctx = lax.axis_index("ctx")
    core = lax.rem(me, 2)
    sibling = (me + 1 - 2 * core, ctx)
    other_ctx = (me, 1 - ctx)
    t, d = xb.shape
    seg = t // 2
    blocks = act.shape[0]
    width = blocks * act.shape[2]
    h = d // 2

    def rows_of(c):
        return pl.ds(pl.multiple_of(c * seg, seg), seg)

    def w_copy(ref, i):
        return pltpu.make_async_copy(ref, wb.at[lax.rem(i, 3)], wsem.at[lax.rem(i, 3)])

    def col(ref, i):
        return ref.at[:, pl.ds(pl.multiple_of(i * d, d), d)]

    def row(ref, i):
        return ref.at[pl.ds(pl.multiple_of(i * d, d), d), :]

    def w_start(i):
        pl.when(i < 6)(lambda: w_copy(col(h_wqkv, lax.rem(i, 3)), i).start())
        pl.when((i >= 6) & (i < 10))(lambda: w_copy(col(h_w1, i - 6), i).start())
        pl.when((i >= 10) & (i < 18))(lambda: w_copy(row(h_w2, lax.rem(i - 10, 4)), i).start())
        pl.when((i >= 18) & (i < 22))(lambda: w_copy(col(h_w1, i - 18), i).start())

    def w_next(i):
        w_copy(row(h_w2, 0), i).wait()
        w_start(i + 2)
        return wb.at[lax.rem(i, 3)]

    def tok_copy():
        return remote(h_tok.at[1 - ctx], xb.at[rows_of(ctx)], ss.at[0], rs.at[0], other_ctx)

    def cot_copy():
        return remote(h_cot.at[1 - ctx], cotb.at[rows_of(ctx)], ss.at[1], rs.at[1], other_ctx)

    def cot_core():
        return remote(cotb, r_cot, ss.at[2], rs.at[2], sibling)

    def mid_core(i):
        return remote(mid.at[2 * i + 1 - core], r_mid.at[i], ss.at[3 + i], rs.at[3 + i], sibling)

    def pre_copy(k):
        return remote(sendw.at[k], pre.at[k], ss.at[5 + k], rs.at[5 + k], other_ctx)

    def load_copy(j):
        src, dst = [(h_tok.at[ctx], xb.at[rows_of(ctx)]), (h_cot.at[ctx], cotb.at[rows_of(ctx)]), (h_wo, wo)][j]
        return pltpu.make_async_copy(src, dst, lsem.at[j])

    outs = [(xb, o_x), (nrm, o_nrm), (qkvb, o_qkv), (sent, o_sent), (ffn, o_ffn), (qkvb.at[0], o_gp), (qkvb.at[1], o_gs),
            (hid, o_gh), (qkvb.at[2], o_out), (keepw, o_keep), (sendw.at[pl.ds(PRE, 4 * SUB - PRE)], o_last), (gfb, o_gf)]

    def out_copy(j):
        return pltpu.make_async_copy(outs[j][0], outs[j][1], osem.at[j])

    @pl.when(tick == 0)
    def _():
        barrier = pltpu.get_barrier_semaphore()
        for p in (other_ctx, sibling):
            pl.semaphore_signal(barrier, inc=1, device_id=p, device_id_type=MESH)
        load_copy(0).start()
        w_start(0)
        w_start(1)
        load_copy(1).start()
        load_copy(2).start()
        pl.semaphore_wait(barrier, 2)
        tok_copy().start()
        small[...] = jnp.zeros_like(small)
        at = lax.broadcasted_iota(jnp.int32, (1, t), 1)
        start = jnp.zeros((1, t), jnp.int32)
        bound = jnp.int32(0)
        for i in range(lengths.shape[1]):
            bound = bound + lengths[ctx, i]
            start = jnp.where(at >= bound, bound, start)
        fill_bias(start, bias, t)
        load_copy(0).wait()

    @pl.when(tick == F_Q2)
    def _():
        tok_copy().wait_recv()
        cot_copy().start()
        out_copy(0).start()

    for own in (True, False):
        first = F_Q1 if own else F_Q2
        here = rows_of(ctx if own else 1 - ctx)

        @pl.when(tick == first)
        def _(here=here):
            n, _ = ln_stats(xb[here, :].astype(F32))
            nrm[here, :] = (n * gain[0:1, :] + offset[0:1, :]).astype(BF)

        @pl.when((tick >= first) & (tick < first + 3))
        def _(here=here, first=first):
            w = w_next(tick)
            qkvb[tick - first, here, :] = dot(nrm[here, :], w[...], 1, 0).astype(BF)

    @pl.when(tick == F_AT)
    def _():
        out_copy(1).start()
        out_copy(2).start()

    @pl.when((tick >= F_AT) & (tick < F_FC))
    def _():
        hd = 64
        for pair in (2 * (tick - F_AT), 2 * (tick - F_AT) + 1):
            at = pl.ds(pl.multiple_of(pair * 128, 128), 128)
            vt = qkvb[2, :, at].astype(F32).T.astype(BF)
            sc = head_lanes(scale, pair, (1, 128), hd)
            for i in range(t // QB):
                k0, k1 = key_range(i)
                qs = slice(i * QB, (i + 1) * QB)
                qm = (both_heads(qkvb[0, qs, at], hd) * (hd**-0.5)).astype(BF)
                st = dot(qkvb[1, k0:k1, at], qm, 1, 1) + bias[i, 0 : k1 - k0, :]
                top = jnp.max(st, axis=0, keepdims=True)
                pt = jnp.exp(st - top)
                total = jnp.sum(pt, axis=0, keepdims=True)
                ot = dot(vt[:, k0:k1], pt.astype(BF), 1, 0) * (1.0 / total)
                o = jnp.concatenate([ot[0:hd, 0:QB], ot[hd:, QB:]], axis=0).T
                sent[qs, at] = (o * sc).astype(BF)
                ls = top + jnp.log(total)
                lse[pair, 0:1, qs] = ls[:, 0:QB]
                lse[pair, 1:2, qs] = ls[:, QB:]

    @pl.when(tick == F_FC)
    def _():
        out_copy(3).start()
        cot_copy().wait_recv()
        load_copy(1).wait()
        cot_core().start()
        load_copy(2).wait()
        n, inv = ln_stats(dot(sent[...], wo[...], 1, 0))
        n1[...] = n
        s1[...] = inv
        hidden = xb[...].astype(F32) + n * gain[1:2, :] + offset[1:2, :]
        hid[...] = hidden
        n, inv = ln_stats(hidden)
        n2[...] = n
        s2[...] = inv
        ffn[...] = (n * gain[2:3, :] + offset[2:3, :]).astype(BF)
        ta[...] = jnp.zeros_like(ta)
        out_copy(4).start()

    @pl.when((tick >= F_FC) & (tick < F_NM))
    def _():
        i = tick - F_FC
        w = w_next(6 + i)
        f = dot(ffn[...], w[...], 1, 0)
        phi = 0.5 + 0.5 * lax.erf(f * (0.5**0.5))
        a = f * phi
        gfb[i] = (phi + f * (jnp.exp(-0.5 * f * f) * 0.3989422804014327)).astype(BF)
        act[i] = a
        ta[...] += jnp.sum(a, axis=-1, keepdims=True)

    @pl.when(tick == F_NM)
    def _():
        mean = ta[...] * (1.0 / width)
        sq = jnp.zeros_like(mean)
        for j in range(blocks):
            c = act[j] - mean
            act[j] = c
            sq += jnp.sum(c * c, axis=-1, keepdims=True)
        smid[...] = lax.rsqrt(sq * (1.0 / width) + EPS)
        ta[...] = jnp.zeros_like(ta)
        tb[...] = jnp.zeros_like(tb)

    @pl.when((tick >= F_NM) & (tick < F_B1))
    def _():
        j = tick - F_NM
        i = lax.rem(j, 2) * 2 + jnp.where(j < 2, 1 - core, core)
        n = act[i] * smid[...]
        nmid[i] = n.astype(BF)
        vec = pl.ds(pl.multiple_of(i * d, d), d)
        mid[i] = (n * mg[:, vec] + mb[:, vec]).astype(BF)
        pl.when(j < 2)(lambda: mid_core(j).start())

    @pl.when(tick == F_A)
    def _():
        out_copy(1).wait()
        out_copy(2).wait()

    @pl.when((tick >= F_B1) & (tick < F_O))
    def _():
        i = tick - F_B1
        w = w_next(10 + i)
        e = dot(cotb[...], w[...], 1, 1)
        n = nmid[i].astype(F32)
        vec = pl.ds(pl.multiple_of(i * d, d), d)
        small[pl.ds(6 + i, 1), :] = colsum(e * n)
        small[pl.ds(6 + blocks + i, 1), :] = colsum(e)
        a = e * mg[:, vec]
        act[i] = a
        ta[...] += jnp.sum(a, axis=-1, keepdims=True)
        tb[...] += jnp.sum(a * n, axis=-1, keepdims=True)

    @pl.when(tick == F_A)
    def _():
        cot_core().wait_recv()
        mid_core(0).wait_recv()
        mid_core(1).wait_recv()

    @pl.when((tick >= F_A) & (tick < F_B1))
    def _():
        k = tick - F_A
        a_at = pl.ds(pl.multiple_of((k // 2) * h, h), h)
        b_at = pl.ds(pl.multiple_of(lax.rem(k, 2) * h, h), h)
        for far in (True, False):
            x = 1 - ctx if far else ctx
            v = dot(mid[2 * x + core, :, a_at], cotb[:, b_at], 0, 0) + dot(r_mid[x, :, a_at], r_cot[:, b_at], 0, 0)
            put_chunk(sendw if far else keepw, k, v.astype(BF))
            if far:
                for j in range(SUB):
                    c = SUB * k + j
                    pl.when(c < PRE)(lambda c=c: pre_copy(c).start())

    @pl.when(tick == F_O)
    def _():
        out_copy(9).start()
        out_copy(10).start()

    @pl.when((tick >= F_O) & (tick < F_B2))
    def _():
        i = tick - F_O
        w = w_next(14 + i)
        hid[...] += dot(mid[i], w[...], 1, 0)

    @pl.when(tick == F_B2 - 1)
    def _():
        qkvb[2] = hid[...].astype(BF)
        out_copy(8).start()

    @pl.when((tick >= F_B2) & (tick < F_END))
    def _():
        i = tick - F_B2
        w = w_next(18 + i)
        n = nmid[i].astype(F32)
        a = act[i] - ta[...] * (1.0 / width) - n * (tb[...] * (1.0 / width))
        gf = (a * smid[...] * gfb[i].astype(F32)).astype(BF)
        gfb[i] = gf
        v = dot(gf, w[...], 1, 1)

        @pl.when(i == 0)
        def _():
            acc[...] = v

        @pl.when(i > 0)
        def _():
            acc[...] += v

    @pl.when(tick == F_END - 1)
    def _():
        out_copy(11).start()
        e = acc[...]
        n = n2[...]
        small[2:3, :] = colsum(e * n)
        small[5:6, :] = colsum(e)
        gh = cotb[...].astype(F32) + ln_back(e, gain[2:3, :], n, s2[...])
        hid[...] = gh
        out_copy(7).start()
        n = n1[...]
        small[1:2, :] = colsum(gh * n)
        small[4:5, :] = colsum(gh)
        gp = ln_back(gh, gain[1:2, :], n, s1[...]).astype(BF)
        qkvb[0] = gp
        out_copy(5).start()
        qkvb[1] = dot(gp, wo[...], 1, 1).astype(BF)
        out_copy(6).start()
        for j in (0, 3, 4, 5, 6, 7, 8, 9, 10, 11):
            out_copy(j).wait()
        tok_copy().wait_send()
        cot_copy().wait_send()
        cot_core().wait_send()
        mid_core(0).wait_send()
        mid_core(1).wait_send()
        for k in range(PRE):
            pre_copy(k).wait()


def front_call(rows, cols, lengths, scale, gain, offset, mg, mb, tok, cot, wqkv, wo, w1, w2):
    seg, d = tok.shape[1:]
    t = 2 * seg
    ff = w1.shape[1]
    blocks = ff // d
    pairs = d // 128
    any_ = pl.BlockSpec(memory_space=pl.ANY)
    smem = pl.BlockSpec(memory_space=pltpu.SMEM)
    whole = lambda shape: pl.BlockSpec(shape, lambda i: (0,) * len(shape))
    vm = lambda *shape: pltpu.VMEM(shape, BF)
    vf = lambda *shape: pltpu.VMEM(shape, F32)
    dma = lambda n: pltpu.SemaphoreType.DMA((n,))
    small = (6 + 2 * blocks + 2, d)
    td = struct((t, d), BF)
    return pl.pallas_call(
        front_kernel,
        grid=(F_END,),
        in_specs=[smem, smem, whole((3, d)), whole((3, d)), whole((1, ff)), whole((1, ff))] + [any_] * 6,
        out_specs=[any_] * 4 + [whole((pairs, 2, t))] + [any_] * 9 + [whole(small)],
        out_shape=[
            td, td, struct((3, t, d), BF), td, struct((pairs, 2, t), F32), td, struct((blocks, t, d), BF), td, td,
            struct((t, d), F32), td, struct((4 * SUB, rows, cols), BF), struct((4 * SUB - PRE, rows, cols), BF),
            struct((PRE, rows, cols), BF), struct(small, F32),
        ],
        scratch_shapes=[
            vm(3, d, d), vm(d, d), vm(t, d), vm(t, d), vm(t, d), vm(3, t, d), vm(t, d), vf(t // QB, QB + REACH, 2 * QB),
            vf(blocks, t, d), vm(blocks, t, d), vm(blocks, t, d), vm(blocks, t, d), vm(2, t, d), vm(t, d),
            vf(t, d), vf(t, d), vf(t, d), vf(t, d), vm(t, d), vm(4 * SUB, rows, cols), vm(4 * SUB, rows, cols),
            vf(t, 1), vf(t, 1), vf(t, 1), vf(t, 1), vf(t, 1), dma(3), dma(3), dma(12), dma(5 + PRE), dma(5 + PRE),
        ],
        compiler_params=pltpu.CompilerParams(collective_id=1, has_side_effects=True, vmem_limit_bytes=60 * 2**20),
    )(lengths, scale, gain, offset, mg, mb, tok, cot, wqkv, wo, w1, w2)


def factors_of(n):
    out = []
    while n > 1:
        out.append(2)
        n //= 2
    return out


ATT_TICKS = (0, 1, 2, 4, 5, 7, 8, 10)
WG_TICKS = (3, 6, 9, 11, 12, 13, 14, 15)
T_IN, T_TAIL = 16, 22


def lags_of(n_rs):
    return (0,) + tuple(range(2, 2 * n_rs - 1)) + (2 * n_rs,)


T_OUT = 25


EVENT_TICKS = tuple(range(T_TAIL))
AHEAD = 16


def count_before(ticks, i):
    done = 0
    for at in sorted(set(ticks)):
        done = done + jnp.where(i > at, ticks.count(at), 0)
    return done


def event_ticks(n_events):
    more = n_events - len(EVENT_TICKS)
    return EVENT_TICKS + tuple(range(T_TAIL, T_TAIL + more))


def send_ticks(n_events):
    made = [0] * (4 * SUB - PRE)
    for at in WG_TICKS:
        made += [at] * SUB
    events = event_ticks(n_events)
    return tuple(max(at, events[max(PRE + j - AHEAD, 0)]) for j, at in enumerate(made))


def tick_count(n_events):
    return T_TAIL + max(n_events - len(EVENT_TICKS), 10)


def main_kernel(factors, lengths, scale, q, k, v, gs, sn, lse, wq, gain,
                h_sent, h_ffn, h_gf, h_gp, h_nrm, h_last, h_keep, h_pre, h_x, h_ghid, h_small, h_out,
                out, gx_own, gx_got, small_out, out_got, *scr):
    tick = pl.program_id(0)
    n_rs = len(factors)
    chunks, rows, cols = out.shape[0], out.shape[2], out.shape[3]
    t, d = h_sent.shape
    hd2 = d // 2
    me = lax.axis_index("rows")
    ctx = lax.axis_index("ctx")
    fs = [2] + factors[1:]
    strides, st = [0], 2
    for f in factors[1:]:
        strides.append(st)
        st *= f
    size = [rows]
    for f in fs[1:]:
        size.append(size[-1] // f)
    pos = [ctx] + [lax.rem(me // strides[i], fs[i]) for i in range(1, n_rs)]
    off = [0]
    for i in range(1, n_rs):
        off.append(off[-1] + pos[i] * size[i])
    bits = []
    b = 1
    while b < lax.axis_size("rows"):
        bits.append(b)
        b *= 2

    def peer(i, j):
        if i == 0:
            return (me, 1 - ctx)
        return (me + ((pos[i] ^ j) - pos[i]) * strides[i], ctx)

    core = lax.rem(me, 2)
    sibling = (me + 1 - 2 * core, ctx)
    other_ctx = (me, 1 - ctx)

    def bit_peer(b):
        return (me + b - 2 * b * lax.rem(me // b, 2), ctx)

    scr = list(scr)
    take = lambda n: [scr.pop(0) for _ in range(n)]
    sendb, acc, gath = take(3)
    recv = [gath] + take(n_rs - 1)
    small_acc, small_recv = take(2)
    o_sent, o_ffn, o_gf, o_gp, o_nrm = take(5)
    r_sent, r_ffn, r_gf, r_gp, r_nrm, r_gq = take(6)
    gall, bias, gk, gv, gqt, xb, gh, gn_acc, gx_send = take(9)
    rs_s, rs_r = take(n_rs), take(n_rs)
    ag_s, ag_r = [None] + take(n_rs - 1), [None] + take(n_rs - 1)
    core_s, core_r, loc, small_s, small_r, swap_s, swap_r, load, gx_s, gx_r = take(10)

    def part(at, n):
        return pl.ds(at if isinstance(at, int) else pl.multiple_of(at, 16), n)

    def rs_copy(i, c, j):
        if i == 0:
            src, dst = sendb.at[c - PRE], gath.at[c]
        else:
            src = acc.at[c, part(off[i - 1] + (pos[i] ^ j) * size[i], size[i])]
            dst = recv[i].at[c, j - 1]
        return remote(src, dst, rs_s[i].at[c, j - 1], rs_r[i].at[c, j - 1], peer(i, j))

    def ag_copy(i, c, j, arriving):
        at = off[i - 1] + (pos[i] ^ j) * size[i] if arriving else off[i]
        ref = gath.at[c, part(at, size[i])]
        return remote(ref, ref, ag_s[i].at[c, j - 1], ag_r[i].at[c, j - 1], peer(i, j))

    def core_copy(c, arriving):
        to = 1 - core if arriving else core
        return remote(gath.at[c], out.at[c, to], core_s.at[c], core_r.at[c], sibling)

    def own_copy(c):
        return pltpu.make_async_copy(gath.at[c], out.at[c, core], loc.at[c])

    def reduce_stage(i, c):
        if i == 0:
            @pl.when(c >= PRE)
            def _():
                rs_copy(0, c, 1).wait_recv()
        else:
            for j in range(1, fs[i]):
                rs_copy(i, c, j).wait_recv()
        here = part(off[i], size[i])
        val = acc[c, here].astype(F32)
        if i == 0:
            val = val + gath[c].astype(F32)
        else:
            for j in range(1, fs[i]):
                val = val + recv[i][c, j - 1].astype(F32)
        if i + 1 < n_rs:
            acc[c, here] = val.astype(BF)
            for j in range(1, fs[i + 1]):
                rs_copy(i + 1, c, j).start()
        else:
            gath[c, here] = val.astype(BF)
            for j in range(1, fs[i]):
                ag_copy(i, c, j, False).start()

    def gather_stage(i, c):
        for j in range(1, fs[i]):
            ag_copy(i, c, j, True).wait_recv()
        if i > 1:
            for j in range(1, fs[i - 1]):
                ag_copy(i - 1, c, j, False).start()
        else:
            core_copy(c, False).start()
            own_copy(c).start()

    def small_copy(i):
        to = other_ctx if i == 0 else bit_peer(bits[i - 1])
        return remote(small_acc.at[i], small_recv.at[i], small_s.at[i], small_r.at[i], to)

    mine = pl.ds(pl.multiple_of(core * hd2, hd2), hd2)
    theirs = pl.ds(pl.multiple_of((1 - core) * hd2, hd2), hd2)
    swaps = [(h_sent, r_sent), (h_gp.at[:, theirs], r_gp), (h_ffn, r_ffn), (h_gf.at[1 - core], r_gf.at[0]), (h_nrm, r_nrm),
             (h_gf.at[3 - core], r_gf.at[1])]
    loads = [(h_sent, o_sent), (h_gp.at[:, mine], o_gp), (h_ffn, o_ffn), (h_gf.at[core], o_gf.at[0]), (h_nrm, o_nrm),
             (h_x, xb), (h_ghid, gh), (h_small, small_acc.at[0]), (h_last, sendb.at[pl.ds(0, 4 * SUB - PRE)]),
             (h_keep, acc.at[pl.ds(0, 4 * SUB)]), (h_pre, gath.at[pl.ds(0, PRE)]), (h_gf.at[2 + core], o_gf.at[1])]

    def swap_copy(j):
        return remote(swaps[j][0], swaps[j][1], swap_s.at[j], swap_r.at[j], sibling)

    def gq_copy():
        return remote(gall.at[1 - core], r_gq, swap_s.at[6], swap_r.at[6], sibling)

    def load_copy(j):
        return pltpu.make_async_copy(loads[j][0], loads[j][1], load.at[j])

    seg = t // 2

    def rows_of(c):
        return pl.ds(pl.multiple_of(c * seg, seg), seg)

    def gx_copy():
        return remote(gx_send, gx_got, gx_s.at[0], gx_r.at[0], other_ctx)

    def out_copy():
        return remote(h_out.at[rows_of(1 - ctx)], out_got, gx_s.at[1], gx_r.at[1], other_ctx)

    @pl.when(tick == 0)
    def _():
        peers = [other_ctx, sibling]
        for i in range(1, n_rs):
            peers += [peer(i, j) for j in range(1, fs[i])]
        barrier = pltpu.get_barrier_semaphore()
        for p in peers:
            pl.semaphore_signal(barrier, inc=1, device_id=p, device_id_type=MESH)
        for j in (10, 9, 8, 0, 1, 2, 3, 11, 4, 5, 6, 7):
            load_copy(j).start()
        pl.semaphore_wait(barrier, len(peers))
        for j in (0, 1, 2, 3, 5, 4):
            swap_copy(j).start()
        for j in (10, 9, 8):
            load_copy(j).wait()
        at = lax.broadcasted_iota(jnp.int32, (1, t), 1)
        start = jnp.zeros((1, t), jnp.int32)
        bound = jnp.int32(0)
        for i in range(lengths.shape[1]):
            bound = bound + lengths[ctx, i]
            start = jnp.where(at >= bound, bound, start)
        fill_bias(start, bias, t)
        load_copy(7).wait()

    pair = count_before(ATT_TICKS, tick)

    @pl.when(count_before(ATT_TICKS, tick + 1) > pair)
    def _():
        hd = q.shape[2] // 2
        kt = k[0].astype(F32).T.astype(BF)
        gsf = gs[...].astype(F32)
        prod = (gsf * sn[...].astype(F32)).T
        d0 = jnp.sum(prod[0:hd], axis=0, keepdims=True)
        d1 = jnp.sum(prod[hd:], axis=0, keepdims=True)
        lane = lax.broadcasted_iota(jnp.int32, (1, d), 1)
        h0 = jnp.sum(d0, axis=-1, keepdims=True)
        h1 = jnp.sum(d1, axis=-1, keepdims=True)
        small_acc[0, 14:15, :] += (
            jnp.where(lane == 2 * pair, h0 / scale[2 * pair], 0.0)
            + jnp.where(lane == 2 * pair + 1, h1 / scale[2 * pair + 1], 0.0)
        )
        ga = (gsf * head_lanes(scale, pair, (1, 2 * hd), hd)).astype(BF)
        gk[...] = jnp.zeros_like(gk)
        gv[...] = jnp.zeros_like(gv)
        for i in range(t // QB):
            k0, k1 = key_range(i)
            qs = slice(i * QB, (i + 1) * QB)
            qm = (both_heads(q[0, qs, :], hd) * (hd**-0.5)).astype(BF)
            gm = both_heads(ga[qs, :], hd)
            sc = dot(k[0, k0:k1, :], qm, 1, 1) + bias[i, 0 : k1 - k0, :]
            ls = jnp.concatenate([lse[0, 0:1, qs], lse[0, 1:2, qs]], axis=1)
            dd = jnp.concatenate([d0[:, qs], d1[:, qs]], axis=1)
            pt = jnp.exp(sc - ls)
            gp = dot(v[0, k0:k1, :], gm, 1, 1)
            ds = (pt * (gp - dd)).astype(BF)
            gv[k0:k1, :] += dot(pt.astype(BF), gm, 1, 0)
            gk[k0:k1, :] += dot(ds, qm, 1, 0)
            gq = dot(kt[:, k0:k1], ds, 1, 0) * (hd**-0.5)
            gqt[:, qs] = jnp.concatenate([gq[0:hd, 0:QB], gq[hd:, QB:]], axis=0)
        per_core = len(ATT_TICKS) // 2
        half = pair // per_core
        at = pl.ds(pl.multiple_of(lax.rem(pair, per_core) * 128, 128), 128)
        gall[half, 0, :, at] = gqt[...].T.astype(BF)
        gall[half, 1, :, at] = gk[...].astype(BF)
        gall[half, 2, :, at] = gv[...].astype(BF)

    @pl.when(tick == ATT_TICKS[-1])
    def _():
        gq_copy().start()

    def wgrad(c, a0, a1, b0, b1):
        for far in (True, False):
            x = 1 - ctx if far else ctx
            val = (dot(a0(x), b0, 0, 0) + dot(a1(x), b1, 0, 0)).astype(BF)
            put_chunk(sendb if far else acc, c - PRE // SUB if far else c, val)

    def half_of(ref):
        return lambda x: ref[:, pl.ds(pl.multiple_of(x * hd2, 128), hd2)]

    @pl.when(tick == T_OUT)
    def _():
        out_copy().start()
        gx_copy().start()

    @pl.when(tick == WG_TICKS[0])
    def _():
        for j in (0, 1):
            load_copy(j).wait()
            swap_copy(j).wait_recv()
        wgrad(4, half_of(o_sent), half_of(r_sent), o_gp[...], r_gp[...])

    @pl.when(tick == WG_TICKS[1])
    def _():
        for j in (2, 3):
            load_copy(j).wait()
            swap_copy(j).wait_recv()
        load_copy(11).wait()
        swap_copy(5).wait_recv()

    block = count_before(WG_TICKS, tick)
    makes = count_before(WG_TICKS, tick + 1) > block

    @pl.when(makes & (block >= 1) & (block < 5))
    def _():
        c = block - 1
        b = lambda ref: ref[c // 2, :, pl.ds(pl.multiple_of(lax.rem(c, 2) * hd2, 128), hd2)]
        wgrad(c + 5, half_of(o_ffn), half_of(r_ffn), b(o_gf), b(r_gf))

    @pl.when(tick == WG_TICKS[5])
    def _():
        load_copy(4).wait()
        swap_copy(4).wait_recv()
        gq_copy().wait_recv()

    @pl.when(makes & (block >= 5))
    def _():
        c = block - 5
        wgrad(c + 9, half_of(o_nrm), half_of(r_nrm), gall[core, c], r_gq[c])

    @pl.when((tick >= T_IN) & (tick < T_TAIL))
    def _():
        j = tick - T_IN
        val = dot(gall[lax.rem(j, 2), j // 2], wq[...], 1, 1)

        @pl.when(j == 0)
        def _():
            gn_acc[...] = val

        @pl.when(j > 0)
        def _():
            gn_acc[...] += val

    @pl.when(tick == T_TAIL - 1)
    def _():
        load_copy(5).wait()
        load_copy(6).wait()
        e = gn_acc[...]
        n, inv = ln_stats(xb[...].astype(F32))
        small_acc[0, 0:1, :] = colsum(e * n)
        small_acc[0, 3:4, :] = colsum(e)
        gh[...] += ln_back(e, gain[0:1, :], n, inv)
        gx_send[...] = gh[rows_of(1 - ctx), :].astype(BF)
        gx_own[...] = gh[rows_of(ctx), :]
        small_copy(0).start()

    def guarded(f, i, c):
        pl.when((c >= 0) & (c < chunks))(lambda: f(i, c))

    lanes = [(reduce_stage, i) for i in range(n_rs)] + [(gather_stage, i) for i in range(n_rs - 1, 0, -1)]

    lags = lags_of(n_rs)
    n_events = chunks + lags[-1]
    sends = send_ticks(n_events)

    def send(c, _):
        rs_copy(0, c, 1).start()
        return 0

    lax.fori_loop(PRE + count_before(sends, tick), PRE + count_before(sends, tick + 1), send, 0)
    events = event_ticks(n_events)
    event = count_before(events, tick)

    @pl.when(count_before(events, tick + 1) > event)
    def _():
        for lag in range(len(lanes) - 1, -1, -1):
            f, i = lanes[lag]
            guarded(f, i, event - lags[lag])

    for i in range(len(bits) + 1):

        @pl.when(tick == T_TAIL + 1 + i)
        def _(i=i):
            small_copy(i).wait_recv()
            if i < len(bits):
                small_acc[i + 1] = small_acc[i] + small_recv[i]
                small_copy(i + 1).start()
            else:
                small_out[...] = small_acc[i] + small_recv[i]

    @pl.when(tick == pl.num_programs(0) - 1)
    def _():
        def finish(c, _):
            for i in range(n_rs):
                for j in range(1, fs[i]):
                    if i == 0:
                        @pl.when(c >= PRE)
                        def _():
                            rs_copy(0, c, 1).wait_send()
                    else:
                        rs_copy(i, c, j).wait_send()
                        ag_copy(i, c, j, False).wait_send()
            core_copy(c, False).wait_send()
            core_copy(c, True).wait_recv()
            own_copy(c).wait()
            return 0

        lax.fori_loop(0, chunks, finish, 0)
        for i in range(len(bits) + 1):
            small_copy(i).wait_send()
        for j in range(6):
            swap_copy(j).wait_send()
        gq_copy().wait_send()
        gx_copy().wait()
        out_copy().wait()


def main_call(factors, rows, cols, lengths, scale, qkv, gsent, sent, lse, w_qkv, gain, ffn_in, gf, gp, normed, last,
              keep, pre, x, ghid, small, out):
    t, d = sent.shape
    h = d // 2
    n = 1
    for f in factors:
        n *= f
    fs = [2] + factors[1:]
    levels = 1
    while n > 1:
        levels += 1
        n //= 2
    size, recv = rows, []
    for f in fs[1:]:
        size //= f
        recv.append(pltpu.VMEM((CHUNKS, f - 1, size, cols), BF))
    dma = lambda *shape: pltpu.SemaphoreType.DMA(shape)
    per = lambda k: [dma(CHUNKS, f - 1) for f in fs[k:]]
    vm = lambda *shape: pltpu.VMEM(shape, BF)
    vf = lambda *shape: pltpu.VMEM(shape, F32)
    pair = lambda i: jnp.minimum(count_before(ATT_TICKS, i), len(ATT_TICKS) - 1)
    part = lambda j: pl.BlockSpec((1, t, 128), lambda i: (j, 0, pair(i)))
    flat = pl.BlockSpec((t, 128), lambda i: (0, pair(i)))
    whole = lambda shape: pl.BlockSpec(shape, lambda i: (0,) * len(shape))
    wcol = lambda i: jnp.clip(i - T_IN, 0, 5)
    any_ = pl.BlockSpec(memory_space=pl.ANY)
    events = CHUNKS + lags_of(len(fs))[-1]
    return pl.pallas_call(
        functools.partial(main_kernel, factors),
        grid=(tick_count(events),),
        in_specs=[
            pl.BlockSpec(memory_space=pltpu.SMEM), pl.BlockSpec(memory_space=pltpu.SMEM),
            part(0), part(1), part(2), flat, flat,
            pl.BlockSpec((1, 2, t), lambda i: (pair(i), 0, 0)),
            pl.BlockSpec((d, h), lambda i: (0, wcol(i))),
            whole((3, d)),
        ] + [any_] * 12,
        out_specs=[any_, whole((t // 2, d)), any_, whole(small.shape), any_],
        out_shape=[
            struct((CHUNKS, 2, rows, cols), BF), struct((t // 2, d), F32), struct((t // 2, d), BF), struct(small.shape, F32),
            struct((t // 2, d), BF),
        ],
        scratch_shapes=[vm(CHUNKS - PRE, rows, cols), vm(CHUNKS, rows, cols), vm(CHUNKS, rows, cols)]
        + recv
        + [vf(levels, *small.shape)] * 2
        + [vm(t, d), vm(t, d), vm(2, t, d), vm(t, h), vm(t, d)]
        + [vm(t, d), vm(t, d), vm(2, t, d), vm(t, h), vm(t, d), vm(3, t, h)]
        + [vm(2, 3, t, h), vf(t // QB, QB + REACH, 2 * QB), vf(t, 128), vf(t, 128), vf(128, t), vm(t, d), vf(t, d), vf(t, d),
           vm(t // 2, d)]
        + per(0) + per(0) + per(1) + per(1)
        + [dma(CHUNKS), dma(CHUNKS), dma(CHUNKS), dma(levels), dma(levels), dma(7), dma(7), dma(12), dma(2), dma(2)],
        compiler_params=pltpu.CompilerParams(collective_id=0, has_side_effects=True, vmem_limit_bytes=60 * 2**20),
    )(lengths, scale, qkv, qkv, qkv, gsent, sent, lse, w_qkv, gain,
      sent, ffn_in, gf, gp, normed, last, keep, pre, x, ghid, small, out)


SLOTS = 8


def finish_kernel(small, got, gx_own, gx_got, own, away, out, gx, g2, g1, go, gq, gn, bn, gmg, gmb, ghs,
                  inb, outb, low, wide, isem, osem, sems):
    ctx = lax.axis_index("ctx")
    seg, d = gx_own.shape
    h = d // 2
    c = got.shape[3]
    blocks = (small.shape[0] - 8) // 2

    def copy(src, dst, j):
        return pltpu.make_async_copy(src, dst, sems.at[j])

    ins = [
        copy(gx_got, low.at[0], 0),
        copy(own.at[pl.ds(pl.multiple_of(ctx * seg, seg), seg)], low.at[1], 1),
        copy(away, low.at[2], 2),
        copy(gx_own, wide.at[1], 3),
    ]
    outs = [
        copy(wide.at[0], gx.at[1 - ctx], 4),
        copy(low.at[1], out.at[ctx], 5),
        copy(low.at[2], out.at[1 - ctx], 6),
        copy(wide.at[1], gx.at[ctx], 7),
    ]

    def place(i):
        k, core = i // 2, i % 2
        if k < 4:
            ref, r, col = g2, core * 2 + k // 2, k % 2
        elif k == 4:
            ref, r, col = go, 0, core
        elif k < 9:
            ref, r, col = g1, 0, (((k - 5) // 2) * 2 + core) * 2 + (k - 5) % 2
        else:
            ref, r, col = gq, 0, (k - 9) * 2 + core
        return ref.at[pl.ds(r * h, h), pl.ds(col * h, h)]

    def load(i):
        src = got.at[pl.ds(i // 2 * SUB, SUB), i % 2]
        return pltpu.make_async_copy(src, inb.at[i % SLOTS], isem.at[i % SLOTS])

    def store(i):
        return pltpu.make_async_copy(outb.at[i % SLOTS], place(i), osem.at[i % SLOTS])

    count = 2 * BLOCKS
    for i in range(SLOTS):
        load(i).start()
    for v in ins:
        v.start()
    half = pl.ds(pl.multiple_of(ctx * h, h), h)
    gn[...] = small[0:3, half]
    bn[...] = small[3:6, half]
    for j in range(blocks // 2):
        at = slice(j * d, (j + 1) * d)
        gmg[:, at] = small[pl.ds(6 + ctx * (blocks // 2) + j, 1), :]
        gmb[:, at] = small[pl.ds(6 + blocks + ctx * (blocks // 2) + j, 1), :]
    n = ghs.shape[1]
    row = small[6 + 2 * blocks : 7 + 2 * blocks, :]
    ghs[...] = jnp.where(ctx == 0, row[:, 0:n], row[:, n : 2 * n])
    for i in range(count):
        load(i).wait()
        if i >= SLOTS:
            store(i - SLOTS).wait()
        groups = h // c // SUB
        for j in range(SUB):
            for m in range(groups):
                at = (j * groups + m) * c
                outb[i % SLOTS, :, at : at + c] = inb[i % SLOTS, j, m * h : (m + 1) * h, :].astype(F32)
        store(i).start()
        if i + SLOTS < count:
            load(i + SLOTS).start()
        if i == SLOTS:
            for j in range(4):
                ins[j].wait()
                if j == 0:
                    wide[0] = low[0].astype(F32)
                outs[j].start()
    for i in range(count - SLOTS, count):
        store(i).wait()
    for v in outs:
        v.wait()


def finish_call(small, got, gx_own, gx_got, own, away, ff, heads):
    seg, d = gx_own.shape
    h = d // 2
    rows, cols = got.shape[2:]
    any_ = pl.BlockSpec(memory_space=pl.ANY)
    vmem = pl.BlockSpec(memory_space=pltpu.VMEM)
    dma = lambda n: pltpu.SemaphoreType.DMA((n,))
    return pl.pallas_call(
        finish_kernel,
        in_specs=[vmem] + [any_] * 5,
        out_specs=[any_] * 6 + [vmem] * 5,
        out_shape=[
            struct((2, seg, d), BF), struct((2, seg, d), F32), struct((ff // 2, d), F32), struct((h, ff), F32),
            struct((h, d), F32), struct((h, 3 * d), F32), struct((3, h), F32), struct((3, h), F32),
            struct((1, ff // 2), F32), struct((1, ff // 2), F32), struct((1, heads // 2), F32),
        ],
        scratch_shapes=[
            pltpu.VMEM((SLOTS, SUB, rows, cols), BF), pltpu.VMEM((SLOTS, h, h), F32),
            pltpu.VMEM((3, seg, d), BF), pltpu.VMEM((2, seg, d), F32), dma(SLOTS), dma(SLOTS), dma(8),
        ],
        compiler_params=pltpu.CompilerParams(vmem_limit_bytes=60 * 2**20),
    )(small, got, gx_own, gx_got, own, away)


def local(
    tokens, cotangent, w_qkv, w_out, w_fc1, w_fc2, norm_gain, norm_bias, mid_gain, mid_bias, head_scale, doc_lengths
):
    n = lax.axis_size("rows")
    factors = factors_of(n)
    d = tokens.shape[2]
    ff = w_fc1.shape[1]
    heads = head_scale.shape[0]
    mg, mb = mid_gain[None, :], mid_bias[None, :]
    pieces = 1
    for f in factors[1:]:
        pieces *= f
    half = d // 2
    rows = max(half, 16 * pieces)
    cols = half * half // rows // SUB
    x, normed, qkv, sent, lse, ffn_in, gf, gp, gsent, ghid, out, keep, last, pre, small = front_call(
        rows, cols, doc_lengths, head_scale, norm_gain, norm_bias, mg, mb, tokens, cotangent, w_qkv, w_out, w_fc1, w_fc2
    )
    got, gx_own, gx_got, small, out_got = main_call(
        factors, rows, cols, doc_lengths, head_scale, qkv, gsent, sent, lse, w_qkv, norm_gain, ffn_in, gf, gp, normed, last,
        keep, pre, x, ghid, small, out,
    )
    out, gx, g2, g1, go, gq, gn, bn, gmg, gmb, ghs = finish_call(small, got, gx_own, gx_got, out, out_got, ff, heads)
    return (out, gx, gq, go, g1, g2, gn, bn, gmg.reshape(-1), gmb.reshape(-1), ghs.reshape(-1))


def solution(mesh):
    rows = P("rows", "ctx", None)
    in_specs = (rows, rows) + (P(),) * 9 + (P("rows", None),)
    ctx0 = P("ctx", None)
    out_specs = (rows, rows, ctx0, ctx0, ctx0, ctx0, P(None, "ctx"), P(None, "ctx"), P("ctx"), P("ctx"), P("ctx"))
    return jax.shard_map(local, mesh=mesh, in_specs=in_specs, out_specs=out_specs, check_vma=False)
```
